32 devices in a mesh: dp: 16 (over z, x, core), rep: 2 (over y).
Axes of the slice: x: 2, y: 2, z: 4, core: 2. Of those that a mesh axis runs over, the one named last changes fastest.
Arguments:
- tokens: bfloat16 [32, 1024, 768], P(('dp', 'rep')), may hold values from -6 to 6
- segment_ids: int32 [32, 1024], P(('dp', 'rep')), may hold values from 0 to 3, never falling along the last dimension, each value on 1 to 512 neighbouring positions
- cotangent: bfloat16 [32, 1024, 768], P(('dp', 'rep')), may hold values from -6 to 6
- w_qkv: float32 [768, 2304], P('dp'), may hold values from -0.21875 to 0.21875
- w_out: float32 [768, 768], P('dp'), may hold values from -0.875 to 0.875
- w_up: float32 [768, 3072], P('dp'), may hold values from -0.21875 to 0.21875
- w_down: float32 [3072, 768], P('dp'), may hold values from -0.109375 to 0.109375
- small_params: float32 [12, 768], P(None, 'dp'), may hold values from -0.35 to 1.5, as said below
- mom1_qkv: float32 [768, 2304], P('dp'), may hold values from -320 to 320
- mom1_out: float32 [768, 768], P('dp'), may hold values from -224 to 224
- mom1_up: float32 [768, 3072], P('dp'), may hold values from -320 to 320
- mom1_down: float32 [3072, 768], P('dp'), may hold values from -640 to 640
- mom1_small: float32 [12, 768], P(None, 'dp'), may hold values from -512 to 512
- mom2_qkv: float32 [768, 2304], P('dp'), may hold values from 1474.56 to 23592.96
- mom2_out: float32 [768, 768], P('dp'), may hold values from 655.36 to 10485.76
- mom2_up: float32 [768, 3072], P('dp'), may hold values from 1474.56 to 23592.96
- mom2_down: float32 [3072, 768], P('dp'), may hold values from 5898.24 to 94371.84
- mom2_small: float32 [12, 768], P(None, 'dp'), may hold values from 4096 to 65536
Outputs:
- out_tokens: bfloat16 [32, 1024, 768], P(('dp', 'rep'))
- grad_tokens: bfloat16 [32, 1024, 768], P(('dp', 'rep'))
- new_qkv: float32 [768, 2304], P('dp')
- new_out: float32 [768, 768], P('dp')
- new_up: float32 [768, 3072], P('dp')
- new_down: float32 [3072, 768], P('dp')
- new_small: float32 [12, 768], P(None, 'dp')
- next1_qkv: float32 [768, 2304], P('dp')
- next1_out: float32 [768, 768], P('dp')
- next1_up: float32 [768, 3072], P('dp')
- next1_down: float32 [3072, 768], P('dp')
- next1_small: float32 [12, 768], P(None, 'dp')
- next2_qkv: float32 [768, 2304], P('dp')
- next2_out: float32 [768, 768], P('dp')
- next2_up: float32 [768, 3072], P('dp')
- next2_down: float32 [3072, 768], P('dp')
- next2_small: float32 [12, 768], P(None, 'dp')
The draws below stay inside these ranges and needn't reach their ends.
Inputs may be any that keep to these rules, and one draw needn't show every extreme that they name: `segment_ids`: each row holds 4 documents in order, each 1 to 512 tokens long, one exactly that long. `small_params`: gains lie in 0.5 to 1.5, biases in -0.35 to 0.35.
All inputs are finite; a program needn't handle non-finite values.
Results may differ from the reference program's by a relative error of at most 0.019.
Values may be sent and summed in bfloat16 or wider, within the bound.
No kernel may reach another device: no remote copies, remote signals or barrier semaphores. Data moves between devices by JAX's collectives and lax.ppermute only.
A program may use at most 192 MiB of HBM per device.

```python
import math
import jax
import jax.numpy as jnp
import numpy as np
from jax import lax

D = 768
HEADS = 12
FF = 3072
TOK_DEV = 1024
SEGS = 4
STEP = 10
SMALL_ROWS = 12
TOKENS = 32768
DEVICES = 32


def draw_small_params(key, part):
    key = jax.random.fold_in(key, 7)
    rows = jnp.arange(SMALL_ROWS)[:, None] + jnp.zeros((1, D), jnp.int32)
    is_gain = (rows == 0) | (rows == 5)
    gains = jax.random.uniform(jax.random.fold_in(key, 11), (SMALL_ROWS, D), jnp.float32, 0.5, 1.5)
    biases = jax.random.uniform(jax.random.fold_in(key, 12), (SMALL_ROWS, D), jnp.float32, -0.35, 0.35)
    return jnp.where(is_gain, gains, biases)


def levels(stream_key, shape, shards, least, largest):
    def one(axis_at, blocks):
        heights = jax.random.uniform(jax.random.fold_in(jax.random.fold_in(stream_key, 6), axis_at), (blocks,), jnp.float32, least / len(shards), largest / len(shards))
        return jnp.repeat(jnp.exp(heights), shape[axis_at] // blocks).reshape((-1,) + (1,) * (len(shape) - axis_at - 1))

    factor_of = one(*shards[0])
    for cut in shards[1:]:
        factor_of = factor_of * one(*cut)
    return factor_of


def split_up(amount, total, most, lean):
    weights = [(1 << 20) // math.isqrt(standing ** lean) + 1 for standing in range(2, amount + 1)]
    spare, given = total - most - (amount - 1), [1] * (amount - 1)
    while spare > 0:
        movable = [i for i in range(amount - 1) if given[i] < most]
        whole, budget = sum([weights[i] for i in movable]), spare
        for i in movable:
            more = min(most - given[i], max(1, budget * weights[i] // whole), spare)
            given[i] = given[i] + more
            spare = spare - more
    return np.array([most] + given)


def ragged_sizes(own_key, number_of, total, most, slope):
    if number_of == 2:
        one = jax.random.randint(own_key, (), max(1, total - most), min(most, total - 1) + 1)
        return jnp.stack([one, total - one])
    sizes = jnp.asarray(split_up(number_of, total, most, slope), jnp.int32)
    pairs = (number_of - 1) // 2
    donor, receiver = sizes[1:1 + 2 * pairs:2], sizes[2:2 + 2 * pairs:2]
    slack = jnp.minimum(donor - 1, most - receiver)
    passed = jax.random.randint(jax.random.fold_in(own_key, 1), (pairs,), 0, 1 << 20) % (slack + 1)
    sizes = sizes.at[1:1 + 2 * pairs:2].set(donor - passed).at[2:2 + 2 * pairs:2].set(receiver + passed)
    return sizes[jax.random.permutation(jax.random.fold_in(own_key, 2), number_of)]


def normal_values(own_key, shape, scale, bound, split=(), kind=jnp.bfloat16):
    values = scale * jax.random.normal(own_key, shape, jnp.float32)
    if split:
        values = values * levels(own_key, shape, split, -0.22, 0.18)
    return jnp.clip(values, -bound, bound).astype(kind)


def setup_inputs(seed: int = 0) -> dict:
    splits = jax.random.split(jax.random.key(seed), 19)
    tokens = normal_values(splits[0], (DEVICES, TOK_DEV, D), 1.0, 6.0, ((0, 32),))
    segment_ids = jax.vmap(lambda own: jnp.searchsorted(jnp.cumsum(ragged_sizes(own, SEGS, TOK_DEV, TOK_DEV // 2, 0)), jnp.arange(TOK_DEV), side="right"))(jax.random.split(splits[1], DEVICES)).reshape((DEVICES, TOK_DEV)).astype(jnp.int32)
    cotangent = normal_values(splits[2], (DEVICES, TOK_DEV, D), 1.0, 6.0, ((0, 32),))
    w_qkv = normal_values(splits[3], (D, 3 * D), D ** -0.5, 0.21875, ((0, 16),), jnp.float32)
    w_out = normal_values(splits[4], (D, D), (D // 16) ** -0.5, 0.875, ((0, 16),), jnp.float32)
    w_up = normal_values(splits[5], (D, FF), D ** -0.5, 0.21875, ((0, 16),), jnp.float32)
    w_down = normal_values(splits[6], (FF, D), FF ** -0.5, 0.109375, ((0, 16),), jnp.float32)
    small_params = draw_small_params(jax.random.fold_in(splits[18], 71), 0)
    mom1_qkv = normal_values(splits[8], (D, 3 * D), (0.3 * TOKENS ** 0.5), 320.0, ((0, 16),), jnp.float32)
    mom1_out = normal_values(splits[9], (D, D), (0.2 * TOKENS ** 0.5), 224.0, ((0, 16),), jnp.float32)
    mom1_up = normal_values(splits[10], (D, FF), (0.3 * TOKENS ** 0.5), 320.0, ((0, 16),), jnp.float32)
    mom1_down = normal_values(splits[11], (FF, D), (0.6 * TOKENS ** 0.5), 640.0, ((0, 16),), jnp.float32)
    mom1_small = normal_values(splits[12], (SMALL_ROWS, D), (0.5 * TOKENS ** 0.5), 512.0, ((1, 16),), jnp.float32)
    mom2_qkv = jnp.clip(jnp.exp(math.log(23592.96) - 2.7725887 * jax.random.uniform(splits[13], (D, 3 * D), jnp.float32) ** levels(splits[13], (D, 3 * D), ((0, 16),), -0.2, 0.2)), 1474.56, 23592.96)
    mom2_out = jnp.clip(jnp.exp(math.log(10485.76) - 2.7725887 * jax.random.uniform(splits[14], (D, D), jnp.float32) ** levels(splits[14], (D, D), ((0, 16),), -0.2, 0.2)), 655.36, 10485.76)
    mom2_up = jnp.clip(jnp.exp(math.log(23592.96) - 2.7725887 * jax.random.uniform(splits[15], (D, FF), jnp.float32) ** levels(splits[15], (D, FF), ((0, 16),), -0.2, 0.2)), 1474.56, 23592.96)
    mom2_down = jnp.clip(jnp.exp(math.log(94371.84) - 2.7725887 * jax.random.uniform(splits[16], (FF, D), jnp.float32) ** levels(splits[16], (FF, D), ((0, 16),), -0.2, 0.2)), 5898.24, 94371.84)
    mom2_small = jnp.clip(jnp.exp(math.log(65536.0) - 2.7725887 * jax.random.uniform(splits[17], (SMALL_ROWS, D), jnp.float32) ** levels(splits[17], (SMALL_ROWS, D), ((1, 16),), -0.2, 0.2)), 4096.0, 65536.0)
    return {"tokens": tokens, "segment_ids": segment_ids, "cotangent": cotangent, "w_qkv": w_qkv, "w_out": w_out, "w_up": w_up, "w_down": w_down, "small_params": small_params, "mom1_qkv": mom1_qkv, "mom1_out": mom1_out, "mom1_up": mom1_up, "mom1_down": mom1_down, "mom1_small": mom1_small, "mom2_qkv": mom2_qkv, "mom2_out": mom2_out, "mom2_up": mom2_up, "mom2_down": mom2_down, "mom2_small": mom2_small}


HIGHEST = lax.Precision.HIGHEST
BETA1 = 0.5
BETA2 = 0.5
ADAM_EPS = 1e-08
DECAY = 0.05
RATES = (0.04, 0.15, 0.04, 0.02, 0.3)

@jax.custom_vjp
def low(v):
    return lax.optimization_barrier(v.astype(jnp.bfloat16)).astype(jnp.float32)

@jax.custom_vjp
def low_back(v):
    return v

def low_keep(v):
    return (low(v), None)

def low_pass(kept, grad):
    return (grad,)

def back_keep(v):
    return (v, None)

def back_low(kept, grad):
    return (low(grad),)
low.defvjp(low_keep, low_pass)
low_back.defvjp(back_keep, back_low)

def both_ways(value):
    return low(low_back(value))

def layer_norm(value, gain, bias):
    center = value - lax.optimization_barrier(jnp.mean(value, -1, keepdims=True))
    spread = lax.optimization_barrier(jnp.mean(center * center, -1, keepdims=True))
    return center * lax.rsqrt(spread + 1e-06) * gain + bias

def mask_softmax(scores, same):
    masked = jnp.where(same, scores, -1000000000.0)
    shifted = jnp.exp(masked - lax.optimization_barrier(jnp.max(masked, -1, keepdims=True)))
    return shifted / lax.optimization_barrier(jnp.sum(shifted, -1, keepdims=True))

def forward(inputs, segment_row, w_qkv, w_out, w_up, w_down, small_params):
    model_width = inputs.shape[1]
    row_count = inputs.shape[0]
    head_size = model_width // HEADS
    score_scale = 1.0 / math.sqrt(head_size)
    low_qkv, low_out, low_up, low_down, smalls = (low(w_qkv), low(w_out), low(w_up), low(w_down), low(small_params))
    pieces = [smalls[place] for place in range(8)]
    gain_one, bias_one, query_bias, value_bias, out_bias, gain_two, bias_two, down_bias = pieces
    up_bias = smalls[8:].reshape(-1)
    normed = low(layer_norm(inputs, gain_one, bias_one))
    projected = jnp.dot(normed, low_qkv, precision=HIGHEST)
    queries = both_ways(projected[:, :model_width] + query_bias)
    keys_all = both_ways(projected[:, model_width:2 * model_width])
    vals_all = both_ways(projected[:, 2 * model_width:] + value_bias)
    same = segment_row[:, None] == segment_row[None, :]

    def split_heads(value):
        return value.reshape(row_count, HEADS, head_size).transpose(1, 0, 2)

    def one_head(head_inputs):
        head_q, head_k, head_v = head_inputs
        scores = low_back(jnp.dot(head_q, head_k.T, precision=HIGHEST) * score_scale)
        probs = low(mask_softmax(scores, same))
        return jnp.dot(probs, head_v, precision=HIGHEST)
    attended = lax.map(jax.checkpoint(one_head), (split_heads(queries), split_heads(keys_all), split_heads(vals_all)))
    mixed = both_ways(attended.transpose(1, 0, 2).reshape(row_count, model_width))
    after_attn = inputs + low_back(jnp.dot(mixed, low_out, precision=HIGHEST)) + out_bias
    normed_two = low(layer_norm(after_attn, gain_two, bias_two))
    pre_act = low_back(jnp.dot(normed_two, low_up, precision=HIGHEST)) + up_bias
    hidden = low(jax.nn.gelu(pre_act, approximate=True))
    return after_attn + low_back(jnp.dot(hidden, low_down, precision=HIGHEST)) + down_bias

def adamw(weight, grad, mom_one, mom_two, rate):
    next_one = BETA1 * mom_one + (1.0 - BETA1) * grad
    next_two = BETA2 * mom_two + (1.0 - BETA2) * grad * grad
    fixed_one = next_one / (1.0 - BETA1 ** STEP)
    fixed_two = next_two / (1.0 - BETA2 ** STEP)
    updated = weight - rate * (fixed_one / (jnp.sqrt(fixed_two) + ADAM_EPS) + DECAY * weight)
    return (updated, next_one, next_two)

def reference(tokens, segment_ids, cotangent, w_qkv, w_out, w_up, w_down, small_params, mom1_qkv, mom1_out, mom1_up, mom1_down, mom1_small, mom2_qkv, mom2_out, mom2_up, mom2_down, mom2_small):
    masters = (w_qkv, w_out, w_up, w_down, small_params)

    def one_row(carry, row_data):
        row_tokens, segment_row, row_grad = row_data

        def run(inputs, *params):
            return forward(inputs, segment_row, *params)
        result, pull = jax.vjp(run, row_tokens.astype(jnp.float32), *masters)
        grads = pull(row_grad.astype(jnp.float32))
        carry = tuple((total + piece for total, piece in zip(carry, grads[1:])))
        return (carry, (result.astype(jnp.bfloat16), grads[0].astype(jnp.bfloat16)))
    start = tuple((jnp.zeros_like(master) for master in masters))
    totals, (outputs, input_grads) = lax.scan(one_row, start, (tokens, segment_ids, cotangent))
    firsts = (mom1_qkv, mom1_out, mom1_up, mom1_down, mom1_small)
    seconds = (mom2_qkv, mom2_out, mom2_up, mom2_down, mom2_small)
    results = [adamw(masters[place], totals[place], firsts[place], seconds[place], RATES[place]) for place in range(5)]
    return (outputs, input_grads, results[0][0], results[1][0], results[2][0], results[3][0], results[4][0], results[0][1], results[1][1], results[2][1], results[3][1], results[4][1], results[0][2], results[1][2], results[2][2], results[3][2], results[4][2])
```

```python
import functools
import math

import jax
import jax.numpy as jnp
from jax import lax
from jax.experimental import pallas as pl
from jax.experimental.pallas import tpu as pltpu
from jax.sharding import PartitionSpec as P

HEADS = 12
STEP = 10
BETA1 = 0.5
BETA2 = 0.5
ADAM_EPS = 1e-08
DECAY = 0.05
RATES = (0.04, 0.15, 0.04, 0.02, 0.3)

bf16 = jnp.bfloat16
f32 = jnp.float32

T = 1024
D = 768
FF = 3072
OWN = 16
RB = D // OWN
FB = FF // OWN // 3
FC = FF // 3
QR = 6 * RB
FR = 8 * RB + 6 * FB
SR = 16
B = 256
NB = T // B
MASK = 2.0**30
VMEM_LIMIT = 56 << 20

VM = pl.BlockSpec(memory_space=pltpu.VMEM)
SM = pl.BlockSpec(memory_space=pltpu.SMEM)


def params(**kw):
    return pltpu.CompilerParams(vmem_limit_bytes=VMEM_LIMIT, **kw)


def sds(shape, dtype):
    return jax.ShapeDtypeStruct(shape, dtype)


def cost(flops, nbytes, trans=0):
    return pl.CostEstimate(flops=int(flops), bytes_accessed=int(nbytes), transcendentals=int(trans))


def dot(a, b, ca, cb):
    return lax.dot_general(a, b, (((ca,), (cb,)), ((), ())), preferred_element_type=f32)


def fold(v):
    return jnp.sum(v.reshape(v.shape[0] // 8, 8, v.shape[1]), axis=0)


def rowsum(v):
    return jnp.sum(fold(v), axis=0, keepdims=True)


def gathered_rows(dst, refs, offs, base, tiles, rows, col):
    for s in range(OWN):
        ref, at = refs[s // 4], s % 4
        off = pl.multiple_of(offs[s] * rows, 16)
        for t in range(tiles):
            dst[pl.ds(off, rows), col + 128 * t : col + 128 * t + 128] = ref[
                at, base + t * rows : base + (t + 1) * rows, :
            ]


def scattered_rows(src, outs, offs, base, tiles, rows, col):
    for s in range(OWN):
        ref, at = outs[s // 8], s % 8
        off = pl.multiple_of(offs[s] * rows, 16)
        for t in range(tiles):
            ref[at, base + t * rows : base + (t + 1) * rows, :] = src[
                pl.ds(off, rows), col + 128 * t : col + 128 * t + 128
            ]


def pack_kernel(small, wq, wo, wu, wd, q0, q1, q2, o, f0, f1, f2):
    qs = (q0, q1, q2)
    fs = (f0, f1, f2)
    for g in range(3):
        for part in range(3):
            for t in range(2):
                c = D * part + 256 * g + 128 * t
                r = (2 * part + t) * RB
                qs[g][r : r + RB, :] = wq[:, c : c + 128].astype(bf16)
    q0[QR : QR + SR, :] = small[...].astype(bf16)
    for t in range(6):
        o[t * RB : (t + 1) * RB, :] = wo[:, 128 * t : 128 * t + 128].astype(bf16)
    for j in range(3):
        for t in range(8):
            a = wu[:, 384 * t + 64 * j : 384 * t + 64 * j + 64]
            b = wu[:, 384 * t + 192 + 64 * j : 384 * t + 192 + 64 * j + 64]
            fs[j][t * RB : (t + 1) * RB, :] = jnp.concatenate([a, b], axis=1).astype(bf16)
        for t in range(6):
            r = 8 * RB + t * FB
            fs[j][r : r + FB, :] = wd[FB * j : FB * j + FB, 128 * t : 128 * t + 128].astype(bf16)


def pack(small, wq, wo, wu, wd):
    small = jnp.pad(small, ((0, SR - small.shape[0]), (0, 128 - small.shape[1])))
    return pl.pallas_call(
        pack_kernel,
        out_shape=[sds((QR + SR, 128), bf16)]
        + [sds((QR, 128), bf16)] * 3
        + [sds((FR, 128), bf16)] * 3,
        in_specs=[VM] * 5,
        out_specs=[VM] * 7,
        compiler_params=params(),
        cost_estimate=cost(0, 6 << 20),
        name="pack",
    )(small, wq, wo, wu, wd)


def norm_kernel(offs, x, p0, p1, p2, p3, n1, n1t, small, *, base):
    @pl.when(pl.program_id(0) == 0)
    def _():
        acc = jnp.zeros((SR, D), f32)
        row = lax.broadcasted_iota(jnp.int32, (128, D), 0)
        col = lax.broadcasted_iota(jnp.int32, (128, D), 1)
        for s in range(OWN):
            ref = (p0, p1, p2, p3)[s // 4]
            hot = jnp.where((col == row + offs[s] * RB) & (row < RB), 1.0, 0.0).astype(bf16)
            acc += dot(ref[s % 4, base : base + SR, :], hot, 1, 0)
        small[...] = acc

    v = x[...].astype(f32)
    c = v - jnp.mean(v, -1, keepdims=True)
    r = lax.rsqrt(jnp.mean(c * c, -1, keepdims=True) + 1e-06)
    n = (c * r * small[0:1, :] + small[1:2, :]).astype(bf16)
    n1[...] = n
    n1t[...] = n.T


def norm_first(offs, x, pieces, base):
    whole = [pl.BlockSpec(p.shape, lambda r: (0, 0, 0)) for p in pieces]
    return pl.pallas_call(
        functools.partial(norm_kernel, base=base),
        grid=(NB,),
        out_shape=[sds((T, D), bf16), sds((D, T), bf16), sds((SR, D), f32)],
        in_specs=[SM, pl.BlockSpec((B, D), lambda r: (r, 0))] + whole,
        out_specs=[
            pl.BlockSpec((B, D), lambda r: (r, 0)),
            pl.BlockSpec((D, B), lambda r: (0, r)),
            pl.BlockSpec((SR, D), lambda r: (0, 0)),
        ],
        compiler_params=params(),
        cost_estimate=cost(1e7, 5 << 20),
        name="norm_first",
    )(offs, x, *pieces)


def segment_tail(segc, segr, minus):
    lane = lax.broadcasted_iota(jnp.int32, (T, 128), 1)
    left = jnp.where((segc[...] == lane) | ((lane >= 4) & (lane < 7)), 1.0, 0.0).astype(bf16)
    sub = lax.broadcasted_iota(jnp.int32, (16, T), 0)
    right = jnp.where((segr[...] != sub) & (sub < 4), -MASK, 0.0)
    return left, right


def three(v):
    hi = v.astype(bf16).astype(f32)
    rest = v - hi
    mid = rest.astype(bf16).astype(f32)
    return hi, mid, rest - mid


def attn_fwd_kernel(
    blk, offs, n1, p0, p1, p2, p3, small, segc, segr,
    q_o, k_o, v_o, mix_o, mixt_o, lse_o, w_o, kn, qt, vt, s_s, *, g,
):
    gathered_rows(w_o, (p0, p1, p2, p3), offs, 0, 6, RB, 0)
    qb = small[2:3, 256 * g : 256 * g + 256]
    vb = small[3:4, 256 * g : 256 * g + 256]
    q = (dot(n1[...], w_o[:, :256], 1, 0) + qb).astype(bf16)
    k = dot(n1[...], w_o[:, 256:512], 1, 0).astype(bf16)
    v = (dot(n1[...], w_o[:, 512:], 1, 0) + vb).astype(bf16)
    q_o[...] = q
    k_o[...] = k
    v_o[...] = v
    left, right = segment_tail(segc, segr, None)
    right = right.astype(bf16)
    qtt = (q * jnp.asarray(0.125, bf16)).T
    zero = jnp.zeros((64, T), bf16)
    pad = jnp.zeros((112, T), bf16)
    for p in range(2):
        kn[p, :, :128] = k[:, 128 * p : 128 * p + 128]
        kn[p, :, 128:] = left
        for e in range(2):
            h = 2 * p + e
            qt[h, 64 * e : 64 * e + 64, :] = qtt[64 * h : 64 * h + 64]
            qt[h, 64 - 64 * e : 128 - 64 * e, :] = zero
            qt[h, 128:144, :] = right
            qt[h, 144:, :] = pad
    vt[...] = v.T
    for i in range(NB):
        lo = blk[0, i]
        hi = blk[1, i]
        cols = slice(i * B, (i + 1) * B)

        def scores(j, tops):
            r = pl.ds(pl.multiple_of(j * B, B), B)
            out = []
            for h in range(4):
                s = dot(kn[h // 2, r, :], qt[h, :, cols], 1, 0)
                s_s[h, r, :] = s
                out.append(jnp.maximum(tops[h], jnp.max(s.reshape(B // 8, 8, B), axis=0)))
            return tuple(out)

        tops = lax.fori_loop(lo, hi, scores, tuple(jnp.full((8, B), -3e38, f32) for _ in range(4)))
        tops = [jnp.max(m, axis=0, keepdims=True) for m in tops]

        def mixing(j, carry):
            sums, accs = carry
            r = pl.ds(pl.multiple_of(j * B, B), B)
            new_sums, new_accs = [], []
            for h in range(4):
                e = jnp.exp(s_s[h, r, :] - tops[h])
                new_sums.append(sums[h] + fold(e))
                new_accs.append(accs[h] + dot(vt[64 * h : 64 * h + 64, r], e.astype(bf16), 1, 0))
            return tuple(new_sums), tuple(new_accs)

        zeros = (
            tuple(jnp.zeros((8, B), f32) for _ in range(4)),
            tuple(jnp.zeros((64, B), f32) for _ in range(4)),
        )
        sums, accs = lax.fori_loop(lo, hi, mixing, zeros)
        for h in range(4):
            total = jnp.sum(sums[h], axis=0, keepdims=True)
            mixt_o[64 * h : 64 * h + 64, cols] = (accs[h] / total).astype(bf16)
            lse_o[h : h + 1, cols] = tops[h] + jnp.log(total)
    mix_o[...] = mixt_o[...].T


def attn_fwd(g, blk, offs, n1, pieces, small, segc, segr):
    return pl.pallas_call(
        functools.partial(attn_fwd_kernel, g=g),
        out_shape=[sds((T, 256), bf16)] * 4
        + [sds((256, T), bf16), sds((4, T), f32), sds((D, D), bf16)],
        in_specs=[SM, SM] + [VM] * 8,
        out_specs=[VM] * 7,
        scratch_shapes=[
            pltpu.VMEM((2, T, 256), bf16),
            pltpu.VMEM((4, 256, T), bf16),
            pltpu.VMEM((256, T), bf16),
            pltpu.VMEM((4, T, B), f32),
        ],
        compiler_params=params(),
        cost_estimate=cost(9e9, 8 << 20, 4e6),
        name="attn_fwd",
    )(blk, offs, n1, *pieces, small, segc, segr)


def post_kernel(offs, x, m0, m1, m2, p0, p1, p2, p3, small, x1_o, n2_o, n2t_o, w):
    @pl.when(pl.program_id(0) == 0)
    def _():
        gathered_rows(w, (p0, p1, p2, p3), offs, 0, 6, RB, 0)

    a = x[...].astype(f32) + small[4:5, :]
    for g, m in enumerate((m0, m1, m2)):
        a += dot(m[...], w[256 * g : 256 * g + 256, :], 1, 0)
    x1_o[...] = a
    c = a - jnp.mean(a, -1, keepdims=True)
    r = lax.rsqrt(jnp.mean(c * c, -1, keepdims=True) + 1e-06)
    n = (c * r * small[5:6, :] + small[6:7, :]).astype(bf16)
    n2_o[...] = n
    n2t_o[...] = n.T


def post_attn(offs, x, mixes, pieces, small):
    rows = pl.BlockSpec((B, D), lambda r: (r, 0))
    part = pl.BlockSpec((B, 256), lambda r: (r, 0))
    return pl.pallas_call(
        post_kernel,
        grid=(NB,),
        out_shape=[sds((T, D), f32), sds((T, D), bf16), sds((D, T), bf16)],
        in_specs=[SM, rows, part, part, part]
        + [pl.BlockSpec(p.shape, lambda r: (0, 0, 0)) for p in pieces]
        + [pl.BlockSpec((SR, D), lambda r: (0, 0))],
        out_specs=[rows, rows, pl.BlockSpec((D, B), lambda r: (0, r))],
        scratch_shapes=[pltpu.VMEM((D, D), bf16)],
        compiler_params=params(),
        cost_estimate=cost(1.2e9, 10 << 20),
        name="post_attn",
    )(offs, x, *mixes, *pieces, small)


C0 = math.sqrt(2.0 / math.pi)
C1 = 0.044715


def ff_kernel(*refs, j, first):
    if first:
        offs, n2, n2t, dy, p0, p1, p2, p3, small = refs[:9]
        acc = None
        rest = refs[9:]
    else:
        offs, n2, n2t, dy, p0, p1, p2, p3, small, acc = refs[:10]
        rest = refs[10:]
    hid_o, acc_o, keep, send, wd, dub, wu, ub, n2ts, dys, ht, dp, gu, gd = rest
    step = pl.program_id(0)
    rows = pl.ds(pl.multiple_of(step * B, B), B)

    @pl.when(step == 0)
    def _():
        gathered_rows(wu, (p0, p1, p2, p3), offs, 0, 8, RB, 0)
        gathered_rows(wd, (p0, p1, p2, p3), offs, 8 * RB, 6, FB, 0)
        for t in range(8):
            halves = []
            for d in (2 * t, 2 * t + 1):
                c = 192 * (d % 4) + FB * j
                halves.append(small[8 + d // 4 : 9 + d // 4, c : c + FB])
            ub[0:1, 128 * t : 128 * t + 128] = jnp.concatenate(halves, axis=1)
        dub[...] = jnp.zeros_like(dub)

    n2ts[:, rows] = n2t[...]
    dys[rows, :] = dy[...]
    for c in range(4):
        cols = slice(256 * c, 256 * c + 256)
        pre = dot(n2[...], wu[:, cols], 1, 0) + ub[0:1, cols]
        dh = dot(dy[...], wd[cols, :], 1, 1)
        sq = pre * pre
        t = jnp.tanh(C0 * pre * (1.0 + C1 * sq))
        half = 0.5 + 0.5 * t
        hid = (pre * half).astype(bf16)
        slope = half + (0.5 * C0) * pre * (1.0 - t * t) * (1.0 + (3.0 * C1) * sq)
        dpre = dh * slope
        dub[0:8, cols] += fold(dpre)
        hid_o[:, cols] = hid
        ht[cols, rows] = hid.T
        dp[rows, cols] = dpre.astype(bf16)
    dn = dot(dp[rows, :], wu[...], 1, 1)
    acc_o[...] = dn if first else acc[...] + dn

    @pl.when(step == NB - 1)
    def _():
        gu[...] = dot(n2ts[...], dp[...], 1, 0).astype(bf16)
        gd[...] = dot(ht[...], dys[...], 1, 0).astype(bf16)
        scattered_rows(gu, (keep, send), offs, 0, 8, RB, 0)
        scattered_rows(gd, (keep, send), offs, 8 * RB, 6, FB, 0)


def feed_forward(j, offs, n2, n2t, dy, pieces, small, acc):
    rows = pl.BlockSpec((B, D), lambda r: (r, 0))
    extra = [] if acc is None else [rows]
    args = [] if acc is None else [acc]
    packed = pl.BlockSpec((8, FR, 128), lambda r: (0, 0, 0))
    return pl.pallas_call(
        functools.partial(ff_kernel, j=j, first=acc is None),
        grid=(NB,),
        out_shape=[
            sds((T, FC), bf16),
            sds((T, D), f32),
            sds((8, FR, 128), bf16),
            sds((8, FR, 128), bf16),
            sds((FC, D), bf16),
            sds((8, FC), f32),
        ],
        in_specs=[SM, rows, pl.BlockSpec((D, B), lambda r: (0, r)), rows]
        + [pl.BlockSpec(p.shape, lambda r: (0, 0, 0), pipeline_mode=pl.Buffered(1)) for p in pieces]
        + [pl.BlockSpec((SR, D), lambda r: (0, 0))]
        + extra,
        out_specs=[
            pl.BlockSpec((B, FC), lambda r: (r, 0)),
            rows,
            packed,
            packed,
            pl.BlockSpec((FC, D), lambda r: (0, 0)),
            pl.BlockSpec((8, FC), lambda r: (0, 0)),
        ],
        scratch_shapes=[
            pltpu.VMEM((D, FC), bf16),
            pltpu.VMEM((8, FC), f32),
            pltpu.VMEM((D, T), bf16),
            pltpu.VMEM((T, D), bf16),
            pltpu.VMEM((FC, T), bf16),
            pltpu.VMEM((T, FC), bf16),
            pltpu.VMEM((D, FC), bf16),
            pltpu.VMEM((FC, D), bf16),
        ],
        compiler_params=params(),
        cost_estimate=cost(9.7e9, 16 << 20, 1e6),
        name="feed_forward",
    )(offs, n2, n2t, dy, *pieces, small, *args)


def norm_back(v, up, gain):
    c = v - jnp.mean(v, -1, keepdims=True)
    r = lax.rsqrt(jnp.mean(c * c, -1, keepdims=True) + 1e-06)
    hat = c * r
    g = up * gain
    back = r * (g - jnp.mean(g, -1, keepdims=True) - hat * jnp.mean(g * hat, -1, keepdims=True))
    return back, up * hat


def mid_kernel(offs, dn2, x1, dy, t0, t1, t2, p0, p1, p2, p3, small,
               dx1_o, dmix_o, keep, send, sums, w, low, go):
    step = pl.program_id(0)
    rows = pl.ds(pl.multiple_of(step * B, B), B)

    @pl.when(step == 0)
    def _():
        gathered_rows(w, (p0, p1, p2, p3), offs, 0, 6, RB, 0)
        sums[...] = jnp.zeros_like(sums)

    d = dy[...].astype(f32)
    up = dn2[...]
    back, hats = norm_back(x1[...], up, small[5:6, :])
    dx1 = d + back
    dx1_o[...] = dx1
    lowered = dx1.astype(bf16)
    low[rows, :] = lowered
    sums[0:8, :] += fold(dx1)
    sums[8:16, :] += fold(hats)
    sums[16:24, :] += fold(up)
    sums[24:32, :] += fold(d)
    dmix_o[...] = dot(lowered, w[...], 1, 1).astype(bf16)

    @pl.when(step == NB - 1)
    def _():
        for g, t in enumerate((t0, t1, t2)):
            go[256 * g : 256 * g + 256, :] = dot(t[...], low[...], 1, 0).astype(bf16)
        scattered_rows(go, (keep, send), offs, 0, 6, RB, 0)


def middle(offs, dn2, x1, dy, mixts, pieces, small):
    rows = pl.BlockSpec((B, D), lambda r: (r, 0))
    packed = pl.BlockSpec((8, QR, 128), lambda r: (0, 0, 0))
    return pl.pallas_call(
        mid_kernel,
        grid=(NB,),
        out_shape=[
            sds((T, D), f32),
            sds((T, D), bf16),
            sds((8, QR, 128), bf16),
            sds((8, QR, 128), bf16),
            sds((32, D), f32),
        ],
        in_specs=[SM, rows, rows, rows]
        + [pl.BlockSpec((256, T), lambda r: (0, 0))] * 3
        + [pl.BlockSpec(p.shape, lambda r: (0, 0, 0)) for p in pieces]
        + [pl.BlockSpec((SR, D), lambda r: (0, 0))],
        out_specs=[rows, rows, packed, packed, pl.BlockSpec((32, D), lambda r: (0, 0))],
        scratch_shapes=[
            pltpu.VMEM((D, D), bf16),
            pltpu.VMEM((T, D), bf16),
            pltpu.VMEM((D, D), bf16),
        ],
        compiler_params=params(),
        cost_estimate=cost(2.4e9, 18 << 20),
        name="middle",
    )(offs, dn2, x1, dy, *mixts, *pieces, small)


def attn_bwd_kernel(
    blk, offs, q, k, v, do, mix, lse, n1t, segc, segr,
    dqkv_o, keep, send, sums, kn, vn, qt, dt, kt, qm, dm, dqt, gw,
):
    left, right = segment_tail(segc, segr, None)
    sub = lax.broadcasted_iota(jnp.int32, (16, T), 0)
    qs = q[...] * jnp.asarray(0.125, bf16)
    qtt = qs.T
    dtt = do[...].T
    kt[...] = k[...].T
    prod = (do[...].astype(f32) * mix[...].astype(f32)).T
    zero = jnp.zeros((64, T), bf16)
    pad = jnp.zeros((112, T), bf16)
    lane = lax.broadcasted_iota(jnp.int32, (T, 128), 1)
    nothing = jnp.zeros((T, 128), bf16)
    for p in range(2):
        at = slice(128 * p, 128 * p + 128)
        kn[p, :, :128] = k[:, at]
        kn[p, :, 128:] = left
        vn[p, :, :128] = v[:, at]
        vn[p, :, 128:] = left
        for e in range(2):
            h = 2 * p + e
            mine = (lane >= 64 * e) & (lane < 64 * e + 64)
            qm[p, e] = jnp.where(mine, qs[:, at], nothing)
            dm[p, e] = jnp.where(mine, do[:, at], nothing)
            for dst, src in ((qt, qtt), (dt, dtt)):
                dst[h, 64 * e : 64 * e + 64, :] = src[64 * h : 64 * h + 64]
                dst[h, 64 - 64 * e : 128 - 64 * e, :] = zero
                dst[h, 144:, :] = pad
            a, b, c = three(-lse[h : h + 1, :])
            tail = jnp.where(sub == 4, a, jnp.where(sub == 5, b, jnp.where(sub == 6, c, right)))
            qt[h, 128:144, :] = tail.astype(bf16)
            a, b, c = three(-rowsum(prod[64 * h : 64 * h + 64, :]))
            tail = jnp.where(sub == 4, a, jnp.where(sub == 5, b, jnp.where(sub == 6, c, 0.0)))
            dt[h, 128:144, :] = tail.astype(bf16)
    dqt[...] = jnp.zeros_like(dqt)
    for j in range(NB):
        lo = blk[0, j]
        hi = blk[1, j]
        keys = slice(j * B, (j + 1) * B)

        def step(i, carry):
            dks, dvs = carry
            cols = pl.ds(pl.multiple_of(i * B, B), B)
            new_dk, new_dv = [], []
            for p in range(2):
                dk, dv = dks[p], dvs[p]
                for e in range(2):
                    h = 2 * p + e
                    pr = jnp.exp(dot(kn[p, keys, :], qt[h, :, cols], 1, 0))
                    ds = (pr * dot(vn[p, keys, :], dt[h, :, cols], 1, 0)).astype(bf16)
                    dv += dot(pr.astype(bf16), dm[p, e, cols, :], 1, 0)
                    dk += dot(ds, qm[p, e, cols, :], 1, 0)
                    dqt[64 * h : 64 * h + 64, cols] += dot(kt[64 * h : 64 * h + 64, keys], ds, 1, 0)
                new_dk.append(dk)
                new_dv.append(dv)
            return tuple(new_dk), tuple(new_dv)

        zeros = tuple(jnp.zeros((B, 128), f32) for _ in range(2))
        dks, dvs = lax.fori_loop(lo, hi, step, (zeros, zeros))
        for p in range(2):
            dqkv_o[keys, 256 + 128 * p : 384 + 128 * p] = dks[p].astype(bf16)
            dqkv_o[keys, 512 + 128 * p : 640 + 128 * p] = dvs[p].astype(bf16)
    dqkv_o[:, :256] = (dqt[...] * 0.125).astype(bf16).T
    sums[:, :256] = fold(dqkv_o[:, :256].astype(f32))
    sums[:, 256:] = fold(dqkv_o[:, 512:].astype(f32))
    gw[...] = dot(n1t[...], dqkv_o[...], 1, 0).astype(bf16)
    scattered_rows(gw, (keep, send), offs, 0, 6, RB, 0)


def attn_bwd(g, blk, offs, q, k, v, dmix, mix, lse, n1t, segc, segr):
    whole = lambda a: pl.BlockSpec(a.shape, lambda r: (0,) * a.ndim)
    outs = [
        sds((T, D), bf16),
        sds((8, QR, 128), bf16),
        sds((8, QR, 128), bf16),
        sds((8, 512), f32),
    ]
    return pl.pallas_call(
        attn_bwd_kernel,
        grid=(1,),
        out_shape=outs,
        in_specs=[SM, SM, whole(q), whole(k), whole(v), pl.BlockSpec((T, 256), lambda r: (0, g))]
        + [whole(a) for a in (mix, lse, n1t, segc, segr)],
        out_specs=[whole(a) for a in outs],
        scratch_shapes=[
            pltpu.VMEM((2, T, 256), bf16),
            pltpu.VMEM((2, T, 256), bf16),
            pltpu.VMEM((4, 256, T), bf16),
            pltpu.VMEM((4, 256, T), bf16),
            pltpu.VMEM((256, T), bf16),
            pltpu.VMEM((2, 2, T, 128), bf16),
            pltpu.VMEM((2, 2, T, 128), bf16),
            pltpu.VMEM((256, T), f32),
            pltpu.VMEM((D, D), bf16),
        ],
        compiler_params=params(),
        cost_estimate=cost(16e9, 10 << 20, 4e6),
        name="attn_bwd",
    )(blk, offs, q, k, v, dmix, mix, lse, n1t, segc, segr)


def last_kernel(offs, d0, d1, d2, w0, w1, w2, x, dx1, small, mids, s0, s1, s2, u0, u1, u2,
                gt_o, keep, send, sums, sg):
    step = pl.program_id(0)

    @pl.when(step == 0)
    def _():
        sums[...] = jnp.zeros_like(sums)

    dn = dot(d0[...], w0[...], 1, 1) + dot(d1[...], w1[...], 1, 1) + dot(d2[...], w2[...], 1, 1)
    back, hats = norm_back(x[...].astype(f32), dn, small[0:1, :])
    gt_o[...] = (dx1[...] + back).astype(bf16)
    sums[0:8, :] += fold(hats)
    sums[8:16, :] += fold(dn)

    @pl.when(step == NB - 1)
    def _():
        total = lambda v: jnp.sum(v, axis=0, keepdims=True)
        sg[...] = jnp.zeros_like(sg)
        sg[0:1, :] = total(sums[0:8, :])
        sg[1:2, :] = total(sums[8:16, :])
        for g, s in enumerate((s0, s1, s2)):
            sg[2:3, 256 * g : 256 * g + 256] = total(s[:, :256])
            sg[3:4, 256 * g : 256 * g + 256] = total(s[:, 256:])
        for n in range(4):
            sg[4 + n : 5 + n, :] = total(mids[8 * n : 8 * n + 8, :])
        ups = [total(u[...]) for u in (u0, u1, u2)]
        for n in range(4):
            parts = []
            for d in range(4 * n, 4 * n + 4):
                for j in range(3):
                    parts.append(ups[j][:, FB * d : FB * d + FB])
            sg[8 + n : 9 + n, :] = jnp.concatenate(parts, axis=1)
        low = sg[...].astype(bf16)
        row = lax.broadcasted_iota(jnp.int32, (D, 128), 0)
        col = lax.broadcasted_iota(jnp.int32, (D, 128), 1)
        for s in range(OWN):
            hot = jnp.where((row == col + offs[s] * RB) & (col < RB), 1.0, 0.0).astype(bf16)
            (keep, send)[s // 8][s % 8, :, :] = dot(low, hot, 1, 0).astype(bf16)


def last_norm(offs, dqkvs, ws, x, dx1, small, mids, ssums, usums):
    rows = pl.BlockSpec((B, D), lambda r: (r, 0))
    whole = lambda a: pl.BlockSpec(a.shape, lambda r: (0,) * a.ndim)
    packed = pl.BlockSpec((8, SR, 128), lambda r: (0, 0, 0))
    return pl.pallas_call(
        last_kernel,
        grid=(NB,),
        out_shape=[sds((T, D), bf16), sds((8, SR, 128), bf16), sds((8, SR, 128), bf16)],
        in_specs=[SM] + [rows] * 3 + [whole(w) for w in ws] + [rows, rows]
        + [whole(a) for a in (small, mids, *ssums, *usums)],
        out_specs=[rows, packed, packed],
        scratch_shapes=[pltpu.VMEM((16, D), f32), pltpu.VMEM((SR, D), f32)],
        compiler_params=params(),
        cost_estimate=cost(3.6e9, 16 << 20),
        name="last_norm",
    )(offs, *dqkvs, *ws, x, dx1, small, mids, *ssums, *usums)


def out_kernel(h0, h1, h2, w0, w1, w2, x1, small, o):
    a = x1[...] + small[7:8, :]
    a += dot(h0[...], w0[...], 1, 0) + dot(h1[...], w1[...], 1, 0) + dot(h2[...], w2[...], 1, 0)
    o[...] = a.astype(bf16)


def layer_out(hids, wds, x1, small):
    rows = pl.BlockSpec((B, D), lambda r: (r, 0))
    return pl.pallas_call(
        out_kernel,
        grid=(NB,),
        out_shape=sds((T, D), bf16),
        in_specs=[pl.BlockSpec((B, FC), lambda r: (r, 0))] * 3
        + [pl.BlockSpec((FC, D), lambda r: (0, 0))] * 3
        + [rows, pl.BlockSpec((SR, D), lambda r: (0, 0))],
        out_specs=rows,
        compiler_params=params(),
        cost_estimate=cost(4.8e9, 16 << 20),
        name="layer_out",
    )(*hids, *wds, x1, small)


def adamw(weight, grad, mom_one, mom_two, rate):
    next_one = BETA1 * mom_one + (1.0 - BETA1) * grad
    next_two = BETA2 * mom_two + (1.0 - BETA2) * grad * grad
    fixed_one = next_one / (1.0 - BETA1**STEP)
    fixed_two = next_two / (1.0 - BETA2**STEP)
    updated = weight - rate * (fixed_one / (jnp.sqrt(fixed_two) + ADAM_EPS) + DECAY * weight)
    return (updated, next_one, next_two)


def adam_qkv_kernel(*refs):
    gs, (w, a, b), outs = refs[:6], refs[6:9], refs[9:12]
    for g in range(3):
        for part in range(3):
            for t in range(2):
                c = D * part + 256 * g + 128 * t
                r = (2 * part + t) * RB
                cols = slice(c, c + 128)
                grad = gs[2 * g][r : r + RB, :].astype(f32) + gs[2 * g + 1][r : r + RB, :].astype(f32)
                for o, val in zip(outs, adamw(w[:, cols], grad, a[:, cols], b[:, cols], RATES[0])):
                    o[:, cols] = val


def adam_out_kernel(g0, g1, w, a, b, *outs):
    for t in range(6):
        cols = slice(128 * t, 128 * t + 128)
        r = t * RB
        grad = g0[r : r + RB, :].astype(f32) + g1[r : r + RB, :].astype(f32)
        for o, val in zip(outs, adamw(w[:, cols], grad, a[:, cols], b[:, cols], RATES[1])):
            o[:, cols] = val


def adam_ff_kernel(*refs):
    gs = refs[:6]
    wu, au, bu, wd, ad, bd = refs[6:12]
    outs_up, outs_down = refs[12:15], refs[15:18]
    both = lambda j, r, n: gs[2 * j][r : r + n, :].astype(f32) + gs[2 * j + 1][r : r + n, :].astype(f32)
    for t in range(8):
        parts = [both(j, t * RB, RB) for j in range(3)]
        grad = jnp.concatenate([p[:, :64] for p in parts] + [p[:, 64:] for p in parts], axis=1)
        cols = slice(384 * t, 384 * t + 384)
        for o, val in zip(outs_up, adamw(wu[:, cols], grad, au[:, cols], bu[:, cols], RATES[2])):
            o[:, cols] = val
    for j in range(3):
        for t in range(6):
            grad = both(j, 8 * RB + t * FB, FB)
            at = (slice(FB * j, FB * j + FB), slice(128 * t, 128 * t + 128))
            for o, val in zip(outs_down, adamw(wd[at], grad, ad[at], bd[at], RATES[3])):
                o[at] = val


def adam_small_kernel(g0, g1, w, a, b, *outs):
    grad = g0[:12, :RB].astype(f32) + g1[:12, :RB].astype(f32)
    for o, val in zip(outs, adamw(w[...], grad, a[...], b[...], RATES[4])):
        o[...] = val


def adam_call(kernel, grads, states, name):
    shapes = [sds(s.shape, f32) for s in states]
    return pl.pallas_call(
        kernel,
        out_shape=shapes,
        in_specs=[VM] * (len(grads) + len(states)),
        out_specs=[VM] * len(shapes),
        compiler_params=params(),
        cost_estimate=cost(1e6, sum(8 * s.size for s in states)),
        name=name,
    )(*grads, *states)


def shifted(f):
    pairs = []
    for z in range(4):
        for x in range(2):
            for c in range(2):
                tz, tx, tc = f(z, x, c)
                pairs.append(((z * 2 + x) * 2 + c, (tz * 2 + tx) * 2 + tc))
    return pairs


TO_CORE = shifted(lambda z, x, c: (z, x, 1 - c))
TO_X = shifted(lambda z, x, c: (z, 1 - x, c))
TO_Z = [shifted(lambda z, x, c, s=s: ((z + s) % 4, x, c)) for s in range(4)]
FROM_Z = [shifted(lambda z, x, c, s=s: ((z - s) % 4, x, c)) for s in range(4)]
TO_Y = [(0, 1), (1, 0)]


def gather_blocks(own):
    parts = [own] + [lax.ppermute(own, "dp", TO_Z[s]) for s in (1, 2, 3)]
    line = jnp.stack(parts)
    side = lax.ppermute(line, "dp", TO_X)
    return line, side, lax.ppermute(line, "dp", TO_CORE), lax.ppermute(side, "dp", TO_CORE)


def add_first_kernel(keep, got, a, b):
    a[...] = (keep[:4].astype(f32) + got[:4].astype(f32)).astype(bf16)
    b[...] = (keep[4:].astype(f32) + got[4:].astype(f32)).astype(bf16)


def add_second_kernel(keep, got, *outs):
    for s in range(4):
        outs[s][...] = (keep[s].astype(f32) + got[s].astype(f32)).astype(bf16)


def add_third_kernel(a, b, c, d, o):
    o[...] = (a[...].astype(f32) + b[...].astype(f32) + c[...].astype(f32) + d[...].astype(f32)).astype(bf16)


def add_call(kernel, args, outs, name):
    out = pl.pallas_call(
        kernel,
        out_shape=outs,
        in_specs=[VM] * len(args),
        out_specs=[VM] * len(outs),
        compiler_params=params(),
        cost_estimate=cost(1e6, sum(2 * a.size for a in args)),
        name=name,
    )(*args)
    return out


def scatter_blocks(keep, send):
    rows = keep.shape[1]
    got = lax.ppermute(send, "dp", TO_CORE)
    mine, other = add_call(add_first_kernel, (keep, got), [sds((4, rows, 128), bf16)] * 2, "add_core")
    got = lax.ppermute(other, "dp", TO_X)
    parts = add_call(add_second_kernel, (mine, got), [sds((rows, 128), bf16)] * 4, "add_x")
    got = [lax.ppermute(parts[s], "dp", FROM_Z[s]) for s in (1, 2, 3)]
    (own,) = add_call(add_third_kernel, (parts[0], *got), [sds((rows, 128), bf16)], "add_z")
    return own, lax.ppermute(own, "rep", TO_Y)


def gather_any(small, wq, wo, wu, wd):
    full = lambda w, axis: lax.all_gather(w.astype(bf16), "dp", axis=axis, tiled=True)
    small = full(small, 1)
    blocks = small.reshape(small.shape[0], OWN, RB).transpose(1, 0, 2)
    blocks = jnp.pad(blocks, ((0, 0), (0, SR - small.shape[0]), (0, 128 - RB)))
    q = full(wq, 0).reshape(OWN, RB, 3, 3, 2, 128).transpose(3, 0, 2, 4, 1, 5).reshape(3, OWN, QR, 128)
    o = full(wo, 0).reshape(OWN, RB, 6, 128).transpose(0, 2, 1, 3).reshape(OWN, QR, 128)
    u = full(wu, 0).reshape(OWN, RB, 8, 2, 3, FB).transpose(4, 0, 2, 1, 3, 5).reshape(3, OWN, 8 * RB, 128)
    d = full(wd, 0).reshape(OWN, 3, FB, 6, 128).transpose(1, 0, 3, 2, 4).reshape(3, OWN, 6 * FB, 128)
    f = jnp.concatenate([u, d], 2)
    first = jnp.concatenate([q[0], blocks], 1)
    cut = lambda a: tuple(a[4 * n : 4 * n + 4] for n in range(4))
    return cut(first), cut(q[1]), cut(q[2]), cut(o), cut(f[0]), cut(f[1]), cut(f[2])


def scatter_any(packs):
    q0, q1, q2, o, f0, f1, f2, s = [jnp.concatenate(p, 0) for p in packs]
    q = jnp.stack([q0, q1, q2]).reshape(3, OWN, 3, 2, RB, 128).transpose(1, 4, 2, 0, 3, 5)
    f = jnp.stack([f0, f1, f2])
    u = f[:, :, : 8 * RB].reshape(3, OWN, 8, RB, 2, FB).transpose(1, 3, 2, 4, 0, 5)
    d = f[:, :, 8 * RB :].reshape(3, OWN, 6, FB, 128).transpose(1, 0, 3, 2, 4)
    o = o.reshape(OWN, 6, RB, 128).transpose(0, 2, 1, 3)
    s = s[:, :12, :RB].transpose(1, 0, 2).reshape(12, D)
    flat = ((q.reshape(D, 3 * D), 0), (o.reshape(D, D), 0), (u.reshape(D, FF), 0), (d.reshape(FF, D), 0), (s, 1))
    out = []
    for g, axis in flat:
        g = lax.psum_scatter(g, "dp", scatter_dimension=axis, tiled=True)
        out.append(lax.psum(g, "rep").astype(f32))
    return out


def shards(tokens, segment_ids, cotangent, *state, wide):
    masters, firsts, seconds = state[:5], state[5:10], state[10:15]
    w_qkv, w_out, w_up, w_down, small_params = masters
    x = tokens[0]
    dy = cotangent[0]
    seg = segment_ids[0]
    segc = seg.reshape(T, 1)
    segr = seg.reshape(1, T)
    begins, ends = seg[::B], seg[B - 1 :: B]
    low = jnp.sum(ends[None, :] < begins[:, None], 1)
    high = jnp.sum(begins[None, :] <= ends[:, None], 1)
    blk = jnp.stack([low, high]).astype(jnp.int32)

    if wide:
        me = lax.axis_index("dp")
        s = jnp.arange(OWN, dtype=jnp.int32)
        z = (me // 4 - s % 4) % 4
        xx = (me // 2 % 2) ^ (s // 4 % 2)
        cc = (me % 2) ^ (s // 8)
        offs = ((z * 2 + xx) * 2 + cc).astype(jnp.int32)
        owns = pack(small_params, w_qkv, w_out, w_up, w_down)
        pieces = [gather_blocks(own) for own in owns]
    else:
        offs = jnp.arange(OWN, dtype=jnp.int32)
        pieces = gather_any(small_params, w_qkv, w_out, w_up, w_down)

    n1, n1t, small = norm_first(offs, x, pieces[0], QR)
    fwd = [attn_fwd(g, blk, offs, n1, pieces[g], small, segc, segr) for g in range(3)]
    x1, n2, n2t = post_attn(offs, x, [f[3] for f in fwd], pieces[3], small)
    acc = None
    ffs = []
    for j in range(3):
        hid, acc, keep, send, wd, dub = feed_forward(j, offs, n2, n2t, dy, pieces[4 + j], small, acc)
        ffs.append((hid, keep, send, wd, dub))
    dx1, dmix, keep_o, send_o, mids = middle(offs, acc, x1, dy, [f[4] for f in fwd], pieces[3], small)
    bwd = []
    for g in range(3):
        q, k, v, mix, _, lse, _ = fwd[g]
        bwd.append(attn_bwd(g, blk, offs, q, k, v, dmix, mix, lse, n1t, segc, segr))
    grad_tokens, keep_s, send_s = last_norm(
        offs, [b[0] for b in bwd], [f[6] for f in fwd], x, dx1, small, mids,
        [b[3] for b in bwd], [f[4] for f in ffs],
    )
    result = layer_out([f[0] for f in ffs], [f[3] for f in ffs], x1, small)
    packs = [(b[1], b[2]) for b in bwd] + [(keep_o, send_o)] + [(f[1], f[2]) for f in ffs] + [(keep_s, send_s)]
    states = [(masters[n], firsts[n], seconds[n]) for n in range(5)]
    if wide:
        done = [scatter_blocks(*p) for p in packs]
        flat = lambda items: [a for pair in items for a in pair]
        new = [None] * 5
        new[0] = adam_call(adam_qkv_kernel, flat(done[:3]), states[0], "adam_qkv")
        new[1] = adam_call(adam_out_kernel, done[3], states[1], "adam_out")
        both = adam_call(adam_ff_kernel, flat(done[4:7]), states[2] + states[3], "adam_ff")
        new[2], new[3] = both[:3], both[3:]
        new[4] = adam_call(adam_small_kernel, done[7], states[4], "adam_small")
    else:
        owned = scatter_any(packs)
        new = [adamw(states[n][0], owned[n], states[n][1], states[n][2], RATES[n]) for n in range(5)]
    return (
        result[None],
        grad_tokens[None],
        *[n[0] for n in new],
        *[n[1] for n in new],
        *[n[2] for n in new],
    )


def solution(mesh):
    rows = P("dp", None)
    small = P(None, "dp")
    state = (rows, rows, rows, rows, small)
    seqs = P(("dp", "rep"), None, None)
    return jax.shard_map(
        functools.partial(shards, wide=mesh.shape["dp"] == 16 and mesh.shape["rep"] == 2),
        mesh=mesh,
        in_specs=(seqs, P(("dp", "rep"), None), seqs) + state * 3,
        out_specs=(seqs, seqs) + state * 3,
        check_vma=False,
    )
```

```python
import functools
import math

import jax
import jax.numpy as jnp
from jax import lax
from jax.experimental import pallas as pl
from jax.experimental.pallas import tpu as pltpu
from jax.sharding import PartitionSpec as P

HEADS = 12
STEP = 10
BETA1 = 0.5
BETA2 = 0.5
ADAM_EPS = 1e-08
DECAY = 0.05
RATES = (0.04, 0.15, 0.04, 0.02, 0.3)

bf16 = jnp.bfloat16
f32 = jnp.float32

T = 1024
D = 768
FF = 3072
OWN = 16
RB = D // OWN
FB = FF // OWN // 3
FC = FF // 3
QR = 6 * RB
FR = 8 * RB + 6 * FB
SR = 16
B = 256
NB = T // B
MASK = 2.0**30
VMEM_LIMIT = 56 << 20

VM = pl.BlockSpec(memory_space=pltpu.VMEM)
SM = pl.BlockSpec(memory_space=pltpu.SMEM)


def params(**kw):
    return pltpu.CompilerParams(vmem_limit_bytes=VMEM_LIMIT, **kw)


ORDER = []
SIDE = []


def call(kernel, args, *, in_specs, out_specs, out_shape, main=False, token=None, **kw):
    side = list(SIDE) if main else []
    if main:
        SIDE.clear()
    extra = list(ORDER)
    single = not isinstance(out_shape, (list, tuple))
    shapes = [out_shape] if single else list(out_shape)
    specs = [out_specs] if single else list(out_specs)
    n, m = len(args), len(shapes)
    side_args = [a for _, more, _, _ in side for a in more]
    side_outs = [o for _, _, outs, _ in side for o in outs]
    grid = "grid" in kw
    whole = lambda a: pl.BlockSpec(a.shape, lambda r, k=len(a.shape): (0,) * k) if grid else VM

    def body(*refs):
        ins = refs[n : n + len(side_args)]
        rest = refs[n + len(side_args) + len(extra) :]
        outs = rest[m : m + len(side_outs)]

        def beside():
            i = o = 0
            for fn, more, results, _ in side:
                fn(*ins[i : i + len(more)], *outs[o : o + len(results)])
                i += len(more)
                o += len(results)

        if side:
            if grid:
                pl.when(pl.program_id(0) == 0)(beside)
            else:
                beside()
        return kernel(*refs[:n], *rest[:m], *rest[m + len(side_outs) :])

    out = pl.pallas_call(
        body,
        in_specs=list(in_specs)
        + [whole(a) for a in side_args]
        + [pl.BlockSpec(memory_space=pl.ANY)] * len(extra),
        out_specs=specs + [whole(a) for a in side_outs],
        out_shape=shapes + side_outs,
        **kw,
    )(*args, *side_args, *extra)
    out = list(out)
    ORDER[:] = [min(out[:m], key=lambda a: a.size) if token is None else out[token]]
    at = m
    for _, _, results, then in side:
        then(out[at : at + len(results)])
        at += len(results)
    return out[0] if single else out[:m]


def wait_here(*arrays):
    anywhere = pl.BlockSpec(memory_space=pl.ANY)
    order = list(ORDER)
    out = call(
        lambda *refs: None,
        arrays,
        out_shape=[sds(a.shape, a.dtype) for a in arrays],
        in_specs=[anywhere] * len(arrays),
        out_specs=[anywhere] * len(arrays),
        input_output_aliases={n: n for n in range(len(arrays))},
        name="wait_here",
    )
    ORDER[:] = order
    return out


def sds(shape, dtype):
    return jax.ShapeDtypeStruct(shape, dtype)


PACE = 0.7


def cost(us=3.0):
    return pl.CostEstimate(flops=int(us * PACE * 1e9), bytes_accessed=1, transcendentals=0)


def dot(a, b, ca, cb):
    return lax.dot_general(a, b, (((ca,), (cb,)), ((), ())), preferred_element_type=f32)


def fold(v):
    return jnp.sum(v.reshape(v.shape[0] // 8, 8, v.shape[1]), axis=0)


def rowsum(v):
    return jnp.sum(fold(v), axis=0, keepdims=True)


def gathered_rows(dst, refs, offs, base, tiles, rows, col):
    per = OWN // len(refs)
    for s in range(OWN):
        ref, at = refs[s // per], s % per
        off = s * rows if offs is None else pl.multiple_of(offs[s] * rows, 16)
        for t in range(tiles):
            dst[pl.ds(off, rows), col + 128 * t : col + 128 * t + 128] = ref[
                at, base + t * rows : base + (t + 1) * rows, :
            ]


def scattered_rows(src, outs, offs, base, tiles, rows, col):
    per = OWN // len(outs)
    for s in range(OWN):
        ref, at = outs[s // per], s % per
        off = s * rows if offs is None else pl.multiple_of(offs[s] * rows, 16)
        for t in range(tiles):
            ref[at, base + t * rows : base + (t + 1) * rows, :] = src[
                pl.ds(off, rows), col + 128 * t : col + 128 * t + 128
            ]


def pack_heads(dst, at, wq, g):
    for part in range(3):
        for t in range(2):
            c = D * part + 256 * g + 128 * t
            r = at + (2 * part + t) * RB
            dst[r : r + RB, :] = wq[:, c : c + 128].astype(bf16)


def pack_kernel(small, wq, wo, wu, wd, q0, q12, rest, token):
    token[...] = jnp.zeros_like(token)
    pack_heads(q0, 0, wq, 0)
    q0[QR : QR + SR, :] = jnp.zeros((SR, 128), bf16)
    q0[QR : QR + 12, :RB] = small[...].astype(bf16)
    pack_heads(q12, 0, wq, 1)
    pack_heads(q12, QR, wq, 2)
    for j in range(3):
        for t in range(8):
            r = FR * j + t * RB
            a = wu[:, 384 * t + 64 * j : 384 * t + 64 * j + 64]
            b = wu[:, 384 * t + 192 + 64 * j : 384 * t + 192 + 64 * j + 64]
            rest[r : r + RB, :] = jnp.concatenate([a, b], axis=1).astype(bf16)
        for t in range(6):
            r = FR * j + 8 * RB + t * FB
            rest[r : r + FB, :] = wd[FB * j : FB * j + FB, 128 * t : 128 * t + 128].astype(bf16)
    for t in range(6):
        r = 3 * FR + t * RB
        rest[r : r + RB, :] = wo[:, 128 * t : 128 * t + 128].astype(bf16)


def pack(*args):
    rows = (QR + SR, 2 * QR, 3 * FR + QR, 16)
    return call(
        pack_kernel,
        args,
        out_shape=[sds((r, 128), bf16) for r in rows],
        in_specs=[VM] * len(args),
        out_specs=[VM] * len(rows),
        compiler_params=params(),
        cost_estimate=cost(2.4),
        name="pack",
    )[:3]


def norm_kernel(offs, x, p0, p1, p2, p3, n1, n1t, small, *, base):
    @pl.when(pl.program_id(0) == 0)
    def _():
        acc = jnp.zeros((SR, D), f32)
        row = lax.broadcasted_iota(jnp.int32, (128, D), 0)
        col = lax.broadcasted_iota(jnp.int32, (128, D), 1)
        for s in range(OWN):
            ref = (p0, p1, p2, p3)[s // 4]
            hot = jnp.where((col == row + offs[s] * RB) & (row < RB), 1.0, 0.0).astype(bf16)
            acc += dot(ref[s % 4, base : base + SR, :], hot, 1, 0)
        small[...] = acc

    v = x[...].astype(f32)
    c = v - jnp.mean(v, -1, keepdims=True)
    r = lax.rsqrt(jnp.mean(c * c, -1, keepdims=True) + 1e-06)
    n = (c * r * small[0:1, :] + small[1:2, :]).astype(bf16)
    n1[...] = n
    n1t[...] = n.T


def norm_first(offs, x, pieces, base):
    whole = [pl.BlockSpec(p.shape, lambda r: (0, 0, 0)) for p in pieces]
    return call(
        functools.partial(norm_kernel, base=base),
        [offs, x, *pieces],
        grid=(NB,),
        out_shape=[sds((T, D), bf16), sds((D, T), bf16), sds((SR, D), f32)],
        in_specs=[SM, pl.BlockSpec((B, D), lambda r: (r, 0))] + whole,
        out_specs=[
            pl.BlockSpec((B, D), lambda r: (r, 0)),
            pl.BlockSpec((D, B), lambda r: (0, r)),
            pl.BlockSpec((SR, D), lambda r: (0, 0)),
        ],
        compiler_params=params(),
        cost_estimate=cost(5),
        name="norm_first",
    )


def segment_tail(segc, segr, minus):
    lane = lax.broadcasted_iota(jnp.int32, (T, 128), 1)
    left = jnp.where((segc[...] == lane) | ((lane >= 4) & (lane < 7)), 1.0, 0.0).astype(bf16)
    sub = lax.broadcasted_iota(jnp.int32, (16, T), 0)
    right = jnp.where((segr[...] != sub) & (sub < 4), -MASK, 0.0)
    return left, right


def three(v):
    hi = v.astype(bf16).astype(f32)
    rest = v - hi
    mid = rest.astype(bf16).astype(f32)
    return hi, mid, rest - mid


def attn_fwd_kernel(
    blk, offs, n1, p0, p1, p2, p3, small, segc, segr,
    q_o, k_o, v_o, mix_o, mixt_o, lse_o, w_o, kn, qt, vt, s_s, *, g,
):
    gathered_rows(w_o, (p0, p1, p2, p3), offs, QR if g == 2 else 0, 6, RB, 0)
    qb = small[2:3, 256 * g : 256 * g + 256]
    vb = small[3:4, 256 * g : 256 * g + 256]
    q = (dot(n1[...], w_o[:, :256], 1, 0) + qb).astype(bf16)
    k = dot(n1[...], w_o[:, 256:512], 1, 0).astype(bf16)
    v = (dot(n1[...], w_o[:, 512:], 1, 0) + vb).astype(bf16)
    q_o[...] = q
    k_o[...] = k
    v_o[...] = v
    left, right = segment_tail(segc, segr, None)
    right = right.astype(bf16)
    qtt = (q * jnp.asarray(0.125, bf16)).T
    zero = jnp.zeros((64, T), bf16)
    pad = jnp.zeros((112, T), bf16)
    for p in range(2):
        kn[p, :, :128] = k[:, 128 * p : 128 * p + 128]
        kn[p, :, 128:] = left
        for e in range(2):
            h = 2 * p + e
            qt[h, 64 * e : 64 * e + 64, :] = qtt[64 * h : 64 * h + 64]
            qt[h, 64 - 64 * e : 128 - 64 * e, :] = zero
            qt[h, 128:144, :] = right
            qt[h, 144:, :] = pad
    vt[...] = v.T
    for i in range(NB):
        lo = blk[0, i]
        hi = blk[1, i]
        cols = slice(i * B, (i + 1) * B)

        def scores(j, tops):
            r = pl.ds(pl.multiple_of(j * B, B), B)
            out = []
            for h in range(4):
                s = dot(kn[h // 2, r, :], qt[h, :, cols], 1, 0)
                s_s[h, r, :] = s
                out.append(jnp.maximum(tops[h], jnp.max(s.reshape(B // 8, 8, B), axis=0)))
            return tuple(out)

        tops = lax.fori_loop(lo, hi, scores, tuple(jnp.full((8, B), -3e38, f32) for _ in range(4)))
        tops = [jnp.max(m, axis=0, keepdims=True) for m in tops]

        def mixing(j, carry):
            sums, accs = carry
            r = pl.ds(pl.multiple_of(j * B, B), B)
            new_sums, new_accs = [], []
            for h in range(4):
                e = jnp.exp(s_s[h, r, :] - tops[h])
                new_sums.append(sums[h] + fold(e))
                new_accs.append(accs[h] + dot(vt[64 * h : 64 * h + 64, r], e.astype(bf16), 1, 0))
            return tuple(new_sums), tuple(new_accs)

        zeros = (
            tuple(jnp.zeros((8, B), f32) for _ in range(4)),
            tuple(jnp.zeros((64, B), f32) for _ in range(4)),
        )
        sums, accs = lax.fori_loop(lo, hi, mixing, zeros)
        for h in range(4):
            total = jnp.sum(sums[h], axis=0, keepdims=True)
            mixt_o[64 * h : 64 * h + 64, cols] = (accs[h] / total).astype(bf16)
            lse_o[h : h + 1, cols] = tops[h] + jnp.log(total)
    mix_o[...] = mixt_o[...].T


def attn_fwd(g, blk, offs, n1, pieces, small, segc, segr):
    return call(
        functools.partial(attn_fwd_kernel, g=g),
        [blk, offs, n1, *pieces, small, segc, segr],
        out_shape=[sds((T, 256), bf16)] * 4
        + [sds((256, T), bf16), sds((4, T), f32), sds((D, D), bf16)],
        in_specs=[SM, SM] + [VM] * 8,
        out_specs=[VM] * 7,
        scratch_shapes=[
            pltpu.VMEM((2, T, 256), bf16),
            pltpu.VMEM((4, 256, T), bf16),
            pltpu.VMEM((256, T), bf16),
            pltpu.VMEM((4, T, B), f32),
        ],
        compiler_params=params(),
        cost_estimate=cost(13),
        name="attn_fwd",
        main=True,
    )


def post_kernel(x, m0, m1, m2, rest, small, x1_o, n2_o, n2t_o, w):
    @pl.when(pl.program_id(0) == 0)
    def _():
        gathered_rows(w, (rest,), None, 0, 6, RB, 0)

    a = x[...].astype(f32) + small[4:5, :]
    for g, m in enumerate((m0, m1, m2)):
        a += dot(m[...], w[256 * g : 256 * g + 256, :], 1, 0)
    x1_o[...] = a
    c = a - jnp.mean(a, -1, keepdims=True)
    r = lax.rsqrt(jnp.mean(c * c, -1, keepdims=True) + 1e-06)
    n = (c * r * small[5:6, :] + small[6:7, :]).astype(bf16)
    n2_o[...] = n
    n2t_o[...] = n.T


def post_attn(x, mixes, rest, small):
    rows = pl.BlockSpec((B, D), lambda r: (r, 0))
    part = pl.BlockSpec((B, 256), lambda r: (r, 0))
    return call(
        post_kernel,
        [x, *mixes, rest, small],
        grid=(NB,),
        out_shape=[sds((T, D), f32), sds((T, D), bf16), sds((D, T), bf16)],
        in_specs=[rows, part, part, part, pl.BlockSpec((OWN, QR, 128), lambda r: (0, 3 * FR // QR, 0))]
        + [pl.BlockSpec((SR, D), lambda r: (0, 0))],
        out_specs=[rows, rows, pl.BlockSpec((D, B), lambda r: (0, r))],
        scratch_shapes=[pltpu.VMEM((D, D), bf16)],
        compiler_params=params(),
        cost_estimate=cost(6.5),
        name="post_attn",
        main=True,
    )


C0 = math.sqrt(2.0 / math.pi)
C1 = 0.044715


def ff_kernel(*refs, j):
    offs, n2, n2t, dy, rest, small = refs[:6]
    acc = refs[6] if j else None
    wu, ub, n2ts, dys, ht, dp, gu, gd = refs[-8:]
    hid_o, acc_o, wd, dub = refs[-12 - (2 if j == 2 else 1) : -8][:4]
    grads = refs[-10:-8] if j == 2 else refs[-9:-8]
    order = offs if j == 2 else None
    step = pl.program_id(0)
    rows = pl.ds(pl.multiple_of(step * B, B), B)

    @pl.when(step == 0)
    def _():
        gathered_rows(wu, (rest,), None, 0, 8, RB, 0)
        gathered_rows(wd, (rest,), None, 8 * RB, 6, FB, 0)
        for t in range(8):
            halves = []
            for d in (2 * t, 2 * t + 1):
                c = 192 * (d % 4) + FB * j
                halves.append(small[8 + d // 4 : 9 + d // 4, c : c + FB])
            ub[0:1, 128 * t : 128 * t + 128] = jnp.concatenate(halves, axis=1)
        dub[...] = jnp.zeros_like(dub)

    n2ts[:, rows] = n2t[...]
    dys[rows, :] = dy[...]
    for c in range(4):
        cols = slice(256 * c, 256 * c + 256)
        pre = dot(n2[...], wu[:, cols], 1, 0) + ub[0:1, cols]
        dh = dot(dy[...], wd[cols, :], 1, 1)
        sq = pre * pre
        t = jnp.tanh(C0 * pre * (1.0 + C1 * sq))
        half = 0.5 + 0.5 * t
        hid = (pre * half).astype(bf16)
        slope = half + (0.5 * C0) * pre * (1.0 - t * t) * (1.0 + (3.0 * C1) * sq)
        dpre = dh * slope
        dub[0:8, cols] += fold(dpre)
        hid_o[:, cols] = hid
        ht[cols, rows] = hid.T
        dp[rows, cols] = dpre.astype(bf16)
    dn = dot(dp[rows, :], wu[...], 1, 1)
    acc_o[...] = acc[...] + dn if j else dn

    @pl.when(step == NB - 1)
    def _():
        gu[...] = dot(n2ts[...], dp[...], 1, 0).astype(bf16)
        gd[...] = dot(ht[...], dys[...], 1, 0).astype(bf16)
        scattered_rows(gu, grads, order, 0, 8, RB, 0)
        scattered_rows(gd, grads, order, 8 * RB, 6, FB, 0)


def feed_forward(j, offs, n2, n2t, dy, rest, small, acc, grads):
    rows = pl.BlockSpec((B, D), lambda r: (r, 0))
    chunk = pl.BlockSpec((OWN, FR, 128), lambda r: (0, j, 0), pipeline_mode=pl.Buffered(1))
    extra = [rows] if j else []
    args = [acc] if j else []
    if j == 1:
        extra.append(pl.BlockSpec(memory_space=pl.ANY))
        args.append(grads)
    if j == 2:
        shapes = [sds((8, FR, 128), bf16)] * 2
        specs = [pl.BlockSpec((8, FR, 128), lambda r: (0, 0, 0))] * 2
    else:
        shapes = [sds((OWN, 2 * FR, 128), bf16)]
        specs = [pl.BlockSpec((OWN, FR, 128), lambda r: (0, j, 0))]
    return call(
        functools.partial(ff_kernel, j=j),
        [offs, n2, n2t, dy, rest, small, *args],
        grid=(NB,),
        out_shape=[sds((T, FC), bf16), sds((T, D), f32), sds((FC, D), bf16), sds((8, FC), f32)] + shapes,
        in_specs=[SM, rows, pl.BlockSpec((D, B), lambda r: (0, r)), rows, chunk]
        + [pl.BlockSpec((SR, D), lambda r: (0, 0))]
        + extra,
        input_output_aliases={7: 4} if j == 1 else {},
        out_specs=[
            pl.BlockSpec((B, FC), lambda r: (r, 0)),
            rows,
            pl.BlockSpec((FC, D), lambda r: (0, 0)),
            pl.BlockSpec((8, FC), lambda r: (0, 0)),
        ]
        + specs,
        scratch_shapes=[
            pltpu.VMEM((D, FC), bf16),
            pltpu.VMEM((8, FC), f32),
            pltpu.VMEM((D, T), bf16),
            pltpu.VMEM((T, D), bf16),
            pltpu.VMEM((FC, T), bf16),
            pltpu.VMEM((T, FC), bf16),
            pltpu.VMEM((D, FC), bf16),
            pltpu.VMEM((FC, D), bf16),
        ],
        compiler_params=params(),
        cost_estimate=cost(17),
        name="feed_forward",
        main=True,
    )


def norm_back(v, up, gain):
    c = v - jnp.mean(v, -1, keepdims=True)
    r = lax.rsqrt(jnp.mean(c * c, -1, keepdims=True) + 1e-06)
    hat = c * r
    g = up * gain
    back = r * (g - jnp.mean(g, -1, keepdims=True) - hat * jnp.mean(g * hat, -1, keepdims=True))
    return back, up * hat


def mid_kernel(offs, dn2, x1, dy, t0, t1, t2, rest, small,
               dx1_o, dmix_o, keep, send, sums, w, low, go):
    step = pl.program_id(0)
    rows = pl.ds(pl.multiple_of(step * B, B), B)

    @pl.when(step == 0)
    def _():
        gathered_rows(w, (rest,), None, 0, 6, RB, 0)
        sums[...] = jnp.zeros_like(sums)

    d = dy[...].astype(f32)
    up = dn2[...]
    back, hats = norm_back(x1[...], up, small[5:6, :])
    dx1 = d + back
    dx1_o[...] = dx1
    lowered = dx1.astype(bf16)
    low[rows, :] = lowered
    sums[0:8, :] += fold(dx1)
    sums[8:16, :] += fold(hats)
    sums[16:24, :] += fold(up)
    sums[24:32, :] += fold(d)
    dmix_o[...] = dot(lowered, w[...], 1, 1).astype(bf16)

    @pl.when(step == NB - 1)
    def _():
        for g, t in enumerate((t0, t1, t2)):
            go[256 * g : 256 * g + 256, :] = dot(t[...], low[...], 1, 0).astype(bf16)
        scattered_rows(go, (keep, send), offs, 0, 6, RB, 0)


def middle(offs, dn2, x1, dy, mixts, rest, small):
    rows = pl.BlockSpec((B, D), lambda r: (r, 0))
    packed = pl.BlockSpec((8, QR, 128), lambda r: (0, 0, 0))
    return call(
        mid_kernel,
        [offs, dn2, x1, dy, *mixts, rest, small],
        grid=(NB,),
        out_shape=[
            sds((T, D), f32),
            sds((T, D), bf16),
            sds((8, QR, 128), bf16),
            sds((8, QR, 128), bf16),
            sds((32, D), f32),
        ],
        in_specs=[SM, rows, rows, rows]
        + [pl.BlockSpec((256, T), lambda r: (0, 0))] * 3
        + [pl.BlockSpec((OWN, QR, 128), lambda r: (0, 3 * FR // QR, 0))]
        + [pl.BlockSpec((SR, D), lambda r: (0, 0))],
        out_specs=[rows, rows, packed, packed, pl.BlockSpec((32, D), lambda r: (0, 0))],
        scratch_shapes=[
            pltpu.VMEM((D, D), bf16),
            pltpu.VMEM((T, D), bf16),
            pltpu.VMEM((D, D), bf16),
        ],
        compiler_params=params(),
        cost_estimate=cost(11),
        name="middle",
        main=True,
    )


def attn_bwd_kernel(
    blk, offs, q, k, v, do, mix, lse, n1t, segc, segr,
    dqkv_o, keep, send, sums, kn, vn, qt, dt, kt, qm, dm, dqt, gw,
):
    left, right = segment_tail(segc, segr, None)
    sub = lax.broadcasted_iota(jnp.int32, (16, T), 0)
    qs = q[...] * jnp.asarray(0.125, bf16)
    qtt = qs.T
    dtt = do[...].T
    kt[...] = k[...].T
    prod = (do[...].astype(f32) * mix[...].astype(f32)).T
    zero = jnp.zeros((64, T), bf16)
    pad = jnp.zeros((112, T), bf16)
    lane = lax.broadcasted_iota(jnp.int32, (T, 128), 1)
    nothing = jnp.zeros((T, 128), bf16)
    for p in range(2):
        at = slice(128 * p, 128 * p + 128)
        kn[p, :, :128] = k[:, at]
        kn[p, :, 128:] = left
        vn[p, :, :128] = v[:, at]
        vn[p, :, 128:] = left
        for e in range(2):
            h = 2 * p + e
            mine = (lane >= 64 * e) & (lane < 64 * e + 64)
            qm[p, e] = jnp.where(mine, qs[:, at], nothing)
            dm[p, e] = jnp.where(mine, do[:, at], nothing)
            for dst, src in ((qt, qtt), (dt, dtt)):
                dst[h, 64 * e : 64 * e + 64, :] = src[64 * h : 64 * h + 64]
                dst[h, 64 - 64 * e : 128 - 64 * e, :] = zero
                dst[h, 144:, :] = pad
            a, b, c = three(-lse[h : h + 1, :])
            tail = jnp.where(sub == 4, a, jnp.where(sub == 5, b, jnp.where(sub == 6, c, right)))
            qt[h, 128:144, :] = tail.astype(bf16)
            a, b, c = three(-rowsum(prod[64 * h : 64 * h + 64, :]))
            tail = jnp.where(sub == 4, a, jnp.where(sub == 5, b, jnp.where(sub == 6, c, 0.0)))
            dt[h, 128:144, :] = tail.astype(bf16)
    dqt[...] = jnp.zeros_like(dqt)
    for j in range(NB):
        lo = blk[0, j]
        hi = blk[1, j]
        keys = slice(j * B, (j + 1) * B)

        def step(i, carry):
            dks, dvs = carry
            cols = pl.ds(pl.multiple_of(i * B, B), B)
            new_dk, new_dv = [], []
            for p in range(2):
                dk, dv = dks[p], dvs[p]
                for e in range(2):
                    h = 2 * p + e
                    pr = jnp.exp(dot(kn[p, keys, :], qt[h, :, cols], 1, 0))
                    ds = (pr * dot(vn[p, keys, :], dt[h, :, cols], 1, 0)).astype(bf16)
                    dv += dot(pr.astype(bf16), dm[p, e, cols, :], 1, 0)
                    dk += dot(ds, qm[p, e, cols, :], 1, 0)
                    dqt[64 * h : 64 * h + 64, cols] += dot(kt[64 * h : 64 * h + 64, keys], ds, 1, 0)
                new_dk.append(dk)
                new_dv.append(dv)
            return tuple(new_dk), tuple(new_dv)

        zeros = tuple(jnp.zeros((B, 128), f32) for _ in range(2))
        dks, dvs = lax.fori_loop(lo, hi, step, (zeros, zeros))
        for p in range(2):
            dqkv_o[keys, 256 + 128 * p : 384 + 128 * p] = dks[p].astype(bf16)
            dqkv_o[keys, 512 + 128 * p : 640 + 128 * p] = dvs[p].astype(bf16)
    dqkv_o[:, :256] = (dqt[...] * 0.125).astype(bf16).T
    sums[:, :256] = fold(dqkv_o[:, :256].astype(f32))
    sums[:, 256:] = fold(dqkv_o[:, 512:].astype(f32))
    gw[...] = dot(n1t[...], dqkv_o[...], 1, 0).astype(bf16)
    scattered_rows(gw, (keep, send), offs, 0, 6, RB, 0)


def attn_bwd(g, blk, offs, q, k, v, dmix, mix, lse, n1t, segc, segr):
    whole = lambda a: pl.BlockSpec(a.shape, lambda r: (0,) * a.ndim)
    outs = [
        sds((T, D), bf16),
        sds((8, QR, 128), bf16),
        sds((8, QR, 128), bf16),
        sds((8, 512), f32),
    ]
    return call(
        attn_bwd_kernel,
        [blk, offs, q, k, v, dmix, mix, lse, n1t, segc, segr],
        grid=(1,),
        out_shape=outs,
        in_specs=[SM, SM, whole(q), whole(k), whole(v), pl.BlockSpec((T, 256), lambda r: (0, g))]
        + [whole(a) for a in (mix, lse, n1t, segc, segr)],
        out_specs=[whole(a) for a in outs],
        scratch_shapes=[
            pltpu.VMEM((2, T, 256), bf16),
            pltpu.VMEM((2, T, 256), bf16),
            pltpu.VMEM((4, 256, T), bf16),
            pltpu.VMEM((4, 256, T), bf16),
            pltpu.VMEM((256, T), bf16),
            pltpu.VMEM((2, 2, T, 128), bf16),
            pltpu.VMEM((2, 2, T, 128), bf16),
            pltpu.VMEM((256, T), f32),
            pltpu.VMEM((D, D), bf16),
        ],
        compiler_params=params(),
        cost_estimate=cost(21),
        name="attn_bwd",
        main=True,
    )


def last_kernel(offs, d0, d1, d2, w0, w1, w2, x, dx1, small, mids, s0, s1, s2, u0, u1, u2,
                gt_o, keep, send, sums, sg):
    step = pl.program_id(0)

    @pl.when(step == 0)
    def _():
        sums[...] = jnp.zeros_like(sums)

    dn = dot(d0[...], w0[...], 1, 1) + dot(d1[...], w1[...], 1, 1) + dot(d2[...], w2[...], 1, 1)
    back, hats = norm_back(x[...].astype(f32), dn, small[0:1, :])
    gt_o[...] = (dx1[...] + back).astype(bf16)
    sums[0:8, :] += fold(hats)
    sums[8:16, :] += fold(dn)

    @pl.when(step == NB - 1)
    def _():
        total = lambda v: jnp.sum(v, axis=0, keepdims=True)
        sg[...] = jnp.zeros_like(sg)
        sg[0:1, :] = total(sums[0:8, :])
        sg[1:2, :] = total(sums[8:16, :])
        for g, s in enumerate((s0, s1, s2)):
            sg[2:3, 256 * g : 256 * g + 256] = total(s[:, :256])
            sg[3:4, 256 * g : 256 * g + 256] = total(s[:, 256:])
        for n in range(4):
            sg[4 + n : 5 + n, :] = total(mids[8 * n : 8 * n + 8, :])
        ups = [total(u[...]) for u in (u0, u1, u2)]
        for n in range(4):
            parts = []
            for d in range(4 * n, 4 * n + 4):
                for j in range(3):
                    parts.append(ups[j][:, FB * d : FB * d + FB])
            sg[8 + n : 9 + n, :] = jnp.concatenate(parts, axis=1)
        low = sg[...].astype(bf16)
        row = lax.broadcasted_iota(jnp.int32, (D, 128), 0)
        col = lax.broadcasted_iota(jnp.int32, (D, 128), 1)
        for s in range(OWN):
            hot = jnp.where((row == col + offs[s] * RB) & (col < RB), 1.0, 0.0).astype(bf16)
            (keep, send)[s // 8][s % 8, :, :] = dot(low, hot, 1, 0).astype(bf16)


def last_norm(offs, dqkvs, ws, x, dx1, small, mids, ssums, usums):
    rows = pl.BlockSpec((B, D), lambda r: (r, 0))
    whole = lambda a: pl.BlockSpec(a.shape, lambda r: (0,) * a.ndim)
    packed = pl.BlockSpec((8, SR, 128), lambda r: (0, 0, 0))
    return call(
        last_kernel,
        [offs, *dqkvs, *ws, x, dx1, small, mids, *ssums, *usums],
        grid=(NB,),
        out_shape=[sds((T, D), bf16), sds((8, SR, 128), bf16), sds((8, SR, 128), bf16)],
        in_specs=[SM] + [rows] * 3 + [whole(w) for w in ws] + [rows, rows]
        + [whole(a) for a in (small, mids, *ssums, *usums)],
        out_specs=[rows, packed, packed],
        scratch_shapes=[pltpu.VMEM((16, D), f32), pltpu.VMEM((SR, D), f32)],
        compiler_params=params(),
        cost_estimate=cost(10.5),
        name="last_norm",
        main=True,
    )


def out_kernel(h0, h1, h2, w0, w1, w2, x1, small, o):
    a = x1[...] + small[7:8, :]
    a += dot(h0[...], w0[...], 1, 0) + dot(h1[...], w1[...], 1, 0) + dot(h2[...], w2[...], 1, 0)
    o[...] = a.astype(bf16)


def layer_out(hids, wds, x1, small):
    rows = pl.BlockSpec((B, D), lambda r: (r, 0))
    return call(
        out_kernel,
        [*hids, *wds, x1, small],
        grid=(NB,),
        out_shape=sds((T, D), bf16),
        in_specs=[pl.BlockSpec((B, FC), lambda r: (r, 0))] * 3
        + [pl.BlockSpec((FC, D), lambda r: (0, 0))] * 3
        + [rows, pl.BlockSpec((SR, D), lambda r: (0, 0))],
        out_specs=rows,
        compiler_params=params(),
        cost_estimate=cost(10),
        name="layer_out",
        main=True,
    )


def adamw(weight, grad, mom_one, mom_two, rate):
    next_one = BETA1 * mom_one + (1.0 - BETA1) * grad
    next_two = BETA2 * mom_two + (1.0 - BETA2) * grad * grad
    fixed_one = next_one / (1.0 - BETA1**STEP)
    fixed_two = next_two / (1.0 - BETA2**STEP)
    updated = weight - rate * (fixed_one / (jnp.sqrt(fixed_two) + ADAM_EPS) + DECAY * weight)
    return (updated, next_one, next_two)


def whole_rows(offs, pair, at, dst):
    half = dst.shape[0] // 2
    for n, y in enumerate((offs[OWN], 1 - offs[OWN])):
        dst[pl.ds(pl.multiple_of(y * half, 16), half), :] = pair[n][at : at + half, :]


def update(outs, at, state, grad, rate):
    for o, val in zip(outs, adamw(state[0][at], grad, state[1][at], state[2][at], rate)):
        o[at] = val


def adam_heads_kernel(offs, *refs):
    pair, last, qkv, out, small = refs[:2], refs[2:4], refs[4:7], refs[7:10], refs[10:13]
    qkv_o, out_o, small_o = refs[13:16], refs[16:19], refs[19:22]
    packs = refs[22:]
    for n in range(3):
        whole_rows(offs, pair, (FR + n * QR) // 2, packs[n])
    for g in range(3):
        for part in range(3):
            for t in range(2):
                c = D * part + 256 * g + 128 * t
                r = (2 * part + t) * RB
                if g < 2:
                    grad = packs[g][r : r + RB, :].astype(f32)
                else:
                    grad = last[0][r : r + RB, :].astype(f32) + last[1][r : r + RB, :].astype(f32)
                update(qkv_o, (slice(None), slice(c, c + 128)), qkv, grad, RATES[0])
    for t in range(6):
        grad = packs[2][t * RB : (t + 1) * RB, :].astype(f32)
        update(out_o, (slice(None), slice(128 * t, 128 * t + 128)), out, grad, RATES[1])
    grad = last[0][QR : QR + SR, :].astype(f32) + last[1][QR : QR + SR, :].astype(f32)
    update(small_o, Ellipsis, small, grad[:12, :RB], RATES[4])


def adam_ff_kernel(offs, *refs):
    two, pair, up, down = refs[:2], refs[2:4], refs[4:7], refs[7:10]
    up_o, down_o = refs[10:13], refs[13:16]
    pack = refs[16]
    whole_rows(offs, pair, 0, pack)

    def total(j, r, n):
        if j == 2:
            return pack[r : r + n, :].astype(f32)
        rows = slice(FR * j + r, FR * j + r + n)
        return two[0][rows, :].astype(f32) + two[1][rows, :].astype(f32)

    for t in range(8):
        parts = [total(j, t * RB, RB) for j in range(3)]
        grad = jnp.concatenate([p[:, :64] for p in parts] + [p[:, 64:] for p in parts], axis=1)
        update(up_o, (slice(None), slice(384 * t, 384 * t + 384)), up, grad, RATES[2])
    for j in range(3):
        for t in range(6):
            at = (slice(FB * j, FB * j + FB), slice(128 * t, 128 * t + 128))
            update(down_o, at, down, total(j, 8 * RB + t * FB, FB), RATES[3])


def adam_call(kernel, offs, grads, states, scratch, name):
    shapes = [sds(s.shape, f32) for s in states]
    return call(
        kernel,
        [offs, *grads, *states],
        out_shape=shapes,
        in_specs=[SM] + [VM] * (len(grads) + len(states)),
        out_specs=[VM] * len(shapes),
        scratch_shapes=[pltpu.VMEM((r, 128), bf16) for r in scratch],
        compiler_params=params(),
        cost_estimate=cost(),
        name=name,
    )


def shifted(f):
    pairs = []
    for z in range(4):
        for x in range(2):
            for c in range(2):
                tz, tx, tc = f(z, x, c)
                pairs.append(((z * 2 + x) * 2 + c, (tz * 2 + tx) * 2 + tc))
    return pairs


TO_CORE = shifted(lambda z, x, c: (z, x, 1 - c))
TO_X = shifted(lambda z, x, c: (z, 1 - x, c))
TO_Z = [shifted(lambda z, x, c, s=s: ((z + s) % 4, x, c)) for s in range(4)]
FROM_Z = [shifted(lambda z, x, c, s=s: ((z - s) % 4, x, c)) for s in range(4)]
TO_Y = [(0, 1), (1, 0)]


def stack_kernel(a, b, c, d, *refs):
    out = refs[len(refs) // 2]
    for n, ref in enumerate((a, b, c, d)):
        out[n] = ref[...]


class Gather:
    def __init__(self, own):
        self.own = own

    def along_z(self):
        self.parts = [self.own] + [lax.ppermute(self.own, "dp", TO_Z[s]) for s in (1, 2, 3)]

    def along_x(self, *later):
        anywhere = pl.BlockSpec(memory_space=pl.ANY)
        outs = call(
            stack_kernel,
            [*self.parts, *[g.own for g in later]],
            out_shape=[sds((4,) + self.own.shape, bf16)] + [sds(g.own.shape, bf16) for g in later],
            in_specs=[VM] * 4 + [anywhere] * len(later),
            out_specs=[VM] + [anywhere] * len(later),
            input_output_aliases={4 + n: 1 + n for n in range(len(later))},
            compiler_params=params(),
            cost_estimate=cost(1.7),
            name="stack",
        )
        for g, own in zip(later, outs[1:]):
            g.own = own
        line = outs[0]
        self.pieces = [line, lax.ppermute(line, "dp", TO_X), lax.ppermute(line, "dp", TO_CORE)]

    def to_core(self, hold=False):
        if hold:
            self.pieces[1] = wait_here(self.pieces[1])[0]
        self.pieces.append(lax.ppermute(self.pieces[1], "dp", TO_CORE))


def add_core_kernel(*refs):
    half = len(refs) // 2 - 1
    a, b = refs[-2:]
    at = 0
    for keep, got in zip(refs[:half], refs[half : 2 * half]):
        rows = keep.shape[1]
        a[:, at : at + rows] = (keep[:4].astype(f32) + got[:4].astype(f32)).astype(bf16)
        b[:, at : at + rows] = (keep[4:].astype(f32) + got[4:].astype(f32)).astype(bf16)
        at += rows


def add_core_half_kernel(offs, *refs):
    n = len(refs) // 2 - 1
    outs = refs[-2:]
    at = 0
    for keep, got in zip(refs[:n], refs[n : 2 * n]):
        half = keep.shape[1] // 2
        for out, y in zip(outs, (offs[OWN], 1 - offs[OWN])):
            rows = pl.ds(pl.multiple_of(y * half, 16), half)
            out[:, at : at + half] = (keep[:, rows].astype(f32) + got[:, rows].astype(f32)).astype(bf16)
        at += half


def add_y_kernel(*refs):
    n = len(refs) // 2 - 1
    a, b = refs[-2:]
    at = 0
    for keep, got in zip(refs[:n], refs[n : 2 * n]):
        rows = keep.shape[2]
        total = (keep[...].astype(f32) + got[...].astype(f32)).astype(bf16)
        a[:, at : at + rows] = total[0]
        b[:, at : at + rows] = total[1]
        at += rows


def add_x_kernel(keep, got, *outs):
    for s in range(4):
        outs[s][...] = (keep[s].astype(f32) + got[s].astype(f32)).astype(bf16)


def add_z_kernel(a, b, c, d, o):
    o[...] = (a[...].astype(f32) + b[...].astype(f32) + c[...].astype(f32) + d[...].astype(f32)).astype(bf16)


def add_call(kernel, args, outs, name, then, beside):
    if beside:
        SIDE.append((kernel, args, outs, then))
        return
    then(add_alone(kernel, args, outs, name))


def add_alone(kernel, args, outs, name):
    return call(
        kernel,
        args,
        out_shape=outs,
        in_specs=[VM] * len(args),
        out_specs=[VM] * len(outs),
        compiler_params=params(),
        cost_estimate=cost(),
        name=name,
    )


class Scatter:
    def __init__(self, *packs):
        self.keeps = [p[0] for p in packs]
        self.rows = sum(k.shape[1] for k in self.keeps)
        self.gots = [lax.ppermute(p[1], "dp", TO_CORE) for p in packs]

    def half_along_y(self, offs):
        self.rows //= 2
        args = (*self.keeps, *self.gots)
        block = lambda r: pl.BlockSpec((2, r, 128), lambda i: (i, 0, 0))
        mine, other = call(
            add_core_half_kernel,
            [offs, *args],
            grid=(4,),
            out_shape=[sds((8, self.rows, 128), bf16)] * 2,
            in_specs=[SM] + [block(a.shape[1]) for a in args],
            out_specs=[block(self.rows)] * 2,
            compiler_params=params(),
            cost_estimate=cost(),
            name="add_core_half",
        )
        self.halves = (mine, lax.ppermute(other, "rep", TO_Y))

    def join_along_x(self, other):
        self.rows += other.rows
        cut = lambda a: a.reshape(2, 4, a.shape[1], 128)
        args = [cut(s.halves[n]) for n in range(2) for s in (self, other)]
        self.mine, send = call(
            add_y_kernel,
            args,
            grid=(4,),
            out_shape=[sds((4, self.rows, 128), bf16)] * 2,
            in_specs=[pl.BlockSpec((2, 1, a.shape[2], 128), lambda i: (0, i, 0, 0)) for a in args],
            out_specs=[pl.BlockSpec((1, self.rows, 128), lambda i: (i, 0, 0))] * 2,
            compiler_params=params(),
            cost_estimate=cost(),
            name="add_y",
        )
        self.got = lax.ppermute(send, "dp", TO_X)

    def along_x(self, beside=False):
        outs = [sds((4, self.rows, 128), bf16)] * 2

        def then(out):
            self.mine = out[0]
            self.got = lax.ppermute(out[1], "dp", TO_X)

        add_call(add_core_kernel, (*self.keeps, *self.gots), outs, "add_core", then, beside)

    def along_z(self, beside=False):
        outs = [sds((self.rows, 128), bf16)] * 4

        def then(parts):
            self.parts = [parts[0]] + [lax.ppermute(parts[s], "dp", FROM_Z[s]) for s in (1, 2, 3)]

        add_call(add_x_kernel, (self.mine, self.got), outs, "add_x", then, beside)

    def along_y(self, beside=False):
        def then(out):
            self.done = (out[0], lax.ppermute(out[0], "rep", TO_Y))

        add_call(add_z_kernel, self.parts, [sds((self.rows, 128), bf16)], "add_z", then, beside)


def gather_any(small, wq, wo, wu, wd):
    full = lambda w, axis: lax.all_gather(w.astype(bf16), "dp", axis=axis, tiled=True)
    small = full(small, 1)
    blocks = small.reshape(small.shape[0], OWN, RB).transpose(1, 0, 2)
    blocks = jnp.pad(blocks, ((0, 0), (0, SR - small.shape[0]), (0, 128 - RB)))
    q = full(wq, 0).reshape(OWN, RB, 3, 3, 2, 128).transpose(3, 0, 2, 4, 1, 5).reshape(3, OWN, QR, 128)
    o = full(wo, 0).reshape(OWN, RB, 6, 128).transpose(0, 2, 1, 3).reshape(OWN, QR, 128)
    u = full(wu, 0).reshape(OWN, RB, 8, 2, 3, FB).transpose(4, 0, 2, 1, 3, 5).reshape(3, OWN, 8 * RB, 128)
    d = full(wd, 0).reshape(OWN, 3, FB, 6, 128).transpose(1, 0, 3, 2, 4).reshape(3, OWN, 6 * FB, 128)
    f = jnp.concatenate([u, d], 2)
    cut = lambda a: tuple(a[4 * n : 4 * n + 4] for n in range(4))
    heads = [cut(jnp.concatenate(p, 1)) for p in ((q[0], blocks), (q[1], q[2]))]
    return heads, jnp.concatenate([f[0], f[1], f[2], o], 1)


def scatter_any(packs, grads):
    q0, q1, q2, o, s = [jnp.concatenate(p, 0) for p in packs]
    q = jnp.stack([q0, q1, q2]).reshape(3, OWN, 3, 2, RB, 128).transpose(1, 4, 2, 0, 3, 5)
    f = grads.reshape(OWN, 3, FR, 128)
    u = f[:, :, : 8 * RB].reshape(OWN, 3, 8, RB, 2, FB).transpose(0, 3, 2, 4, 1, 5)
    d = f[:, :, 8 * RB :].reshape(OWN, 3, 6, FB, 128).transpose(0, 1, 3, 2, 4)
    o = o.reshape(OWN, 6, RB, 128).transpose(0, 2, 1, 3)
    s = s[:, :12, :RB].transpose(1, 0, 2).reshape(12, D)
    flat = ((q.reshape(D, 3 * D), 0), (o.reshape(D, D), 0), (u.reshape(D, FF), 0), (d.reshape(FF, D), 0), (s, 1))
    out = []
    for g, axis in flat:
        g = lax.psum_scatter(g, "dp", scatter_dimension=axis, tiled=True)
        out.append(lax.psum(g, "rep").astype(f32))
    return out


def shards(tokens, segment_ids, cotangent, *state, wide):
    masters, firsts, seconds = state[:5], state[5:10], state[10:15]
    w_qkv, w_out, w_up, w_down, small_params = masters
    x = tokens[0]
    dy = cotangent[0]
    seg = segment_ids[0]
    segc = seg.reshape(T, 1)
    segr = seg.reshape(1, T)
    begins, ends = seg[::B], seg[B - 1 :: B]
    low = jnp.sum(ends[None, :] < begins[:, None], 1)
    high = jnp.sum(begins[None, :] <= ends[:, None], 1)
    blk = jnp.stack([low, high]).astype(jnp.int32)

    ORDER.clear()
    if wide:
        me = lax.axis_index("dp")
        s = jnp.arange(OWN, dtype=jnp.int32)
        z = (me // 4 - s % 4) % 4
        xx = (me // 2 % 2) ^ (s // 4 % 2)
        cc = (me % 2) ^ (s // 8)
        offs = jnp.append((z * 2 + xx) * 2 + cc, lax.axis_index("rep")).astype(jnp.int32)
        lines = [Gather(own) for own in pack(small_params, w_qkv, w_out, w_up, w_down)]
        lines[0].along_z()
        rest = lax.all_gather(lines[2].own, "dp", axis=0, tiled=True).reshape(OWN, 3 * FR + QR, 128)
        lines[0].along_x(lines[1])
        lines[0].to_core()
        lines[1].along_z()
        heads = [lines[0].pieces, None]
    else:
        offs = jnp.arange(OWN, dtype=jnp.int32)
        heads, rest = gather_any(small_params, w_qkv, w_out, w_up, w_down)

    n1, n1t, small = norm_first(offs, x, heads[0], QR)
    fwd = []
    if wide:
        lines[1].along_x()
        heads[1] = lines[1].pieces
    for g in range(3):
        fwd.append(attn_fwd(g, blk, offs, n1, heads[min(g, 1)], small, segc, segr))
        if wide and g == 0:
            lines[1].to_core(hold=True)
    x1, n2, n2t = post_attn(x, [f[3] for f in fwd], rest, small)
    sent = []

    def send(*packs):
        if wide:
            sent.append(Scatter(*packs))

    def move(n, name, beside=False):
        if wide:
            getattr(sent[n], "along_" + name)(beside)

    acc = grads = None
    ffs = []
    for j in range(3):
        hid, acc, wd, dub, *grad = feed_forward(j, offs, n2, n2t, dy, rest, small, acc, grads)
        ffs.append((hid, wd, dub))
        if j < 2:
            grads = grad[0]
        if j == 1 and wide:
            own_ff = lax.psum_scatter(grads.reshape(-1, 128), "dp", scatter_dimension=0, tiled=True)
    send(grad)
    dx1, dmix, keep_o, send_o, mids = middle(offs, acc, x1, dy, [f[4] for f in fwd], rest, small)
    if wide:
        sent[0].half_along_y(offs)
    bwd = []
    for g in range(3):
        q, k, v, mix, _, lse, _ = fwd[g]
        bwd.append(attn_bwd(g, blk, offs, q, k, v, dmix, mix, lse, n1t, segc, segr))
        if g == 0 and wide:
            ORDER.append(sent[0].halves[1])
        if g == 1 and wide:
            send(bwd[0][1:3], bwd[1][1:3], (keep_o, send_o))
            sent[1].half_along_y(offs)
    if wide:
        sent[0].join_along_x(sent[1])
    grad_tokens, keep_s, send_s = last_norm(
        offs, [b[0] for b in bwd], [f[6] for f in fwd], x, dx1, small, mids,
        [b[3] for b in bwd], [f[2] for f in ffs],
    )
    send(bwd[2][1:3], (keep_s, send_s))
    move(2, "x")
    move(0, "z")
    result = layer_out([f[0] for f in ffs], [f[1] for f in ffs], x1, small)
    move(2, "z")
    move(0, "y")
    states = [(masters[n], firsts[n], seconds[n]) for n in range(5)]
    new = [None] * 5
    if wide:
        (own_ff,) = wait_here(own_ff)
        pair = (own_ff, lax.ppermute(own_ff, "rep", TO_Y))
        move(2, "y")
        both = adam_call(adam_ff_kernel, offs, (*pair, *sent[0].done), states[2] + states[3], (FR,), "adam_ff")
        new[2], new[3] = both[:3], both[3:]
        both = adam_call(
            adam_heads_kernel, offs, (*sent[0].done, *sent[2].done),
            states[0] + states[1] + states[4], (QR, QR, QR), "adam_heads",
        )
        new[0], new[1], new[4] = both[:3], both[3:6], both[6:]
    else:
        packs = [(b[1], b[2]) for b in bwd] + [(keep_o, send_o), (keep_s, send_s)]
        owned = scatter_any(packs, jnp.concatenate([grads, jnp.concatenate(grad, 0)], 1))
        new = [adamw(states[n][0], owned[n], states[n][1], states[n][2], RATES[n]) for n in range(5)]
    return (
        result[None],
        grad_tokens[None],
        *[n[0] for n in new],
        *[n[1] for n in new],
        *[n[2] for n in new],
    )


def solution(mesh):
    rows = P("dp", None)
    small = P(None, "dp")
    state = (rows, rows, rows, rows, small)
    seqs = P(("dp", "rep"), None, None)
    return jax.shard_map(
        functools.partial(shards, wide=mesh.shape["dp"] == 16 and mesh.shape["rep"] == 2),
        mesh=mesh,
        in_specs=(seqs, P(("dp", "rep"), None), seqs) + state * 3,
        out_specs=(seqs, seqs) + state * 3,
        check_vma=False,
    )
```

```python
import functools
import math

import jax
import jax.numpy as jnp
from jax import lax
from jax.experimental import pallas as pl
from jax.experimental.pallas import tpu as pltpu
from jax.sharding import PartitionSpec as P

HEADS = 12
STEP = 10
BETA1 = 0.5
BETA2 = 0.5
ADAM_EPS = 1e-08
DECAY = 0.05
RATES = (0.04, 0.15, 0.04, 0.02, 0.3)

bf16 = jnp.bfloat16
f32 = jnp.float32

T = 1024
D = 768
FF = 3072
OWN = 16
RB = D // OWN
FB = FF // OWN // 3
FC = FF // 3
QR = 6 * RB
FR = 8 * RB + 6 * FB
SR = 16
B = 256
NB = T // B
FBLK = 1024
FN = T // FBLK
FCOL = 256
MASK = 2.0**30
VMEM_LIMIT = 56 << 20

VM = pl.BlockSpec(memory_space=pltpu.VMEM)
SM = pl.BlockSpec(memory_space=pltpu.SMEM)


def params(**kw):
    return pltpu.CompilerParams(vmem_limit_bytes=VMEM_LIMIT, **kw)


ORDER = []
SIDE = []


def call(kernel, args, *, in_specs, out_specs, out_shape, main=False, token=None, **kw):
    side = list(SIDE) if main else []
    if main:
        SIDE.clear()
    extra = list(ORDER)
    single = not isinstance(out_shape, (list, tuple))
    shapes = [out_shape] if single else list(out_shape)
    specs = [out_specs] if single else list(out_specs)
    n, m = len(args), len(shapes)
    side_args = [a for _, more, _, _ in side for a in more]
    side_outs = [o for _, _, outs, _ in side for o in outs]
    grid = "grid" in kw
    whole = lambda a: pl.BlockSpec(a.shape, lambda r, k=len(a.shape): (0,) * k) if grid else VM

    def body(*refs):
        ins = refs[n : n + len(side_args)]
        rest = refs[n + len(side_args) + len(extra) :]
        outs = rest[m : m + len(side_outs)]

        def beside():
            i = o = 0
            for fn, more, results, _ in side:
                fn(*ins[i : i + len(more)], *outs[o : o + len(results)])
                i += len(more)
                o += len(results)

        if side:
            if grid:
                pl.when(pl.program_id(0) == 0)(beside)
            else:
                beside()
        return kernel(*refs[:n], *rest[:m], *rest[m + len(side_outs) :])

    out = pl.pallas_call(
        body,
        in_specs=list(in_specs)
        + [whole(a) for a in side_args]
        + [pl.BlockSpec(memory_space=pl.ANY)] * len(extra),
        out_specs=specs + [whole(a) for a in side_outs],
        out_shape=shapes + side_outs,
        **kw,
    )(*args, *side_args, *extra)
    out = list(out)
    ORDER[:] = [min(out[:m], key=lambda a: a.size) if token is None else out[token]]
    at = m
    for _, _, results, then in side:
        then(out[at : at + len(results)])
        at += len(results)
    return out[0] if single else out[:m]


def wait_here(*arrays):
    anywhere = pl.BlockSpec(memory_space=pl.ANY)
    order = list(ORDER)
    out = call(
        lambda *refs: None,
        arrays,
        out_shape=[sds(a.shape, a.dtype) for a in arrays],
        in_specs=[anywhere] * len(arrays),
        out_specs=[anywhere] * len(arrays),
        input_output_aliases={n: n for n in range(len(arrays))},
        name="wait_here",
    )
    ORDER[:] = order
    return out


def sds(shape, dtype):
    return jax.ShapeDtypeStruct(shape, dtype)


PACE = 0.7


def cost(us=3.0):
    return pl.CostEstimate(flops=int(us * PACE * 1e9), bytes_accessed=1, transcendentals=0)


def dot(a, b, ca, cb):
    return lax.dot_general(a, b, (((ca,), (cb,)), ((), ())), preferred_element_type=f32)


def fold(v):
    return jnp.sum(v.reshape(v.shape[0] // 8, 8, v.shape[1]), axis=0)


def rowsum(v):
    return jnp.sum(fold(v), axis=0, keepdims=True)


def gathered_rows(dst, refs, offs, base, tiles, rows, col):
    per = OWN // len(refs)
    for s in range(OWN):
        ref, at = refs[s // per], s % per
        off = s * rows if offs is None else pl.multiple_of(offs[s] * rows, 16)
        for t in range(tiles):
            dst[pl.ds(off, rows), col + 128 * t : col + 128 * t + 128] = ref[
                at, base + t * rows : base + (t + 1) * rows, :
            ]


def scattered_rows(src, outs, offs, base, tiles, rows, col):
    per = OWN // len(outs)
    for s in range(OWN):
        ref, at = outs[s // per], s % per
        off = s * rows if offs is None else pl.multiple_of(offs[s] * rows, 16)
        for t in range(tiles):
            ref[at, base + t * rows : base + (t + 1) * rows, :] = src[
                pl.ds(off, rows), col + 128 * t : col + 128 * t + 128
            ]


def pack_heads(dst, at, wq, g):
    for part in range(3):
        for t in range(2):
            c = D * part + 256 * g + 128 * t
            r = at + (2 * part + t) * RB
            dst[r : r + RB, :] = wq[:, c : c + 128].astype(bf16)


def pack_kernel(small, wq, wo, wu, wd, q0, q12, rest, token):
    token[...] = jnp.zeros_like(token)
    pack_heads(q0, 0, wq, 0)
    q0[QR : QR + SR, :] = jnp.zeros((SR, 128), bf16)
    q0[QR : QR + 12, :RB] = small[...].astype(bf16)
    pack_heads(q12, 0, wq, 1)
    pack_heads(q12, QR, wq, 2)
    for j in range(3):
        for t in range(8):
            r = FR * j + t * RB
            a = wu[:, 384 * t + 64 * j : 384 * t + 64 * j + 64]
            b = wu[:, 384 * t + 192 + 64 * j : 384 * t + 192 + 64 * j + 64]
            rest[r : r + RB, :] = jnp.concatenate([a, b], axis=1).astype(bf16)
        for t in range(6):
            r = FR * j + 8 * RB + t * FB
            rest[r : r + FB, :] = wd[FB * j : FB * j + FB, 128 * t : 128 * t + 128].astype(bf16)
    for t in range(6):
        r = 3 * FR + t * RB
        rest[r : r + RB, :] = wo[:, 128 * t : 128 * t + 128].astype(bf16)


def pack(*args):
    rows = (QR + SR, 2 * QR, 3 * FR + QR, 16)
    return call(
        pack_kernel,
        args,
        out_shape=[sds((r, 128), bf16) for r in rows],
        in_specs=[VM] * len(args),
        out_specs=[VM] * len(rows),
        compiler_params=params(),
        cost_estimate=cost(2.4),
        name="pack",
    )[:3]


def norm_kernel(offs, x, p0, p1, p2, p3, n1, n1t, small, *, base):
    @pl.when(pl.program_id(0) == 0)
    def _():
        acc = jnp.zeros((SR, D), f32)
        row = lax.broadcasted_iota(jnp.int32, (128, D), 0)
        col = lax.broadcasted_iota(jnp.int32, (128, D), 1)
        for s in range(OWN):
            ref = (p0, p1, p2, p3)[s // 4]
            hot = jnp.where((col == row + offs[s] * RB) & (row < RB), 1.0, 0.0).astype(bf16)
            acc += dot(ref[s % 4, base : base + SR, :], hot, 1, 0)
        small[...] = acc

    v = x[...].astype(f32)
    c = v - jnp.mean(v, -1, keepdims=True)
    r = lax.rsqrt(jnp.mean(c * c, -1, keepdims=True) + 1e-06)
    n = (c * r * small[0:1, :] + small[1:2, :]).astype(bf16)
    n1[...] = n
    n1t[...] = n.T


def norm_first(offs, x, pieces, base):
    whole = [pl.BlockSpec(p.shape, lambda r: (0, 0, 0)) for p in pieces]
    return call(
        functools.partial(norm_kernel, base=base),
        [offs, x, *pieces],
        grid=(NB,),
        out_shape=[sds((T, D), bf16), sds((D, T), bf16), sds((SR, D), f32)],
        in_specs=[SM, pl.BlockSpec((B, D), lambda r: (r, 0))] + whole,
        out_specs=[
            pl.BlockSpec((B, D), lambda r: (r, 0)),
            pl.BlockSpec((D, B), lambda r: (0, r)),
            pl.BlockSpec((SR, D), lambda r: (0, 0)),
        ],
        compiler_params=params(),
        cost_estimate=cost(5),
        name="norm_first",
    )


def segment_tail(segc, segr, minus):
    lane = lax.broadcasted_iota(jnp.int32, (T, 128), 1)
    left = jnp.where((segc[...] == lane) | ((lane >= 4) & (lane < 7)), 1.0, 0.0).astype(bf16)
    sub = lax.broadcasted_iota(jnp.int32, (16, T), 0)
    right = jnp.where((segr[...] != sub) & (sub < 4), -MASK, 0.0)
    return left, right


def three(v):
    hi = v.astype(bf16).astype(f32)
    rest = v - hi
    mid = rest.astype(bf16).astype(f32)
    return hi, mid, rest - mid


def attn_fwd_kernel(
    blk, offs, n1, p0, p1, p2, p3, small, segc, segr,
    q_o, k_o, v_o, mix_o, mixt_o, lse_o, w_o, kn, qt, vt, s_s, *, g,
):
    gathered_rows(w_o, (p0, p1, p2, p3), offs, QR if g == 2 else 0, 6, RB, 0)
    qb = small[2:3, 256 * g : 256 * g + 256]
    vb = small[3:4, 256 * g : 256 * g + 256]
    q = (dot(n1[...], w_o[:, :256], 1, 0) + qb).astype(bf16)
    k = dot(n1[...], w_o[:, 256:512], 1, 0).astype(bf16)
    v = (dot(n1[...], w_o[:, 512:], 1, 0) + vb).astype(bf16)
    q_o[...] = q
    k_o[...] = k
    v_o[...] = v
    left, right = segment_tail(segc, segr, None)
    right = right.astype(bf16)
    qtt = (q * jnp.asarray(0.125, bf16)).T
    zero = jnp.zeros((64, T), bf16)
    pad = jnp.zeros((112, T), bf16)
    for p in range(2):
        kn[p, :, :128] = k[:, 128 * p : 128 * p + 128]
        kn[p, :, 128:] = left
        for e in range(2):
            h = 2 * p + e
            qt[h, 64 * e : 64 * e + 64, :] = qtt[64 * h : 64 * h + 64]
            qt[h, 64 - 64 * e : 128 - 64 * e, :] = zero
            qt[h, 128:144, :] = right
            qt[h, 144:, :] = pad
    vt[...] = v.T
    for i in range(NB):
        lo = blk[0, i]
        hi = blk[1, i]
        cols = slice(i * B, (i + 1) * B)

        def scores(j, tops):
            r = pl.ds(pl.multiple_of(j * B, B), B)
            out = []
            for h in range(4):
                s = dot(kn[h // 2, r, :], qt[h, :, cols], 1, 0)
                s_s[h, r, :] = s
                out.append(jnp.maximum(tops[h], jnp.max(s.reshape(B // 8, 8, B), axis=0)))
            return tuple(out)

        tops = lax.fori_loop(lo, hi, scores, tuple(jnp.full((8, B), -3e38, f32) for _ in range(4)))
        tops = [jnp.max(m, axis=0, keepdims=True) for m in tops]

        def mixing(j, carry):
            sums, accs = carry
            r = pl.ds(pl.multiple_of(j * B, B), B)
            new_sums, new_accs = [], []
            for h in range(4):
                e = jnp.exp(s_s[h, r, :] - tops[h])
                new_sums.append(sums[h] + fold(e))
                new_accs.append(accs[h] + dot(vt[64 * h : 64 * h + 64, r], e.astype(bf16), 1, 0))
            return tuple(new_sums), tuple(new_accs)

        zeros = (
            tuple(jnp.zeros((8, B), f32) for _ in range(4)),
            tuple(jnp.zeros((64, B), f32) for _ in range(4)),
        )
        sums, accs = lax.fori_loop(lo, hi, mixing, zeros)
        for h in range(4):
            total = jnp.sum(sums[h], axis=0, keepdims=True)
            mixt_o[64 * h : 64 * h + 64, cols] = (accs[h] / total).astype(bf16)
            lse_o[h : h + 1, cols] = tops[h] + jnp.log(total)
    mix_o[...] = mixt_o[...].T


def attn_fwd(g, blk, offs, n1, pieces, small, segc, segr):
    return call(
        functools.partial(attn_fwd_kernel, g=g),
        [blk, offs, n1, *pieces, small, segc, segr],
        out_shape=[sds((T, 256), bf16)] * 4
        + [sds((256, T), bf16), sds((4, T), f32), sds((D, D), bf16)],
        in_specs=[SM, SM] + [VM] * 8,
        out_specs=[VM] * 7,
        scratch_shapes=[
            pltpu.VMEM((2, T, 256), bf16),
            pltpu.VMEM((4, 256, T), bf16),
            pltpu.VMEM((256, T), bf16),
            pltpu.VMEM((4, T, B), f32),
        ],
        compiler_params=params(),
        cost_estimate=cost(13),
        name="attn_fwd",
        main=True,
    )


def post_kernel(x, m0, m1, m2, rest, small, x1_o, n2_o, n2t_o, w):
    @pl.when(pl.program_id(0) == 0)
    def _():
        gathered_rows(w, (rest,), None, 0, 6, RB, 0)

    a = x[...].astype(f32) + small[4:5, :]
    for g, m in enumerate((m0, m1, m2)):
        a += dot(m[...], w[256 * g : 256 * g + 256, :], 1, 0)
    x1_o[...] = a
    c = a - jnp.mean(a, -1, keepdims=True)
    r = lax.rsqrt(jnp.mean(c * c, -1, keepdims=True) + 1e-06)
    n = (c * r * small[5:6, :] + small[6:7, :]).astype(bf16)
    n2_o[...] = n
    n2t_o[...] = n.T


def post_attn(x, mixes, rest, small):
    rows = pl.BlockSpec((B, D), lambda r: (r, 0))
    part = pl.BlockSpec((B, 256), lambda r: (r, 0))
    return call(
        post_kernel,
        [x, *mixes, rest, small],
        grid=(NB,),
        out_shape=[sds((T, D), f32), sds((T, D), bf16), sds((D, T), bf16)],
        in_specs=[rows, part, part, part, pl.BlockSpec((OWN, QR, 128), lambda r: (0, 3 * FR // QR, 0))]
        + [pl.BlockSpec((SR, D), lambda r: (0, 0))],
        out_specs=[rows, rows, pl.BlockSpec((D, B), lambda r: (0, r))],
        scratch_shapes=[pltpu.VMEM((D, D), bf16)],
        compiler_params=params(),
        cost_estimate=cost(6.5),
        name="post_attn",
        main=True,
    )


C0 = math.sqrt(2.0 / math.pi)
C1 = 0.044715


def ff_chunk(row, n2, dy, wu, wd, ub, dub, hid_o, ht, dp):
    size = n2.shape[0]
    rows = pl.ds(pl.multiple_of(row * size, size), size)
    for c in range(FC // FCOL):
        cols = slice(FCOL * c, FCOL * c + FCOL)
        pre = dot(n2, wu[:, cols], 1, 0) + ub[0:1, cols]
        dh = dot(dy, wd[cols, :], 1, 1)
        sq = pre * pre
        t = jnp.tanh(C0 * pre * (1.0 + C1 * sq))
        half = 0.5 + 0.5 * t
        hid = (pre * half).astype(bf16)
        slope = half + (0.5 * C0) * pre * (1.0 - t * t) * (1.0 + (3.0 * C1) * sq)
        dpre = dh * slope
        dub[0:8, cols] += fold(dpre)
        hid_o[:, cols] = hid
        ht[cols, rows] = hid.T
        dp[rows, cols] = dpre.astype(bf16)
    return dot(dp[rows, :], wu[...], 1, 1)


def ff_weights(rest, wu, wd):
    gathered_rows(wu, (rest,), None, 0, 8, RB, 0)
    gathered_rows(wd, (rest,), None, 8 * RB, 6, FB, 0)


def ff_bias(j, small, ub):
    for t in range(8):
        halves = []
        for d in (2 * t, 2 * t + 1):
            c = 192 * (d % 4) + FB * j
            halves.append(small[8 + d // 4 : 9 + d // 4, c : c + FB])
        ub[0:1, 128 * t : 128 * t + 128] = jnp.concatenate(halves, axis=1)


def ff_grads(grads, order, n2ts, dp, ht, dys, gu, gd):
    gu[...] = dot(n2ts[...], dp[...], 1, 0).astype(bf16)
    gd[...] = dot(ht[...], dys[...], 1, 0).astype(bf16)
    scattered_rows(gu, grads, order, 0, 8, RB, 0)
    scattered_rows(gd, grads, order, 8 * RB, 6, FB, 0)


FF_SCRATCH = [
    pltpu.VMEM((D, FC), bf16),
    pltpu.VMEM((FC, D), bf16),
    pltpu.VMEM((8, FC), f32),
    pltpu.VMEM((D, T), bf16),
    pltpu.VMEM((T, D), bf16),
    pltpu.VMEM((FC, T), bf16),
    pltpu.VMEM((T, FC), bf16),
    pltpu.VMEM((D, FC), bf16),
    pltpu.VMEM((FC, D), bf16),
]


def ff_two_kernel(n2, n2t, dy, rest, small, hid_o, acc_o, grads, dub,
                  wu, wd, ub, n2ts, dys, ht, dp, gu, gd, n2s, acc):
    j, row = pl.program_id(0), pl.program_id(1)
    rows = pl.ds(pl.multiple_of(row * FBLK, FBLK), FBLK)

    @pl.when(row == 0)
    def _():
        ff_weights(rest, wu, wd)
        dub[...] = jnp.zeros_like(dub)
        for n in range(2):
            pl.when(j == n)(functools.partial(ff_bias, n, small, ub))

    @pl.when(j == 0)
    def _():
        n2ts[:, rows] = n2t[...]
        dys[rows, :] = dy[...]
        n2s[rows, :] = n2[...]
        acc[rows, :] = jnp.zeros((FBLK, D), f32)

    dn = acc[rows, :] + ff_chunk(row, n2s[rows, :], dys[rows, :], wu, wd, ub, dub, hid_o, ht, dp)
    acc[rows, :] = dn
    acc_o[...] = dn

    @pl.when(row == FN - 1)
    def _():
        ff_grads((grads,), None, n2ts, dp, ht, dys, gu, gd)


def feed_forward_two(n2, n2t, dy, rest, small):
    first = lambda j, r: r + (FN - 1 - r) * j
    rows = pl.BlockSpec((FBLK, D), lambda j, r: (first(j, r), 0))
    return call(
        ff_two_kernel,
        [n2, n2t, dy, rest, small],
        grid=(2, FN),
        out_shape=[
            sds((T, 2 * FC), bf16),
            sds((T, D), f32),
            sds((OWN, 2 * FR, 128), bf16),
            sds((8, 2 * FC), f32),
        ],
        in_specs=[
            rows,
            pl.BlockSpec((D, FBLK), lambda j, r: (0, first(j, r))),
            rows,
            pl.BlockSpec((OWN, FR, 128), lambda j, r: (0, j, 0)),
            pl.BlockSpec((SR, D), lambda j, r: (0, 0)),
        ],
        out_specs=[
            pl.BlockSpec((FBLK, FC), lambda j, r: (r, j)),
            pl.BlockSpec((FBLK, D), lambda j, r: (r * j, 0)),
            pl.BlockSpec((OWN, FR, 128), lambda j, r: (0, j, 0)),
            pl.BlockSpec((8, FC), lambda j, r: (0, j)),
        ],
        scratch_shapes=FF_SCRATCH + [pltpu.VMEM((T, D), bf16), pltpu.VMEM((T, D), f32)],
        compiler_params=params(),
        cost_estimate=cost(28),
        name="feed_forward_two",
        main=True,
    )


def norm_back(v, up, gain):
    c = v - jnp.mean(v, -1, keepdims=True)
    r = lax.rsqrt(jnp.mean(c * c, -1, keepdims=True) + 1e-06)
    hat = c * r
    g = up * gain
    back = r * (g - jnp.mean(g, -1, keepdims=True) - hat * jnp.mean(g * hat, -1, keepdims=True))
    return back, up * hat


def ff_last_kernel(offs, n2, n2t, dy, rest, small, acc, x1, t0, t1, t2, rest_o,
                   hid_o, dub, dx1_o, dmix_o, keep, send, keep_o, send_o, sums,
                   wu, wd, ub, n2ts, dys, ht, dp, gu, gd, w, low, go):
    row = pl.program_id(0)
    rows = pl.ds(pl.multiple_of(row * B, B), B)

    @pl.when(row == 0)
    def _():
        ff_weights(rest, wu, wd)
        ff_bias(2, small, ub)
        gathered_rows(w, (rest_o,), None, 0, 6, RB, 0)
        dub[...] = jnp.zeros_like(dub)
        sums[...] = jnp.zeros_like(sums)

    n2ts[:, rows] = n2t[...]
    dys[rows, :] = dy[...]
    up = acc[...] + ff_chunk(row, n2[...], dy[...], wu, wd, ub, dub, hid_o, ht, dp)
    d = dy[...].astype(f32)
    back, hats = norm_back(x1[...], up, small[5:6, :])
    dx1 = d + back
    dx1_o[...] = dx1
    lowered = dx1.astype(bf16)
    low[rows, :] = lowered
    sums[0:8, :] += fold(dx1)
    sums[8:16, :] += fold(hats)
    sums[16:24, :] += fold(up)
    sums[24:32, :] += fold(d)
    dmix_o[...] = dot(lowered, w[...], 1, 1).astype(bf16)

    @pl.when(row == NB - 1)
    def _():
        ff_grads((keep, send), offs, n2ts, dp, ht, dys, gu, gd)
        for g, t in enumerate((t0, t1, t2)):
            go[256 * g : 256 * g + 256, :] = dot(t[...], low[...], 1, 0).astype(bf16)
        scattered_rows(go, (keep_o, send_o), offs, 0, 6, RB, 0)


def feed_forward_last(offs, n2, n2t, dy, rest, small, acc, x1, mixts):
    rows = pl.BlockSpec((B, D), lambda r: (r, 0))
    packed = pl.BlockSpec((8, FR, 128), lambda r: (0, 0, 0))
    packed_o = pl.BlockSpec((8, QR, 128), lambda r: (0, 0, 0))
    once = dict(pipeline_mode=pl.Buffered(1))
    return call(
        ff_last_kernel,
        [offs, n2, n2t, dy, rest, small, acc, x1, *mixts, rest],
        grid=(NB,),
        out_shape=[
            sds((T, FC), bf16),
            sds((8, FC), f32),
            sds((T, D), f32),
            sds((T, D), bf16),
            sds((8, FR, 128), bf16),
            sds((8, FR, 128), bf16),
            sds((8, QR, 128), bf16),
            sds((8, QR, 128), bf16),
            sds((32, D), f32),
        ],
        in_specs=[
            SM,
            rows,
            pl.BlockSpec((D, B), lambda r: (0, r)),
            rows,
            pl.BlockSpec((OWN, FR, 128), lambda r: (0, 2, 0), **once),
            pl.BlockSpec((SR, D), lambda r: (0, 0)),
            rows,
            rows,
        ]
        + [pl.BlockSpec((256, T), lambda r: (0, 0), **once)] * 3
        + [pl.BlockSpec((OWN, QR, 128), lambda r: (0, 3 * FR // QR, 0), **once)],
        out_specs=[
            pl.BlockSpec((B, FC), lambda r: (r, 0)),
            pl.BlockSpec((8, FC), lambda r: (0, 0)),
            rows,
            rows,
            packed,
            packed,
            packed_o,
            packed_o,
            pl.BlockSpec((32, D), lambda r: (0, 0)),
        ],
        scratch_shapes=FF_SCRATCH
        + [pltpu.VMEM((D, D), bf16), pltpu.VMEM((T, D), bf16), pltpu.VMEM((D, D), bf16)],
        compiler_params=params(),
        cost_estimate=cost(22),
        name="feed_forward_last",
        main=True,
    )


def attn_bwd_kernel(
    blk, offs, q, k, v, do, mix, lse, n1t, segc, segr,
    dqkv_o, keep, send, sums, kn, vn, qt, dt, kt, qm, dm, dqt, gw,
):
    left, right = segment_tail(segc, segr, None)
    sub = lax.broadcasted_iota(jnp.int32, (16, T), 0)
    qs = q[...] * jnp.asarray(0.125, bf16)
    qtt = qs.T
    dtt = do[...].T
    kt[...] = k[...].T
    prod = (do[...].astype(f32) * mix[...].astype(f32)).T
    zero = jnp.zeros((64, T), bf16)
    pad = jnp.zeros((112, T), bf16)
    lane = lax.broadcasted_iota(jnp.int32, (T, 128), 1)
    nothing = jnp.zeros((T, 128), bf16)
    for p in range(2):
        at = slice(128 * p, 128 * p + 128)
        kn[p, :, :128] = k[:, at]
        kn[p, :, 128:] = left
        vn[p, :, :128] = v[:, at]
        vn[p, :, 128:] = left
        for e in range(2):
            h = 2 * p + e
            mine = (lane >= 64 * e) & (lane < 64 * e + 64)
            qm[p, e] = jnp.where(mine, qs[:, at], nothing)
            dm[p, e] = jnp.where(mine, do[:, at], nothing)
            for dst, src in ((qt, qtt), (dt, dtt)):
                dst[h, 64 * e : 64 * e + 64, :] = src[64 * h : 64 * h + 64]
                dst[h, 64 - 64 * e : 128 - 64 * e, :] = zero
                dst[h, 144:, :] = pad
            a, b, c = three(-lse[h : h + 1, :])
            tail = jnp.where(sub == 4, a, jnp.where(sub == 5, b, jnp.where(sub == 6, c, right)))
            qt[h, 128:144, :] = tail.astype(bf16)
            a, b, c = three(-rowsum(prod[64 * h : 64 * h + 64, :]))
            tail = jnp.where(sub == 4, a, jnp.where(sub == 5, b, jnp.where(sub == 6, c, 0.0)))
            dt[h, 128:144, :] = tail.astype(bf16)
    dqt[...] = jnp.zeros_like(dqt)
    for j in range(NB):
        lo = blk[0, j]
        hi = blk[1, j]
        keys = slice(j * B, (j + 1) * B)

        def step(i, carry):
            dks, dvs = carry
            cols = pl.ds(pl.multiple_of(i * B, B), B)
            new_dk, new_dv = [], []
            for p in range(2):
                hs = (2 * p, 2 * p + 1)
                s2 = [dot(kn[p, keys, :], qt[h, :, cols], 1, 0) for h in hs]
                d2 = [dot(vn[p, keys, :], dt[h, :, cols], 1, 0) for h in hs]
                p2 = [jnp.exp(s) for s in s2]
                g2 = [(a * b).astype(bf16) for a, b in zip(p2, d2)]
                pr = jnp.concatenate([a.astype(bf16) for a in p2], axis=1)
                gr = jnp.concatenate(g2, axis=1)
                new_dv.append(dvs[p] + dot(pr, jnp.concatenate([dm[p, 0, cols, :], dm[p, 1, cols, :]], axis=0), 1, 0))
                new_dk.append(dks[p] + dot(gr, jnp.concatenate([qm[p, 0, cols, :], qm[p, 1, cols, :]], axis=0), 1, 0))
                for e in range(2):
                    h = 2 * p + e
                    dqt[64 * h : 64 * h + 64, cols] += dot(kt[64 * h : 64 * h + 64, keys], g2[e], 1, 0)
            return tuple(new_dk), tuple(new_dv)

        zeros = tuple(jnp.zeros((B, 128), f32) for _ in range(2))
        dks, dvs = lax.fori_loop(lo, hi, step, (zeros, zeros))
        for p in range(2):
            dqkv_o[keys, 256 + 128 * p : 384 + 128 * p] = dks[p].astype(bf16)
            dqkv_o[keys, 512 + 128 * p : 640 + 128 * p] = dvs[p].astype(bf16)
    dqkv_o[:, :256] = (dqt[...] * 0.125).astype(bf16).T
    sums[:, :256] = fold(dqkv_o[:, :256].astype(f32))
    sums[:, 256:] = fold(dqkv_o[:, 512:].astype(f32))
    gw[...] = dot(n1t[...], dqkv_o[...], 1, 0).astype(bf16)
    scattered_rows(gw, (keep, send), offs, 0, 6, RB, 0)


def attn_bwd(g, blk, offs, q, k, v, dmix, mix, lse, n1t, segc, segr):
    whole = lambda a: pl.BlockSpec(a.shape, lambda r: (0,) * a.ndim)
    outs = [
        sds((T, D), bf16),
        sds((8, QR, 128), bf16),
        sds((8, QR, 128), bf16),
        sds((8, 512), f32),
    ]
    return call(
        attn_bwd_kernel,
        [blk, offs, q, k, v, dmix, mix, lse, n1t, segc, segr],
        grid=(1,),
        out_shape=outs,
        in_specs=[SM, SM, whole(q), whole(k), whole(v), pl.BlockSpec((T, 256), lambda r: (0, g))]
        + [whole(a) for a in (mix, lse, n1t, segc, segr)],
        out_specs=[whole(a) for a in outs],
        scratch_shapes=[
            pltpu.VMEM((2, T, 256), bf16),
            pltpu.VMEM((2, T, 256), bf16),
            pltpu.VMEM((4, 256, T), bf16),
            pltpu.VMEM((4, 256, T), bf16),
            pltpu.VMEM((256, T), bf16),
            pltpu.VMEM((2, 2, T, 128), bf16),
            pltpu.VMEM((2, 2, T, 128), bf16),
            pltpu.VMEM((256, T), f32),
            pltpu.VMEM((D, D), bf16),
        ],
        compiler_params=params(),
        cost_estimate=cost(21),
        name="attn_bwd",
        main=True,
    )


def last_kernel(offs, d0, d1, d2, w0, w1, w2, x, dx1, small, mids, s0, s1, s2, u0, u1,
                gt_o, keep, send, sums, sg):
    step = pl.program_id(0)

    @pl.when(step == 0)
    def _():
        sums[...] = jnp.zeros_like(sums)

    dn = dot(d0[...], w0[...], 1, 1) + dot(d1[...], w1[...], 1, 1) + dot(d2[...], w2[...], 1, 1)
    back, hats = norm_back(x[...].astype(f32), dn, small[0:1, :])
    gt_o[...] = (dx1[...] + back).astype(bf16)
    sums[0:8, :] += fold(hats)
    sums[8:16, :] += fold(dn)

    @pl.when(step == NB - 1)
    def _():
        total = lambda v: jnp.sum(v, axis=0, keepdims=True)
        sg[...] = jnp.zeros_like(sg)
        sg[0:1, :] = total(sums[0:8, :])
        sg[1:2, :] = total(sums[8:16, :])
        for g, s in enumerate((s0, s1, s2)):
            sg[2:3, 256 * g : 256 * g + 256] = total(s[:, :256])
            sg[3:4, 256 * g : 256 * g + 256] = total(s[:, 256:])
        for n in range(4):
            sg[4 + n : 5 + n, :] = total(mids[8 * n : 8 * n + 8, :])
        ups = [total(u0[:, :FC]), total(u0[:, FC:]), total(u1[...])]
        for n in range(4):
            parts = []
            for d in range(4 * n, 4 * n + 4):
                for j in range(3):
                    parts.append(ups[j][:, FB * d : FB * d + FB])
            sg[8 + n : 9 + n, :] = jnp.concatenate(parts, axis=1)
        low = sg[...].astype(bf16)
        row = lax.broadcasted_iota(jnp.int32, (D, 128), 0)
        col = lax.broadcasted_iota(jnp.int32, (D, 128), 1)
        for s in range(OWN):
            hot = jnp.where((row == col + offs[s] * RB) & (col < RB), 1.0, 0.0).astype(bf16)
            (keep, send)[s // 8][s % 8, :, :] = dot(low, hot, 1, 0).astype(bf16)


def last_norm(offs, dqkvs, ws, x, dx1, small, mids, ssums, usums):
    rows = pl.BlockSpec((B, D), lambda r: (r, 0))
    whole = lambda a: pl.BlockSpec(a.shape, lambda r: (0,) * a.ndim)
    packed = pl.BlockSpec((8, SR, 128), lambda r: (0, 0, 0))
    return call(
        last_kernel,
        [offs, *dqkvs, *ws, x, dx1, small, mids, *ssums, *usums],
        grid=(NB,),
        out_shape=[sds((T, D), bf16), sds((8, SR, 128), bf16), sds((8, SR, 128), bf16)],
        in_specs=[SM] + [rows] * 3 + [whole(w) for w in ws] + [rows, rows]
        + [whole(a) for a in (small, mids, *ssums, *usums)],
        out_specs=[rows, packed, packed],
        scratch_shapes=[pltpu.VMEM((16, D), f32), pltpu.VMEM((SR, D), f32)],
        compiler_params=params(),
        cost_estimate=cost(10.5),
        name="last_norm",
        main=True,
    )


def out_kernel(h01, h2, r0, r1, r2, x1, small, o, wd):
    @pl.when(pl.program_id(0) == 0)
    def _():
        for j, ref in enumerate((r0, r1, r2)):
            gathered_rows(wd.at[FC * j : FC * j + FC], (ref,), None, 0, 6, FB, 0)

    a = x1[...] + small[7:8, :]
    a += dot(h01[...], wd[: 2 * FC, :], 1, 0) + dot(h2[...], wd[2 * FC :, :], 1, 0)
    o[...] = a.astype(bf16)


def layer_out(h01, h2, rest, x1, small):
    rows = pl.BlockSpec((B, D), lambda r: (r, 0))
    downs = [pl.BlockSpec((OWN, FR // 2, 128), lambda r, j=j: (0, 2 * j + 1, 0)) for j in range(3)]
    return call(
        out_kernel,
        [h01, h2, rest, rest, rest, x1, small],
        grid=(NB,),
        out_shape=sds((T, D), bf16),
        in_specs=[pl.BlockSpec((B, 2 * FC), lambda r: (r, 0)), pl.BlockSpec((B, FC), lambda r: (r, 0))]
        + downs
        + [rows, pl.BlockSpec((SR, D), lambda r: (0, 0))],
        out_specs=rows,
        scratch_shapes=[pltpu.VMEM((FF, D), bf16)],
        compiler_params=params(),
        cost_estimate=cost(10),
        name="layer_out",
        main=True,
    )


def adamw(weight, grad, mom_one, mom_two, rate):
    next_one = BETA1 * mom_one + (1.0 - BETA1) * grad
    next_two = BETA2 * mom_two + (1.0 - BETA2) * grad * grad
    fixed_one = next_one / (1.0 - BETA1**STEP)
    fixed_two = next_two / (1.0 - BETA2**STEP)
    updated = weight - rate * (fixed_one / (jnp.sqrt(fixed_two) + ADAM_EPS) + DECAY * weight)
    return (updated, next_one, next_two)


def whole_rows(offs, pair, at, dst):
    half = dst.shape[0] // 2
    for n, y in enumerate((offs[OWN], 1 - offs[OWN])):
        dst[pl.ds(pl.multiple_of(y * half, 16), half), :] = pair[n][at : at + half, :]


def update(outs, at, state, grad, rate):
    for o, val in zip(outs, adamw(state[0][at], grad, state[1][at], state[2][at], rate)):
        o[at] = val


def adam_heads_kernel(offs, *refs):
    pair, last, qkv, out, small = refs[:2], refs[2:4], refs[4:7], refs[7:10], refs[10:13]
    qkv_o, out_o, small_o = refs[13:16], refs[16:19], refs[19:22]
    packs = refs[22:]
    for n in range(3):
        whole_rows(offs, pair, (FR + n * QR) // 2, packs[n])
    for g in range(3):
        for part in range(3):
            for t in range(2):
                c = D * part + 256 * g + 128 * t
                r = (2 * part + t) * RB
                if g < 2:
                    grad = packs[g][r : r + RB, :].astype(f32)
                else:
                    grad = last[0][r : r + RB, :].astype(f32) + last[1][r : r + RB, :].astype(f32)
                update(qkv_o, (slice(None), slice(c, c + 128)), qkv, grad, RATES[0])
    for t in range(6):
        grad = packs[2][t * RB : (t + 1) * RB, :].astype(f32)
        update(out_o, (slice(None), slice(128 * t, 128 * t + 128)), out, grad, RATES[1])
    grad = last[0][QR : QR + SR, :].astype(f32) + last[1][QR : QR + SR, :].astype(f32)
    update(small_o, Ellipsis, small, grad[:12, :RB], RATES[4])


def adam_ff_kernel(offs, *refs):
    two, pair, up, down = refs[:2], refs[2:4], refs[4:7], refs[7:10]
    up_o, down_o = refs[10:13], refs[13:16]
    pack = refs[16]
    whole_rows(offs, pair, 0, pack)

    def total(j, r, n):
        if j == 2:
            return pack[r : r + n, :].astype(f32)
        rows = slice(FR * j + r, FR * j + r + n)
        return two[0][rows, :].astype(f32) + two[1][rows, :].astype(f32)

    for t in range(8):
        parts = [total(j, t * RB, RB) for j in range(3)]
        grad = jnp.concatenate([p[:, :64] for p in parts] + [p[:, 64:] for p in parts], axis=1)
        update(up_o, (slice(None), slice(384 * t, 384 * t + 384)), up, grad, RATES[2])
    for j in range(3):
        for t in range(6):
            at = (slice(FB * j, FB * j + FB), slice(128 * t, 128 * t + 128))
            update(down_o, at, down, total(j, 8 * RB + t * FB, FB), RATES[3])


def adam_call(kernel, offs, grads, states, scratch, name):
    shapes = [sds(s.shape, f32) for s in states]
    return call(
        kernel,
        [offs, *grads, *states],
        out_shape=shapes,
        in_specs=[SM] + [VM] * (len(grads) + len(states)),
        out_specs=[VM] * len(shapes),
        scratch_shapes=[pltpu.VMEM((r, 128), bf16) for r in scratch],
        compiler_params=params(),
        cost_estimate=cost(),
        name=name,
    )


def shifted(f):
    pairs = []
    for z in range(4):
        for x in range(2):
            for c in range(2):
                tz, tx, tc = f(z, x, c)
                pairs.append(((z * 2 + x) * 2 + c, (tz * 2 + tx) * 2 + tc))
    return pairs


TO_CORE = shifted(lambda z, x, c: (z, x, 1 - c))
TO_X = shifted(lambda z, x, c: (z, 1 - x, c))
TO_Z = [shifted(lambda z, x, c, s=s: ((z + s) % 4, x, c)) for s in range(4)]
FROM_Z = [shifted(lambda z, x, c, s=s: ((z - s) % 4, x, c)) for s in range(4)]
TO_Y = [(0, 1), (1, 0)]


def stack_kernel(a, b, c, d, *refs):
    out = refs[len(refs) // 2]
    for n, ref in enumerate((a, b, c, d)):
        out[n] = ref[...]


class Gather:
    def __init__(self, own):
        self.own = own

    def along_z(self):
        self.parts = [self.own] + [lax.ppermute(self.own, "dp", TO_Z[s]) for s in (1, 2, 3)]

    def along_x(self, *later):
        anywhere = pl.BlockSpec(memory_space=pl.ANY)
        outs = call(
            stack_kernel,
            [*self.parts, *[g.own for g in later]],
            out_shape=[sds((4,) + self.own.shape, bf16)] + [sds(g.own.shape, bf16) for g in later],
            in_specs=[VM] * 4 + [anywhere] * len(later),
            out_specs=[VM] + [anywhere] * len(later),
            input_output_aliases={4 + n: 1 + n for n in range(len(later))},
            compiler_params=params(),
            cost_estimate=cost(1.7),
            name="stack",
        )
        for g, own in zip(later, outs[1:]):
            g.own = own
        line = outs[0]
        self.pieces = [line, lax.ppermute(line, "dp", TO_X), lax.ppermute(line, "dp", TO_CORE)]

    def to_core(self, hold=False):
        if hold:
            self.pieces[1] = wait_here(self.pieces[1])[0]
        self.pieces.append(lax.ppermute(self.pieces[1], "dp", TO_CORE))


def add_core_kernel(*refs):
    half = len(refs) // 2 - 1
    a, b = refs[-2:]
    at = 0
    for keep, got in zip(refs[:half], refs[half : 2 * half]):
        rows = keep.shape[1]
        a[:, at : at + rows] = (keep[:4].astype(f32) + got[:4].astype(f32)).astype(bf16)
        b[:, at : at + rows] = (keep[4:].astype(f32) + got[4:].astype(f32)).astype(bf16)
        at += rows


def add_core_half_kernel(offs, *refs):
    n = len(refs) // 2 - 1
    outs = refs[-2:]
    at = 0
    for keep, got in zip(refs[:n], refs[n : 2 * n]):
        half = keep.shape[1] // 2
        for out, y in zip(outs, (offs[OWN], 1 - offs[OWN])):
            rows = pl.ds(pl.multiple_of(y * half, 16), half)
            out[:, at : at + half] = (keep[:, rows].astype(f32) + got[:, rows].astype(f32)).astype(bf16)
        at += half


def add_y_kernel(*refs):
    n = len(refs) // 2 - 1
    a, b = refs[-2:]
    at = 0
    for keep, got in zip(refs[:n], refs[n : 2 * n]):
        rows = keep.shape[2]
        total = (keep[...].astype(f32) + got[...].astype(f32)).astype(bf16)
        a[:, at : at + rows] = total[0]
        b[:, at : at + rows] = total[1]
        at += rows


def add_x_kernel(keep, got, *outs):
    for s in range(4):
        outs[s][...] = (keep[s].astype(f32) + got[s].astype(f32)).astype(bf16)


def add_z_kernel(a, b, c, d, o):
    o[...] = (a[...].astype(f32) + b[...].astype(f32) + c[...].astype(f32) + d[...].astype(f32)).astype(bf16)


def add_call(kernel, args, outs, name, then, beside):
    if beside:
        SIDE.append((kernel, args, outs, then))
        return
    then(add_alone(kernel, args, outs, name))


def add_alone(kernel, args, outs, name):
    return call(
        kernel,
        args,
        out_shape=outs,
        in_specs=[VM] * len(args),
        out_specs=[VM] * len(outs),
        compiler_params=params(),
        cost_estimate=cost(),
        name=name,
    )


class Scatter:
    def __init__(self, *packs):
        self.keeps = [p[0] for p in packs]
        self.rows = sum(k.shape[1] for k in self.keeps)
        self.gots = [lax.ppermute(p[1], "dp", TO_CORE) for p in packs]

    def half_along_y(self, offs):
        self.rows //= 2
        args = (*self.keeps, *self.gots)
        block = lambda r: pl.BlockSpec((2, r, 128), lambda i: (i, 0, 0))
        mine, other = call(
            add_core_half_kernel,
            [offs, *args],
            grid=(4,),
            out_shape=[sds((8, self.rows, 128), bf16)] * 2,
            in_specs=[SM] + [block(a.shape[1]) for a in args],
            out_specs=[block(self.rows)] * 2,
            compiler_params=params(),
            cost_estimate=cost(),
            name="add_core_half",
        )
        self.halves = (mine, lax.ppermute(other, "rep", TO_Y))

    def join_along_x(self, other):
        self.rows += other.rows
        cut = lambda a: a.reshape(2, 4, a.shape[1], 128)
        args = [cut(s.halves[n]) for n in range(2) for s in (self, other)]
        self.mine, send = call(
            add_y_kernel,
            args,
            grid=(4,),
            out_shape=[sds((4, self.rows, 128), bf16)] * 2,
            in_specs=[pl.BlockSpec((2, 1, a.shape[2], 128), lambda i: (0, i, 0, 0)) for a in args],
            out_specs=[pl.BlockSpec((1, self.rows, 128), lambda i: (i, 0, 0))] * 2,
            compiler_params=params(),
            cost_estimate=cost(),
            name="add_y",
        )
        self.got = lax.ppermute(send, "dp", TO_X)

    def along_x(self, beside=False):
        outs = [sds((4, self.rows, 128), bf16)] * 2

        def then(out):
            self.mine = out[0]
            self.got = lax.ppermute(out[1], "dp", TO_X)

        add_call(add_core_kernel, (*self.keeps, *self.gots), outs, "add_core", then, beside)

    def along_z(self, beside=False):
        outs = [sds((self.rows, 128), bf16)] * 4

        def then(parts):
            self.parts = [parts[0]] + [lax.ppermute(parts[s], "dp", FROM_Z[s]) for s in (1, 2, 3)]

        add_call(add_x_kernel, (self.mine, self.got), outs, "add_x", then, beside)

    def along_y(self, beside=False):
        def then(out):
            self.done = (out[0], lax.ppermute(out[0], "rep", TO_Y))

        add_call(add_z_kernel, self.parts, [sds((self.rows, 128), bf16)], "add_z", then, beside)


def gather_any(small, wq, wo, wu, wd):
    full = lambda w, axis: lax.all_gather(w.astype(bf16), "dp", axis=axis, tiled=True)
    small = full(small, 1)
    blocks = small.reshape(small.shape[0], OWN, RB).transpose(1, 0, 2)
    blocks = jnp.pad(blocks, ((0, 0), (0, SR - small.shape[0]), (0, 128 - RB)))
    q = full(wq, 0).reshape(OWN, RB, 3, 3, 2, 128).transpose(3, 0, 2, 4, 1, 5).reshape(3, OWN, QR, 128)
    o = full(wo, 0).reshape(OWN, RB, 6, 128).transpose(0, 2, 1, 3).reshape(OWN, QR, 128)
    u = full(wu, 0).reshape(OWN, RB, 8, 2, 3, FB).transpose(4, 0, 2, 1, 3, 5).reshape(3, OWN, 8 * RB, 128)
    d = full(wd, 0).reshape(OWN, 3, FB, 6, 128).transpose(1, 0, 3, 2, 4).reshape(3, OWN, 6 * FB, 128)
    f = jnp.concatenate([u, d], 2)
    cut = lambda a: tuple(a[4 * n : 4 * n + 4] for n in range(4))
    heads = [cut(jnp.concatenate(p, 1)) for p in ((q[0], blocks), (q[1], q[2]))]
    return heads, jnp.concatenate([f[0], f[1], f[2], o], 1)


def scatter_any(packs, grads):
    q0, q1, q2, o, s = [jnp.concatenate(p, 0) for p in packs]
    q = jnp.stack([q0, q1, q2]).reshape(3, OWN, 3, 2, RB, 128).transpose(1, 4, 2, 0, 3, 5)
    f = grads.reshape(OWN, 3, FR, 128)
    u = f[:, :, : 8 * RB].reshape(OWN, 3, 8, RB, 2, FB).transpose(0, 3, 2, 4, 1, 5)
    d = f[:, :, 8 * RB :].reshape(OWN, 3, 6, FB, 128).transpose(0, 1, 3, 2, 4)
    o = o.reshape(OWN, 6, RB, 128).transpose(0, 2, 1, 3)
    s = s[:, :12, :RB].transpose(1, 0, 2).reshape(12, D)
    flat = ((q.reshape(D, 3 * D), 0), (o.reshape(D, D), 0), (u.reshape(D, FF), 0), (d.reshape(FF, D), 0), (s, 1))
    out = []
    for g, axis in flat:
        g = lax.psum_scatter(g, "dp", scatter_dimension=axis, tiled=True)
        out.append(lax.psum(g, "rep").astype(f32))
    return out


def shards(tokens, segment_ids, cotangent, *state, wide):
    masters, firsts, seconds = state[:5], state[5:10], state[10:15]
    w_qkv, w_out, w_up, w_down, small_params = masters
    x = tokens[0]
    dy = cotangent[0]
    seg = segment_ids[0]
    segc = seg.reshape(T, 1)
    segr = seg.reshape(1, T)
    begins, ends = seg[::B], seg[B - 1 :: B]
    low = jnp.sum(ends[None, :] < begins[:, None], 1)
    high = jnp.sum(begins[None, :] <= ends[:, None], 1)
    blk = jnp.stack([low, high]).astype(jnp.int32)

    ORDER.clear()
    if wide:
        me = lax.axis_index("dp")
        s = jnp.arange(OWN, dtype=jnp.int32)
        z = (me // 4 - s % 4) % 4
        xx = (me // 2 % 2) ^ (s // 4 % 2)
        cc = (me % 2) ^ (s // 8)
        offs = jnp.append((z * 2 + xx) * 2 + cc, lax.axis_index("rep")).astype(jnp.int32)
        lines = [Gather(own) for own in pack(small_params, w_qkv, w_out, w_up, w_down)]
        lines[0].along_z()
        rest = lax.all_gather(lines[2].own, "dp", axis=0, tiled=True).reshape(OWN, 3 * FR + QR, 128)
        lines[0].along_x(lines[1])
        lines[0].to_core()
        lines[1].along_z()
        heads = [lines[0].pieces, None]
    else:
        offs = jnp.arange(OWN, dtype=jnp.int32)
        heads, rest = gather_any(small_params, w_qkv, w_out, w_up, w_down)

    n1, n1t, small = norm_first(offs, x, heads[0], QR)
    fwd = []
    if wide:
        lines[1].along_x()
        heads[1] = lines[1].pieces
    for g in range(3):
        fwd.append(attn_fwd(g, blk, offs, n1, heads[min(g, 1)], small, segc, segr))
        if wide and g == 0:
            lines[1].to_core(hold=True)
    x1, n2, n2t = post_attn(x, [f[3] for f in fwd], rest, small)
    sent = []

    def send(*packs):
        if wide:
            sent.append(Scatter(*packs))

    def move(n, name, beside=False):
        if wide:
            getattr(sent[n], "along_" + name)(beside)

    h01, acc, grads, u01 = feed_forward_two(n2, n2t, dy, rest, small)
    if wide:
        own_ff = lax.psum_scatter(grads.reshape(-1, 128), "dp", scatter_dimension=0, tiled=True)
    h2, u2, dx1, dmix, *grad, keep_o, send_o, mids = feed_forward_last(
        offs, n2, n2t, dy, rest, small, acc, x1, [f[4] for f in fwd]
    )
    send(grad)
    bwd = []
    for g in range(3):
        q, k, v, mix, _, lse, _ = fwd[g]
        bwd.append(attn_bwd(g, blk, offs, q, k, v, dmix, mix, lse, n1t, segc, segr))
        if g == 0 and wide:
            sent[0].half_along_y(offs)
        if g == 1 and wide:
            send(bwd[0][1:3], bwd[1][1:3], (keep_o, send_o))
            ORDER.append(sent[0].halves[1])
            sent[1].half_along_y(offs)
    if wide:
        sent[0].join_along_x(sent[1])
    grad_tokens, keep_s, send_s = last_norm(
        offs, [b[0] for b in bwd], [f[6] for f in fwd], x, dx1, small, mids,
        [b[3] for b in bwd], [u01, u2],
    )
    send(bwd[2][1:3], (keep_s, send_s))
    move(2, "x")
    move(0, "z")
    result = layer_out(h01, h2, rest, x1, small)
    move(2, "z")
    move(0, "y")
    states = [(masters[n], firsts[n], seconds[n]) for n in range(5)]
    new = [None] * 5
    if wide:
        (own_ff,) = wait_here(own_ff)
        pair = (own_ff, lax.ppermute(own_ff, "rep", TO_Y))
        move(2, "y")
        both = adam_call(adam_ff_kernel, offs, (*pair, *sent[0].done), states[2] + states[3], (FR,), "adam_ff")
        new[2], new[3] = both[:3], both[3:]
        both = adam_call(
            adam_heads_kernel, offs, (*sent[0].done, *sent[2].done),
            states[0] + states[1] + states[4], (QR, QR, QR), "adam_heads",
        )
        new[0], new[1], new[4] = both[:3], both[3:6], both[6:]
    else:
        packs = [(b[1], b[2]) for b in bwd] + [(keep_o, send_o), (keep_s, send_s)]
        owned = scatter_any(packs, jnp.concatenate([grads, jnp.concatenate(grad, 0)], 1))
        new = [adamw(states[n][0], owned[n], states[n][1], states[n][2], RATES[n]) for n in range(5)]
    return (
        result[None],
        grad_tokens[None],
        *[n[0] for n in new],
        *[n[1] for n in new],
        *[n[2] for n in new],
    )


def solution(mesh):
    rows = P("dp", None)
    small = P(None, "dp")
    state = (rows, rows, rows, rows, small)
    seqs = P(("dp", "rep"), None, None)
    return jax.shard_map(
        functools.partial(shards, wide=mesh.shape["dp"] == 16 and mesh.shape["rep"] == 2),
        mesh=mesh,
        in_specs=(seqs, P(("dp", "rep"), None), seqs) + state * 3,
        out_specs=(seqs, seqs) + state * 3,
        check_vma=False,
    )
```

```python
import functools
import math

import jax
import jax.numpy as jnp
from jax import lax
from jax.experimental import pallas as pl
from jax.experimental.pallas import tpu as pltpu
from jax.sharding import PartitionSpec as P

HEADS = 12
STEP = 10
BETA1 = 0.5
BETA2 = 0.5
ADAM_EPS = 1e-08
DECAY = 0.05
RATES = (0.04, 0.15, 0.04, 0.02, 0.3)

bf16 = jnp.bfloat16
f32 = jnp.float32

T = 1024
D = 768
FF = 3072
OWN = 16
RB = D // OWN
FB = FF // OWN // 3
FC = FF // 3
QR = 6 * RB
FR = 8 * RB + 6 * FB
SR = 16
B = 256
NB = T // B
LB = 256
LONGEST = 512
FBLK = 1024
FN = T // FBLK
FCOL = 256
MASK = 2.0**30
VMEM_LIMIT = 56 << 20

VM = pl.BlockSpec(memory_space=pltpu.VMEM)
SM = pl.BlockSpec(memory_space=pltpu.SMEM)


def params(**kw):
    return pltpu.CompilerParams(vmem_limit_bytes=VMEM_LIMIT, **kw)


ORDER = []
SIDE = []


def call(kernel, args, *, in_specs, out_specs, out_shape, main=False, token=None, **kw):
    side = list(SIDE) if main else []
    if main:
        SIDE.clear()
    extra = list(ORDER)
    single = not isinstance(out_shape, (list, tuple))
    shapes = [out_shape] if single else list(out_shape)
    specs = [out_specs] if single else list(out_specs)
    n, m = len(args), len(shapes)
    side_args = [a for _, more, _, _ in side for a in more]
    side_outs = [o for _, _, outs, _ in side for o in outs]
    grid = "grid" in kw
    whole = lambda a: pl.BlockSpec(a.shape, lambda r, k=len(a.shape): (0,) * k) if grid else VM

    def body(*refs):
        ins = refs[n : n + len(side_args)]
        rest = refs[n + len(side_args) + len(extra) :]
        outs = rest[m : m + len(side_outs)]

        def beside():
            i = o = 0
            for fn, more, results, _ in side:
                fn(*ins[i : i + len(more)], *outs[o : o + len(results)])
                i += len(more)
                o += len(results)

        if side:
            if grid:
                pl.when(pl.program_id(0) == 0)(beside)
            else:
                beside()
        return kernel(*refs[:n], *rest[:m], *rest[m + len(side_outs) :])

    out = pl.pallas_call(
        body,
        in_specs=list(in_specs)
        + [whole(a) for a in side_args]
        + [pl.BlockSpec(memory_space=pl.ANY)] * len(extra),
        out_specs=specs + [whole(a) for a in side_outs],
        out_shape=shapes + side_outs,
        **kw,
    )(*args, *side_args, *extra)
    out = list(out)
    ORDER[:] = [min(out[:m], key=lambda a: a.size) if token is None else out[token]]
    at = m
    for _, _, results, then in side:
        then(out[at : at + len(results)])
        at += len(results)
    return out[0] if single else out[:m]


def wait_here(*arrays):
    anywhere = pl.BlockSpec(memory_space=pl.ANY)
    order = list(ORDER)
    out = call(
        lambda *refs: None,
        arrays,
        out_shape=[sds(a.shape, a.dtype) for a in arrays],
        in_specs=[anywhere] * len(arrays),
        out_specs=[anywhere] * len(arrays),
        input_output_aliases={n: n for n in range(len(arrays))},
        name="wait_here",
    )
    ORDER[:] = order
    return out


def sds(shape, dtype):
    return jax.ShapeDtypeStruct(shape, dtype)


PACE = 0.7


def cost(us=3.0):
    return pl.CostEstimate(flops=int(us * PACE * 1e9), bytes_accessed=1, transcendentals=0)


def dot(a, b, ca, cb):
    return lax.dot_general(a, b, (((ca,), (cb,)), ((), ())), preferred_element_type=f32)


def fold(v):
    return jnp.sum(v.reshape(v.shape[0] // 8, 8, v.shape[1]), axis=0)


def rowsum(v):
    return jnp.sum(fold(v), axis=0, keepdims=True)


def gathered_rows(dst, refs, offs, base, tiles, rows, col):
    per = OWN // len(refs)
    for s in range(OWN):
        ref, at = refs[s // per], s % per
        off = s * rows if offs is None else pl.multiple_of(offs[s] * rows, 16)
        for t in range(tiles):
            dst[pl.ds(off, rows), col + 128 * t : col + 128 * t + 128] = ref[
                at, base + t * rows : base + (t + 1) * rows, :
            ]


def scattered_rows(src, outs, offs, base, tiles, rows, col):
    per = OWN // len(outs)
    for s in range(OWN):
        ref, at = outs[s // per], s % per
        off = s * rows if offs is None else pl.multiple_of(offs[s] * rows, 16)
        for t in range(tiles):
            ref[at, base + t * rows : base + (t + 1) * rows, :] = src[
                pl.ds(off, rows), col + 128 * t : col + 128 * t + 128
            ]


def pack_heads(dst, at, wq, g):
    for part in range(3):
        for t in range(2):
            c = D * part + 256 * g + 128 * t
            r = at + (2 * part + t) * RB
            dst[r : r + RB, :] = wq[:, c : c + 128].astype(bf16)


def pack_rest_kernel(wo, wu, wd, rest):
    for j in range(3):
        for t in range(8):
            r = FR * j + t * RB
            a = wu[:, 384 * t + 64 * j : 384 * t + 64 * j + 64]
            b = wu[:, 384 * t + 192 + 64 * j : 384 * t + 192 + 64 * j + 64]
            rest[r : r + RB, :] = jnp.concatenate([a, b], axis=1).astype(bf16)
        for t in range(6):
            r = FR * j + 8 * RB + t * FB
            rest[r : r + FB, :] = wd[FB * j : FB * j + FB, 128 * t : 128 * t + 128].astype(bf16)
    for t in range(6):
        r = 3 * FR + t * RB
        rest[r : r + RB, :] = wo[:, 128 * t : 128 * t + 128].astype(bf16)


def pack_heads_kernel(small, wq, q0, q12, token):
    token[...] = jnp.zeros_like(token)
    pack_heads(q0, 0, wq, 0)
    q0[QR : QR + SR, :] = jnp.zeros((SR, 128), bf16)
    q0[QR : QR + 12, :RB] = small[...].astype(bf16)
    pack_heads(q12, 0, wq, 1)
    pack_heads(q12, QR, wq, 2)


def pack(kernel, args, rows, name):
    return call(
        kernel,
        args,
        out_shape=[sds((r, 128), bf16) for r in rows],
        in_specs=[VM] * len(args),
        out_specs=[VM] * len(rows),
        compiler_params=params(),
        cost_estimate=cost(1.5),
        name=name,
    )


def norm_kernel(offs, x, p0, p1, p2, p3, n1, n1t, small, *, base):
    @pl.when(pl.program_id(0) == 0)
    def _():
        acc = jnp.zeros((SR, D), f32)
        row = lax.broadcasted_iota(jnp.int32, (128, D), 0)
        col = lax.broadcasted_iota(jnp.int32, (128, D), 1)
        for s in range(OWN):
            ref = (p0, p1, p2, p3)[s // 4]
            hot = jnp.where((col == row + offs[s] * RB) & (row < RB), 1.0, 0.0).astype(bf16)
            acc += dot(ref[s % 4, base : base + SR, :], hot, 1, 0)
        small[...] = acc

    v = x[...].astype(f32)
    c = v - jnp.mean(v, -1, keepdims=True)
    r = lax.rsqrt(jnp.mean(c * c, -1, keepdims=True) + 1e-06)
    n = (c * r * small[0:1, :] + small[1:2, :]).astype(bf16)
    n1[...] = n
    n1t[...] = n.T


def norm_first(offs, x, pieces, base):
    whole = [pl.BlockSpec(p.shape, lambda r: (0, 0, 0)) for p in pieces]
    return call(
        functools.partial(norm_kernel, base=base),
        [offs, x, *pieces],
        grid=(NB,),
        out_shape=[sds((T, D), bf16), sds((D, T), bf16), sds((SR, D), f32)],
        in_specs=[SM, pl.BlockSpec((B, D), lambda r: (r, 0))] + whole,
        out_specs=[
            pl.BlockSpec((B, D), lambda r: (r, 0)),
            pl.BlockSpec((D, B), lambda r: (0, r)),
            pl.BlockSpec((SR, D), lambda r: (0, 0)),
        ],
        compiler_params=params(),
        cost_estimate=cost(5),
        name="norm_first",
    )


def segment_tail(segc, segr, minus):
    lane = lax.broadcasted_iota(jnp.int32, (T, 128), 1)
    left = jnp.where((segc[...] == lane) | ((lane >= 4) & (lane < 7)), 1.0, 0.0).astype(bf16)
    sub = lax.broadcasted_iota(jnp.int32, (16, T), 0)
    right = jnp.where((segr[...] != sub) & (sub < 4), -MASK, 0.0)
    return left, right


def near(i):
    return [j for j in range(NB) if (abs(i - j) - 1) * B + 1 < LONGEST]


def three(v):
    hi = v.astype(bf16).astype(f32)
    rest = v - hi
    mid = rest.astype(bf16).astype(f32)
    return hi, mid, rest - mid


def attn_fwd_kernel(
    offs, n1, p0, p1, p2, p3, small, segc, segr,
    q_o, k_o, v_o, mix_o, mixt_o, lse_o, w_o, kn, qt, vt, s_s, *, g,
):
    gathered_rows(w_o, (p0, p1, p2, p3), offs, QR if g == 2 else 0, 6, RB, 0)
    qb = small[2:3, 256 * g : 256 * g + 256]
    vb = small[3:4, 256 * g : 256 * g + 256]
    q = (dot(n1[...], w_o[:, :256], 1, 0) + qb).astype(bf16)
    k = dot(n1[...], w_o[:, 256:512], 1, 0).astype(bf16)
    v = (dot(n1[...], w_o[:, 512:], 1, 0) + vb).astype(bf16)
    q_o[...] = q
    k_o[...] = k
    v_o[...] = v
    left, right = segment_tail(segc, segr, None)
    right = right.astype(bf16)
    qtt = (q * jnp.asarray(0.125, bf16)).T
    zero = jnp.zeros((64, T), bf16)
    pad = jnp.zeros((112, T), bf16)
    for p in range(2):
        kn[p, :, :128] = k[:, 128 * p : 128 * p + 128]
        kn[p, :, 128:] = left
        for e in range(2):
            h = 2 * p + e
            qt[h, 64 * e : 64 * e + 64, :] = qtt[64 * h : 64 * h + 64]
            qt[h, 64 - 64 * e : 128 - 64 * e, :] = zero
            qt[h, 128:144, :] = right
            qt[h, 144:, :] = pad
    vt[...] = v.T
    for i in range(NB):
        cols = slice(i * B, (i + 1) * B)
        tops, sums, accs = [], [], []
        for h in range(4):
            top = None
            for j in near(i):
                r = slice(j * B, (j + 1) * B)
                s = dot(kn[h // 2, r, :], qt[h, :, cols], 1, 0)
                s_s[h, r, :] = s
                most = jnp.max(s.reshape(B // 8, 8, B), axis=0)
                top = most if top is None else jnp.maximum(top, most)
            tops.append(jnp.max(top, axis=0, keepdims=True))
            part, acc = jnp.zeros((8, B), f32), jnp.zeros((64, B), f32)
            for j in near(i):
                r = slice(j * B, (j + 1) * B)
                e = jnp.exp(s_s[h, r, :] - tops[h])
                part += fold(e)
                acc += dot(vt[64 * h : 64 * h + 64, r], e.astype(bf16), 1, 0)
            sums.append(part)
            accs.append(acc)
        for h in range(4):
            total = jnp.sum(sums[h], axis=0, keepdims=True)
            mixt_o[64 * h : 64 * h + 64, cols] = (accs[h] / total).astype(bf16)
            lse_o[h : h + 1, cols] = tops[h] + jnp.log(total)
    mix_o[...] = mixt_o[...].T


def attn_fwd(g, offs, n1, pieces, small, segc, segr):
    return call(
        functools.partial(attn_fwd_kernel, g=g),
        [offs, n1, *pieces, small, segc, segr],
        out_shape=[sds((T, 256), bf16)] * 4
        + [sds((256, T), bf16), sds((4, T), f32), sds((D, D), bf16)],
        in_specs=[SM] + [VM] * 8,
        out_specs=[VM] * 7,
        scratch_shapes=[
            pltpu.VMEM((2, T, 256), bf16),
            pltpu.VMEM((4, 256, T), bf16),
            pltpu.VMEM((256, T), bf16),
            pltpu.VMEM((4, T, B), f32),
        ],
        compiler_params=params(),
        cost_estimate=cost(13),
        name="attn_fwd",
        main=True,
    )


def post_kernel(x, m0, m1, m2, rest, small, x1_o, n2_o, n2t_o, w):
    @pl.when(pl.program_id(0) == 0)
    def _():
        gathered_rows(w, (rest,), None, 0, 6, RB, 0)

    a = x[...].astype(f32) + small[4:5, :]
    for g, m in enumerate((m0, m1, m2)):
        a += dot(m[...], w[256 * g : 256 * g + 256, :], 1, 0)
    x1_o[...] = a
    c = a - jnp.mean(a, -1, keepdims=True)
    r = lax.rsqrt(jnp.mean(c * c, -1, keepdims=True) + 1e-06)
    n = (c * r * small[5:6, :] + small[6:7, :]).astype(bf16)
    n2_o[...] = n
    n2t_o[...] = n.T


def post_attn(x, mixes, rest, small):
    rows = pl.BlockSpec((B, D), lambda r: (r, 0))
    part = pl.BlockSpec((B, 256), lambda r: (r, 0))
    return call(
        post_kernel,
        [x, *mixes, rest, small],
        grid=(NB,),
        out_shape=[sds((T, D), f32), sds((T, D), bf16), sds((D, T), bf16)],
        in_specs=[rows, part, part, part, pl.BlockSpec((OWN, QR, 128), lambda r: (0, 3 * FR // QR, 0))]
        + [pl.BlockSpec((SR, D), lambda r: (0, 0))],
        out_specs=[rows, rows, pl.BlockSpec((D, B), lambda r: (0, r))],
        scratch_shapes=[pltpu.VMEM((D, D), bf16)],
        compiler_params=params(),
        cost_estimate=cost(6.5),
        name="post_attn",
        main=True,
    )


C0 = math.sqrt(2.0 / math.pi)
C1 = 0.044715


def ff_chunk(row, n2, dy, wu, wd, ub, dub, hid_o, ht, dp):
    size = n2.shape[0]
    rows = pl.ds(pl.multiple_of(row * size, size), size)
    for c in range(FC // FCOL):
        cols = slice(FCOL * c, FCOL * c + FCOL)
        pre = dot(n2, wu[:, cols], 1, 0) + ub[0:1, cols]
        dh = dot(dy, wd[cols, :], 1, 1)
        sq = pre * pre
        t = jnp.tanh(C0 * pre * (1.0 + C1 * sq))
        half = 0.5 + 0.5 * t
        hid = (pre * half).astype(bf16)
        slope = half + (0.5 * C0) * pre * (1.0 - t * t) * (1.0 + (3.0 * C1) * sq)
        dpre = dh * slope
        dub[0:8, cols] += fold(dpre)
        hid_o[:, cols] = hid
        ht[cols, rows] = hid.T
        dp[rows, cols] = dpre.astype(bf16)
    return dot(dp[rows, :], wu[...], 1, 1)


def ff_weights(rest, wu, wd):
    gathered_rows(wu, (rest,), None, 0, 8, RB, 0)
    gathered_rows(wd, (rest,), None, 8 * RB, 6, FB, 0)


def ff_bias(j, small, ub):
    for t in range(8):
        halves = []
        for d in (2 * t, 2 * t + 1):
            c = 192 * (d % 4) + FB * j
            halves.append(small[8 + d // 4 : 9 + d // 4, c : c + FB])
        ub[0:1, 128 * t : 128 * t + 128] = jnp.concatenate(halves, axis=1)


def ff_grads(grads, order, n2ts, dp, ht, dys, gu, gd):
    gu[...] = dot(n2ts[...], dp[...], 1, 0).astype(bf16)
    gd[...] = dot(ht[...], dys[...], 1, 0).astype(bf16)
    scattered_rows(gu, grads, order, 0, 8, RB, 0)
    scattered_rows(gd, grads, order, 8 * RB, 6, FB, 0)


FF_SCRATCH = [
    pltpu.VMEM((D, FC), bf16),
    pltpu.VMEM((FC, D), bf16),
    pltpu.VMEM((8, FC), f32),
    pltpu.VMEM((D, T), bf16),
    pltpu.VMEM((T, D), bf16),
    pltpu.VMEM((FC, T), bf16),
    pltpu.VMEM((T, FC), bf16),
    pltpu.VMEM((D, FC), bf16),
    pltpu.VMEM((FC, D), bf16),
]


def ff_two_kernel(n2, n2t, dy, rest, small, hid_o, acc_o, grads, dub,
                  wu, wd, ub, n2ts, dys, ht, dp, gu, gd, n2s, acc):
    j, row = pl.program_id(0), pl.program_id(1)
    rows = pl.ds(pl.multiple_of(row * FBLK, FBLK), FBLK)

    @pl.when(row == 0)
    def _():
        ff_weights(rest, wu, wd)
        dub[...] = jnp.zeros_like(dub)
        for n in range(2):
            pl.when(j == n)(functools.partial(ff_bias, n, small, ub))

    @pl.when(j == 0)
    def _():
        n2ts[:, rows] = n2t[...]
        dys[rows, :] = dy[...]
        n2s[rows, :] = n2[...]
        acc[rows, :] = jnp.zeros((FBLK, D), f32)

    dn = acc[rows, :] + ff_chunk(row, n2s[rows, :], dys[rows, :], wu, wd, ub, dub, hid_o, ht, dp)
    acc[rows, :] = dn
    acc_o[...] = dn

    @pl.when(row == FN - 1)
    def _():
        ff_grads((grads,), None, n2ts, dp, ht, dys, gu, gd)


def feed_forward_two(n2, n2t, dy, rest, small):
    first = lambda j, r: r + (FN - 1 - r) * j
    rows = pl.BlockSpec((FBLK, D), lambda j, r: (first(j, r), 0))
    return call(
        ff_two_kernel,
        [n2, n2t, dy, rest, small],
        grid=(2, FN),
        out_shape=[
            sds((T, 2 * FC), bf16),
            sds((T, D), f32),
            sds((OWN, 2 * FR, 128), bf16),
            sds((8, 2 * FC), f32),
        ],
        in_specs=[
            rows,
            pl.BlockSpec((D, FBLK), lambda j, r: (0, first(j, r))),
            rows,
            pl.BlockSpec((OWN, FR, 128), lambda j, r: (0, j, 0)),
            pl.BlockSpec((SR, D), lambda j, r: (0, 0)),
        ],
        out_specs=[
            pl.BlockSpec((FBLK, FC), lambda j, r: (r, j)),
            pl.BlockSpec((FBLK, D), lambda j, r: (r * j, 0)),
            pl.BlockSpec((OWN, FR, 128), lambda j, r: (0, j, 0)),
            pl.BlockSpec((8, FC), lambda j, r: (0, j)),
        ],
        scratch_shapes=FF_SCRATCH + [pltpu.VMEM((T, D), bf16), pltpu.VMEM((T, D), f32)],
        compiler_params=params(),
        cost_estimate=cost(28),
        name="feed_forward_two",
        main=True,
    )


def norm_back(v, up, gain):
    c = v - jnp.mean(v, -1, keepdims=True)
    r = lax.rsqrt(jnp.mean(c * c, -1, keepdims=True) + 1e-06)
    hat = c * r
    g = up * gain
    back = r * (g - jnp.mean(g, -1, keepdims=True) - hat * jnp.mean(g * hat, -1, keepdims=True))
    return back, up * hat


def ff_last_kernel(offs, n2, n2t, dy, rest, small, acc, x1, t0, t1, t2, rest_o,
                   hid_o, dub, dx1_o, dmix_o, keep, send, keep_o, send_o, sums,
                   wu, wd, ub, n2ts, dys, ht, dp, gu, gd, w, low, go):
    row = pl.program_id(0)
    rows = pl.ds(pl.multiple_of(row * B, B), B)

    @pl.when(row == 0)
    def _():
        ff_weights(rest, wu, wd)
        ff_bias(2, small, ub)
        gathered_rows(w, (rest_o,), None, 0, 6, RB, 0)
        dub[...] = jnp.zeros_like(dub)
        sums[...] = jnp.zeros_like(sums)

    n2ts[:, rows] = n2t[...]
    dys[rows, :] = dy[...]
    up = acc[...] + ff_chunk(row, n2[...], dy[...], wu, wd, ub, dub, hid_o, ht, dp)
    d = dy[...].astype(f32)
    back, hats = norm_back(x1[...], up, small[5:6, :])
    dx1 = d + back
    dx1_o[...] = dx1
    lowered = dx1.astype(bf16)
    low[rows, :] = lowered
    sums[0:8, :] += fold(dx1)
    sums[8:16, :] += fold(hats)
    sums[16:24, :] += fold(up)
    sums[24:32, :] += fold(d)
    dmix_o[...] = dot(lowered, w[...], 1, 1).astype(bf16)

    @pl.when(row == NB - 1)
    def _():
        ff_grads((keep, send), offs, n2ts, dp, ht, dys, gu, gd)
        for g, t in enumerate((t0, t1, t2)):
            go[256 * g : 256 * g + 256, :] = dot(t[...], low[...], 1, 0).astype(bf16)
        scattered_rows(go, (keep_o, send_o), offs, 0, 6, RB, 0)


def feed_forward_last(offs, n2, n2t, dy, rest, small, acc, x1, mixts):
    rows = pl.BlockSpec((B, D), lambda r: (r, 0))
    packed = pl.BlockSpec((8, FR, 128), lambda r: (0, 0, 0))
    packed_o = pl.BlockSpec((8, QR, 128), lambda r: (0, 0, 0))
    once = dict(pipeline_mode=pl.Buffered(1))
    return call(
        ff_last_kernel,
        [offs, n2, n2t, dy, rest, small, acc, x1, *mixts, rest],
        grid=(NB,),
        out_shape=[
            sds((T, FC), bf16),
            sds((8, FC), f32),
            sds((T, D), f32),
            sds((T, D), bf16),
            sds((8, FR, 128), bf16),
            sds((8, FR, 128), bf16),
            sds((8, QR, 128), bf16),
            sds((8, QR, 128), bf16),
            sds((32, D), f32),
        ],
        in_specs=[
            SM,
            rows,
            pl.BlockSpec((D, B), lambda r: (0, r)),
            rows,
            pl.BlockSpec((OWN, FR, 128), lambda r: (0, 2, 0), **once),
            pl.BlockSpec((SR, D), lambda r: (0, 0)),
            rows,
            rows,
        ]
        + [pl.BlockSpec((256, T), lambda r: (0, 0), **once)] * 3
        + [pl.BlockSpec((OWN, QR, 128), lambda r: (0, 3 * FR // QR, 0), **once)],
        out_specs=[
            pl.BlockSpec((B, FC), lambda r: (r, 0)),
            pl.BlockSpec((8, FC), lambda r: (0, 0)),
            rows,
            rows,
            packed,
            packed,
            packed_o,
            packed_o,
            pl.BlockSpec((32, D), lambda r: (0, 0)),
        ],
        scratch_shapes=FF_SCRATCH
        + [pltpu.VMEM((D, D), bf16), pltpu.VMEM((T, D), bf16), pltpu.VMEM((D, D), bf16)],
        compiler_params=params(),
        cost_estimate=cost(22),
        name="feed_forward_last",
        main=True,
    )


def attn_bwd_kernel(
    offs, q, k, v, do, mix, lse, n1t, segc, segr,
    dqkv_o, keep, send, sums, kn, vn, qt, dt, kt, qm, dm, dqt, gw,
):
    left, right = segment_tail(segc, segr, None)
    sub = lax.broadcasted_iota(jnp.int32, (16, T), 0)
    qs = q[...] * jnp.asarray(0.125, bf16)
    qtt = qs.T
    dtt = do[...].T
    kt[...] = k[...].T
    prod = (do[...].astype(f32) * mix[...].astype(f32)).T
    zero = jnp.zeros((64, T), bf16)
    pad = jnp.zeros((112, T), bf16)
    lane = lax.broadcasted_iota(jnp.int32, (T, 128), 1)
    nothing = jnp.zeros((T, 128), bf16)
    for p in range(2):
        at = slice(128 * p, 128 * p + 128)
        kn[p, :, :128] = k[:, at]
        kn[p, :, 128:] = left
        vn[p, :, :128] = v[:, at]
        vn[p, :, 128:] = left
        for e in range(2):
            h = 2 * p + e
            mine = (lane >= 64 * e) & (lane < 64 * e + 64)
            qm[p, e] = jnp.where(mine, qs[:, at], nothing)
            dm[p, e] = jnp.where(mine, do[:, at], nothing)
            for dst, src in ((qt, qtt), (dt, dtt)):
                dst[h, 64 * e : 64 * e + 64, :] = src[64 * h : 64 * h + 64]
                dst[h, 64 - 64 * e : 128 - 64 * e, :] = zero
                dst[h, 144:, :] = pad
            a, b, c = three(-lse[h : h + 1, :])
            tail = jnp.where(sub == 4, a, jnp.where(sub == 5, b, jnp.where(sub == 6, c, right)))
            qt[h, 128:144, :] = tail.astype(bf16)
            a, b, c = three(-rowsum(prod[64 * h : 64 * h + 64, :]))
            tail = jnp.where(sub == 4, a, jnp.where(sub == 5, b, jnp.where(sub == 6, c, 0.0)))
            dt[h, 128:144, :] = tail.astype(bf16)
    dqt[...] = jnp.zeros_like(dqt)
    for j in range(NB):
        keys = slice(j * B, (j + 1) * B)

        def step(i, carry):
            dks, dvs = carry
            cols = slice(i * B, (i + 1) * B)
            new_dk, new_dv = [], []
            for p in range(2):
                hs = (2 * p, 2 * p + 1)
                s2 = [dot(kn[p, keys, :], qt[h, :, cols], 1, 0) for h in hs]
                d2 = [dot(vn[p, keys, :], dt[h, :, cols], 1, 0) for h in hs]
                p2 = [jnp.exp(s) for s in s2]
                g2 = [(a * b).astype(bf16) for a, b in zip(p2, d2)]
                pr = jnp.concatenate([a.astype(bf16) for a in p2], axis=1)
                gr = jnp.concatenate(g2, axis=1)
                new_dv.append(dvs[p] + dot(pr, jnp.concatenate([dm[p, 0, cols, :], dm[p, 1, cols, :]], axis=0), 1, 0))
                new_dk.append(dks[p] + dot(gr, jnp.concatenate([qm[p, 0, cols, :], qm[p, 1, cols, :]], axis=0), 1, 0))
                for e in range(2):
                    h = 2 * p + e
                    dqt[64 * h : 64 * h + 64, cols] += dot(kt[64 * h : 64 * h + 64, keys], g2[e], 1, 0)
            return tuple(new_dk), tuple(new_dv)

        dks = dvs = tuple(jnp.zeros((B, 128), f32) for _ in range(2))
        for i in near(j):
            dks, dvs = step(i, (dks, dvs))
        for p in range(2):
            dqkv_o[keys, 256 + 128 * p : 384 + 128 * p] = dks[p].astype(bf16)
            dqkv_o[keys, 512 + 128 * p : 640 + 128 * p] = dvs[p].astype(bf16)
    dqkv_o[:, :256] = (dqt[...] * 0.125).astype(bf16).T
    sums[:, :256] = fold(dqkv_o[:, :256].astype(f32))
    sums[:, 256:] = fold(dqkv_o[:, 512:].astype(f32))
    gw[...] = dot(n1t[...], dqkv_o[...], 1, 0).astype(bf16)
    scattered_rows(gw, (keep, send), offs, 0, 6, RB, 0)


def attn_bwd(g, offs, q, k, v, dmix, mix, lse, n1t, segc, segr):
    whole = lambda a: pl.BlockSpec(a.shape, lambda r: (0,) * a.ndim)
    outs = [
        sds((T, D), bf16),
        sds((8, QR, 128), bf16),
        sds((8, QR, 128), bf16),
        sds((8, 512), f32),
    ]
    return call(
        attn_bwd_kernel,
        [offs, q, k, v, dmix, mix, lse, n1t, segc, segr],
        grid=(1,),
        out_shape=outs,
        in_specs=[SM, whole(q), whole(k), whole(v), pl.BlockSpec((T, 256), lambda r: (0, g))]
        + [whole(a) for a in (mix, lse, n1t, segc, segr)],
        out_specs=[whole(a) for a in outs],
        scratch_shapes=[
            pltpu.VMEM((2, T, 256), bf16),
            pltpu.VMEM((2, T, 256), bf16),
            pltpu.VMEM((4, 256, T), bf16),
            pltpu.VMEM((4, 256, T), bf16),
            pltpu.VMEM((256, T), bf16),
            pltpu.VMEM((2, 2, T, 128), bf16),
            pltpu.VMEM((2, 2, T, 128), bf16),
            pltpu.VMEM((256, T), f32),
            pltpu.VMEM((D, D), bf16),
        ],
        compiler_params=params(),
        cost_estimate=cost(21),
        name="attn_bwd",
        main=True,
    )


def last_kernel(offs, d0, d1, d2, w0, w1, w2, x, dx1, small, mids, s0, s1, s2, u0, u1,
                gt_o, keep, send, sums, sg):
    step = pl.program_id(0)

    @pl.when(step == 0)
    def _():
        sums[...] = jnp.zeros_like(sums)

    dn = dot(d0[...], w0[...], 1, 1) + dot(d1[...], w1[...], 1, 1) + dot(d2[...], w2[...], 1, 1)
    back, hats = norm_back(x[...].astype(f32), dn, small[0:1, :])
    gt_o[...] = (dx1[...] + back).astype(bf16)
    sums[0:8, :] += fold(hats)
    sums[8:16, :] += fold(dn)

    @pl.when(step == T // LB - 1)
    def _():
        total = lambda v: jnp.sum(v, axis=0, keepdims=True)
        sg[...] = jnp.zeros_like(sg)
        sg[0:1, :] = total(sums[0:8, :])
        sg[1:2, :] = total(sums[8:16, :])
        for g, s in enumerate((s0, s1, s2)):
            sg[2:3, 256 * g : 256 * g + 256] = total(s[:, :256])
            sg[3:4, 256 * g : 256 * g + 256] = total(s[:, 256:])
        for n in range(4):
            sg[4 + n : 5 + n, :] = total(mids[8 * n : 8 * n + 8, :])
        ups = [total(u0[:, :FC]), total(u0[:, FC:]), total(u1[...])]
        for n in range(4):
            parts = []
            for d in range(4 * n, 4 * n + 4):
                for j in range(3):
                    parts.append(ups[j][:, FB * d : FB * d + FB])
            sg[8 + n : 9 + n, :] = jnp.concatenate(parts, axis=1)
        low = sg[...].astype(bf16)
        row = lax.broadcasted_iota(jnp.int32, (D, 128), 0)
        col = lax.broadcasted_iota(jnp.int32, (D, 128), 1)
        for s in range(OWN):
            hot = jnp.where((row == col + offs[s] * RB) & (col < RB), 1.0, 0.0).astype(bf16)
            (keep, send)[s // 8][s % 8, :, :] = dot(low, hot, 1, 0).astype(bf16)


def last_norm(offs, dqkvs, ws, x, dx1, small, mids, ssums, usums):
    rows = pl.BlockSpec((LB, D), lambda r: (r, 0))
    whole = lambda a: pl.BlockSpec(a.shape, lambda r: (0,) * a.ndim)
    packed = pl.BlockSpec((8, SR, 128), lambda r: (0, 0, 0))
    return call(
        last_kernel,
        [offs, *dqkvs, *ws, x, dx1, small, mids, *ssums, *usums],
        grid=(T // LB,),
        out_shape=[sds((T, D), bf16), sds((8, SR, 128), bf16), sds((8, SR, 128), bf16)],
        in_specs=[SM] + [rows] * 3 + [whole(w) for w in ws] + [rows, rows]
        + [whole(a) for a in (small, mids, *ssums, *usums)],
        out_specs=[rows, packed, packed],
        scratch_shapes=[pltpu.VMEM((16, D), f32), pltpu.VMEM((SR, D), f32)],
        compiler_params=params(),
        cost_estimate=cost(10.5),
        name="last_norm",
        main=True,
    )


def out_kernel(h01, h2, r0, r1, r2, x1, small, o, wd):
    @pl.when(pl.program_id(0) == 0)
    def _():
        for j, ref in enumerate((r0, r1, r2)):
            gathered_rows(wd.at[FC * j : FC * j + FC], (ref,), None, 0, 6, FB, 0)

    a = x1[...] + small[7:8, :]
    a += dot(h01[...], wd[: 2 * FC, :], 1, 0) + dot(h2[...], wd[2 * FC :, :], 1, 0)
    o[...] = a.astype(bf16)


def layer_out(h01, h2, rest, x1, small):
    rows = pl.BlockSpec((B, D), lambda r: (r, 0))
    downs = [pl.BlockSpec((OWN, FR // 2, 128), lambda r, j=j: (0, 2 * j + 1, 0)) for j in range(3)]
    return call(
        out_kernel,
        [h01, h2, rest, rest, rest, x1, small],
        grid=(NB,),
        out_shape=sds((T, D), bf16),
        in_specs=[pl.BlockSpec((B, 2 * FC), lambda r: (r, 0)), pl.BlockSpec((B, FC), lambda r: (r, 0))]
        + downs
        + [rows, pl.BlockSpec((SR, D), lambda r: (0, 0))],
        out_specs=rows,
        scratch_shapes=[pltpu.VMEM((FF, D), bf16)],
        compiler_params=params(),
        cost_estimate=cost(10),
        name="layer_out",
        main=True,
    )


def adamw(weight, grad, mom_one, mom_two, rate):
    next_one = BETA1 * mom_one + (1.0 - BETA1) * grad
    next_two = BETA2 * mom_two + (1.0 - BETA2) * grad * grad
    fixed_one = next_one / (1.0 - BETA1**STEP)
    fixed_two = next_two / (1.0 - BETA2**STEP)
    updated = weight - rate * (fixed_one / (jnp.sqrt(fixed_two) + ADAM_EPS) + DECAY * weight)
    return (updated, next_one, next_two)


def whole_rows(offs, pair, at, dst):
    half = dst.shape[0] // 2
    for n, y in enumerate((offs[OWN], 1 - offs[OWN])):
        dst[pl.ds(pl.multiple_of(y * half, 16), half), :] = pair[n][at : at + half, :]


def update(outs, at, state, grad, rate):
    for o, val in zip(outs, adamw(state[0][at], grad, state[1][at], state[2][at], rate)):
        o[at] = val


def adam_out_kernel(offs, *refs):
    pair, out, out_o, pack = refs[:2], refs[2:5], refs[5:8], refs[8]
    whole_rows(offs, pair, FR // 2, pack)
    for t in range(6):
        grad = pack[t * RB : (t + 1) * RB, :].astype(f32)
        update(out_o, (slice(None), slice(128 * t, 128 * t + 128)), out, grad, RATES[1])


def adam_heads_kernel(offs, *refs):
    last, qkv, small = refs[:2], refs[2:5], refs[5:8]
    qkv_o, small_o, packs = refs[8:11], refs[11:14], refs[14:]
    for n in range(2):
        whole_rows(offs, last, n * QR // 2, packs[n])
    both = lambda r, n: last[0][QR + r : QR + r + n, :].astype(f32) + last[1][QR + r : QR + r + n, :].astype(f32)
    for g in range(3):
        for part in range(3):
            for t in range(2):
                c = D * part + 256 * g + 128 * t
                r = (2 * part + t) * RB
                grad = packs[g][r : r + RB, :].astype(f32) if g < 2 else both(r, RB)
                update(qkv_o, (slice(None), slice(c, c + 128)), qkv, grad, RATES[0])
    update(small_o, Ellipsis, small, both(QR, SR)[:12, :RB], RATES[4])


def adam_ff_kernel(offs, *refs):
    two, pair, up, down = refs[:2], refs[2:4], refs[4:7], refs[7:10]
    up_o, down_o = refs[10:13], refs[13:16]
    pack = refs[16]
    whole_rows(offs, pair, 0, pack)

    def total(j, r, n):
        if j == 2:
            return pack[r : r + n, :].astype(f32)
        rows = slice(FR * j + r, FR * j + r + n)
        return two[0][rows, :].astype(f32) + two[1][rows, :].astype(f32)

    for t in range(8):
        parts = [total(j, t * RB, RB) for j in range(3)]
        grad = jnp.concatenate([p[:, :64] for p in parts] + [p[:, 64:] for p in parts], axis=1)
        update(up_o, (slice(None), slice(384 * t, 384 * t + 384)), up, grad, RATES[2])
    for j in range(3):
        for t in range(6):
            at = (slice(FB * j, FB * j + FB), slice(128 * t, 128 * t + 128))
            update(down_o, at, down, total(j, 8 * RB + t * FB, FB), RATES[3])


def adam_call(kernel, offs, grads, states, scratch, name):
    shapes = [sds(s.shape, f32) for s in states]
    return call(
        kernel,
        [offs, *grads, *states],
        out_shape=shapes,
        in_specs=[SM] + [VM] * (len(grads) + len(states)),
        out_specs=[VM] * len(shapes),
        scratch_shapes=[pltpu.VMEM((r, 128), bf16) for r in scratch],
        compiler_params=params(),
        cost_estimate=cost(),
        name=name,
    )


def shifted(f):
    pairs = []
    for z in range(4):
        for x in range(2):
            for c in range(2):
                tz, tx, tc = f(z, x, c)
                pairs.append(((z * 2 + x) * 2 + c, (tz * 2 + tx) * 2 + tc))
    return pairs


TO_CORE = shifted(lambda z, x, c: (z, x, 1 - c))
TO_X = shifted(lambda z, x, c: (z, 1 - x, c))
TO_Z = [shifted(lambda z, x, c, s=s: ((z + s) % 4, x, c)) for s in range(4)]
FROM_Z = [shifted(lambda z, x, c, s=s: ((z - s) % 4, x, c)) for s in range(4)]
TO_Y = [(0, 1), (1, 0)]


def stack_kernel(a, b, c, d, *refs):
    out = refs[len(refs) // 2]
    for n, ref in enumerate((a, b, c, d)):
        out[n] = ref[...]


class Gather:
    def __init__(self, own):
        self.own = own

    def along_z(self):
        self.parts = [self.own] + [lax.ppermute(self.own, "dp", TO_Z[s]) for s in (1, 2, 3)]

    def along_x(self, *later):
        anywhere = pl.BlockSpec(memory_space=pl.ANY)
        outs = call(
            stack_kernel,
            [*self.parts, *[g.own for g in later]],
            out_shape=[sds((4,) + self.own.shape, bf16)] + [sds(g.own.shape, bf16) for g in later],
            in_specs=[VM] * 4 + [anywhere] * len(later),
            out_specs=[VM] + [anywhere] * len(later),
            input_output_aliases={4 + n: 1 + n for n in range(len(later))},
            compiler_params=params(),
            cost_estimate=cost(1.7),
            name="stack",
        )
        for g, own in zip(later, outs[1:]):
            g.own = own
        line = outs[0]
        self.pieces = [line, lax.ppermute(line, "dp", TO_X), lax.ppermute(line, "dp", TO_CORE)]

    def to_core(self, hold=False):
        if hold:
            self.pieces[1] = wait_here(self.pieces[1])[0]
        self.pieces.append(lax.ppermute(self.pieces[1], "dp", TO_CORE))


def add_core_kernel(*refs):
    half = len(refs) // 2 - 1
    a, b = refs[-2:]
    at = 0
    for keep, got in zip(refs[:half], refs[half : 2 * half]):
        rows = keep.shape[1]
        a[:, at : at + rows] = (keep[:4].astype(f32) + got[:4].astype(f32)).astype(bf16)
        b[:, at : at + rows] = (keep[4:].astype(f32) + got[4:].astype(f32)).astype(bf16)
        at += rows


def add_core_half_kernel(offs, *refs):
    n = len(refs) // 2 - 1
    outs = refs[-2:]
    at = 0
    for keep, got in zip(refs[:n], refs[n : 2 * n]):
        half = keep.shape[1] // 2
        for out, y in zip(outs, (offs[OWN], 1 - offs[OWN])):
            rows = pl.ds(pl.multiple_of(y * half, 16), half)
            out[:, at : at + half] = (keep[:, rows].astype(f32) + got[:, rows].astype(f32)).astype(bf16)
        at += half


def add_y_kernel(*refs):
    n = len(refs) // 2 - 1
    a, b = refs[-2:]
    at = 0
    for keep, got in zip(refs[:n], refs[n : 2 * n]):
        rows = keep.shape[2]
        total = (keep[...].astype(f32) + got[...].astype(f32)).astype(bf16)
        a[:, at : at + rows] = total[0]
        b[:, at : at + rows] = total[1]
        at += rows


def add_x_kernel(*refs):
    pairs, outs = refs[:-4], refs[-4:]
    at = 0
    for keep, got in zip(pairs[::2], pairs[1::2]):
        rows = keep.shape[1]
        for s in range(4):
            outs[s][at : at + rows, :] = (keep[s].astype(f32) + got[s].astype(f32)).astype(bf16)
        at += rows


def add_z_kernel(a, b, c, d, o):
    o[...] = (a[...].astype(f32) + b[...].astype(f32) + c[...].astype(f32) + d[...].astype(f32)).astype(bf16)


def add_call(kernel, args, outs, name, then, beside):
    if beside:
        SIDE.append((kernel, args, outs, then))
        return
    then(add_alone(kernel, args, outs, name))


def add_alone(kernel, args, outs, name):
    return call(
        kernel,
        args,
        out_shape=outs,
        in_specs=[VM] * len(args),
        out_specs=[VM] * len(outs),
        compiler_params=params(),
        cost_estimate=cost(),
        name=name,
    )


class Scatter:
    def __init__(self, *packs):
        self.keeps = [p[0] for p in packs]
        self.rows = sum(k.shape[1] for k in self.keeps)
        self.gots = [lax.ppermute(p[1], "dp", TO_CORE) for p in packs]

    def half_along_y(self, offs):
        self.rows //= 2
        args = (*self.keeps, *self.gots)
        block = lambda r: pl.BlockSpec((4, r, 128), lambda i: (i, 0, 0))
        mine, other = call(
            add_core_half_kernel,
            [offs, *args],
            grid=(2,),
            out_shape=[sds((8, self.rows, 128), bf16)] * 2,
            in_specs=[SM] + [block(a.shape[1]) for a in args],
            out_specs=[block(self.rows)] * 2,
            compiler_params=params(),
            cost_estimate=cost(),
            name="add_core_half",
        )
        self.halves = (mine, lax.ppermute(other, "rep", TO_Y))

    def sums_along_x(self):
        cut = lambda a: a.reshape(2, 4, a.shape[1], 128)
        args = [cut(half) for half in self.halves]
        self.mine, send = call(
            add_y_kernel,
            args,
            grid=(2,),
            out_shape=[sds((4, self.rows, 128), bf16)] * 2,
            in_specs=[pl.BlockSpec((2, 2, a.shape[2], 128), lambda i: (0, i, 0, 0)) for a in args],
            out_specs=[pl.BlockSpec((2, self.rows, 128), lambda i: (i, 0, 0))] * 2,
            compiler_params=params(),
            cost_estimate=cost(),
            name="add_y",
        )
        self.got = lax.ppermute(send, "dp", TO_X)

    def along_x(self, beside=False):
        outs = [sds((4, self.rows, 128), bf16)] * 2

        def then(out):
            self.mine = out[0]
            self.got = lax.ppermute(out[1], "dp", TO_X)

        add_call(add_core_kernel, (*self.keeps, *self.gots), outs, "add_core", then, beside)

    def along_z(self, *others):
        pairs = [a for s in (self, *others) for a in (s.mine, s.got)]
        self.rows += sum(s.rows for s in others)
        outs = [sds((self.rows, 128), bf16)] * 4

        def then(parts):
            self.parts = [parts[0]] + [lax.ppermute(parts[s], "dp", FROM_Z[s]) for s in (1, 2, 3)]

        add_call(add_x_kernel, pairs, outs, "add_x", then, False)

    def along_y(self, beside=False):
        def then(out):
            self.done = (out[0], lax.ppermute(out[0], "rep", TO_Y))

        add_call(add_z_kernel, self.parts, [sds((self.rows, 128), bf16)], "add_z", then, beside)


def gather_any(small, wq, wo, wu, wd):
    full = lambda w, axis: lax.all_gather(w.astype(bf16), "dp", axis=axis, tiled=True)
    small = full(small, 1)
    blocks = small.reshape(small.shape[0], OWN, RB).transpose(1, 0, 2)
    blocks = jnp.pad(blocks, ((0, 0), (0, SR - small.shape[0]), (0, 128 - RB)))
    q = full(wq, 0).reshape(OWN, RB, 3, 3, 2, 128).transpose(3, 0, 2, 4, 1, 5).reshape(3, OWN, QR, 128)
    o = full(wo, 0).reshape(OWN, RB, 6, 128).transpose(0, 2, 1, 3).reshape(OWN, QR, 128)
    u = full(wu, 0).reshape(OWN, RB, 8, 2, 3, FB).transpose(4, 0, 2, 1, 3, 5).reshape(3, OWN, 8 * RB, 128)
    d = full(wd, 0).reshape(OWN, 3, FB, 6, 128).transpose(1, 0, 3, 2, 4).reshape(3, OWN, 6 * FB, 128)
    f = jnp.concatenate([u, d], 2)
    cut = lambda a: tuple(a[4 * n : 4 * n + 4] for n in range(4))
    heads = [cut(jnp.concatenate(p, 1)) for p in ((q[0], blocks), (q[1], q[2]))]
    return heads, jnp.concatenate([f[0], f[1], f[2], o], 1)


def scatter_any(packs, grads):
    q0, q1, q2, o, s = [jnp.concatenate(p, 0) for p in packs]
    q = jnp.stack([q0, q1, q2]).reshape(3, OWN, 3, 2, RB, 128).transpose(1, 4, 2, 0, 3, 5)
    f = grads.reshape(OWN, 3, FR, 128)
    u = f[:, :, : 8 * RB].reshape(OWN, 3, 8, RB, 2, FB).transpose(0, 3, 2, 4, 1, 5)
    d = f[:, :, 8 * RB :].reshape(OWN, 3, 6, FB, 128).transpose(0, 1, 3, 2, 4)
    o = o.reshape(OWN, 6, RB, 128).transpose(0, 2, 1, 3)
    s = s[:, :12, :RB].transpose(1, 0, 2).reshape(12, D)
    flat = ((q.reshape(D, 3 * D), 0), (o.reshape(D, D), 0), (u.reshape(D, FF), 0), (d.reshape(FF, D), 0), (s, 1))
    out = []
    for g, axis in flat:
        g = lax.psum_scatter(g, "dp", scatter_dimension=axis, tiled=True)
        out.append(lax.psum(g, "rep").astype(f32))
    return out


def shards(tokens, segment_ids, cotangent, *state, wide):
    masters, firsts, seconds = state[:5], state[5:10], state[10:15]
    w_qkv, w_out, w_up, w_down, small_params = masters
    x = tokens[0]
    dy = cotangent[0]
    seg = segment_ids[0]
    segc = seg.reshape(T, 1)
    segr = seg.reshape(1, T)
    ORDER.clear()
    if wide:
        me = lax.axis_index("dp")
        s = jnp.arange(OWN, dtype=jnp.int32)
        z = (me // 4 - s % 4) % 4
        xx = (me // 2 % 2) ^ (s // 4 % 2)
        cc = (me % 2) ^ (s // 8)
        offs = jnp.append((z * 2 + xx) * 2 + cc, lax.axis_index("rep")).astype(jnp.int32)
        (own_rest,) = pack(pack_rest_kernel, (w_out, w_up, w_down), (3 * FR + QR,), "pack_rest")
        rest = lax.all_gather(own_rest, "dp", axis=0, tiled=True).reshape(OWN, 3 * FR + QR, 128)
        owns = pack(pack_heads_kernel, (small_params, w_qkv), (QR + SR, 2 * QR, 16), "pack_heads")
        lines = [Gather(own) for own in owns[:2]]
        lines[0].along_z()
        lines[0].along_x(lines[1])
        lines[0].to_core()
        lines[1].along_z()
        heads = [lines[0].pieces, None]
    else:
        offs = jnp.arange(OWN, dtype=jnp.int32)
        heads, rest = gather_any(small_params, w_qkv, w_out, w_up, w_down)

    n1, n1t, small = norm_first(offs, x, heads[0], QR)
    fwd = []
    if wide:
        lines[1].along_x()
        heads[1] = lines[1].pieces
    for g in range(3):
        fwd.append(attn_fwd(g, offs, n1, heads[min(g, 1)], small, segc, segr))
        if wide and g == 0:
            lines[1].to_core(hold=True)
    x1, n2, n2t = post_attn(x, [f[3] for f in fwd], rest, small)
    sent = []

    def send(*packs):
        if wide:
            sent.append(Scatter(*packs))

    h01, acc, grads, u01 = feed_forward_two(n2, n2t, dy, rest, small)
    if wide:
        own_ff = lax.psum_scatter(grads.reshape(-1, 128), "dp", scatter_dimension=0, tiled=True)
    h2, u2, dx1, dmix, *grad, keep_o, send_o, mids = feed_forward_last(
        offs, n2, n2t, dy, rest, small, acc, x1, [f[4] for f in fwd]
    )
    send(grad, (keep_o, send_o))
    states = [(masters[n], firsts[n], seconds[n]) for n in range(5)]
    new = [None] * 5
    bwd = []
    for g in range(3):
        q, k, v, mix, _, lse, _ = fwd[g]
        bwd.append(attn_bwd(g, offs, q, k, v, dmix, mix, lse, n1t, segc, segr))
        if g == 0 and wide:
            sent[0].half_along_y(offs)
        if g == 1 and wide:
            send(bwd[0][1:3], bwd[1][1:3])
            sent[1].half_along_y(offs)
            sent[0].sums_along_x()
    if wide:
        sent[0].along_z()
        sent[1].sums_along_x()
        (own_ff,) = wait_here(own_ff)
        pair = (own_ff, lax.ppermute(own_ff, "rep", TO_Y))
    grad_tokens, keep_s, send_s = last_norm(
        offs, [b[0] for b in bwd], [f[6] for f in fwd], x, dx1, small, mids,
        [b[3] for b in bwd], [u01, u2],
    )
    if wide:
        send(bwd[2][1:3], (keep_s, send_s))
        ORDER.append(pair[1])
        sent[0].along_y()
        ORDER.append(sent[1].got)
        sent[2].along_x()
        both = adam_call(adam_ff_kernel, offs, (*pair, *sent[0].done), states[2] + states[3], (FR,), "adam_ff")
        new[2], new[3] = both[:3], both[3:]
        sent[1].along_z(sent[2])
    result = layer_out(h01, h2, rest, x1, small)
    if wide:
        sent[1].along_y()
        new[1] = adam_call(adam_out_kernel, offs, sent[0].done, states[1], (QR,), "adam_out")
        both = adam_call(adam_heads_kernel, offs, sent[1].done, states[0] + states[4], (QR, QR), "adam_heads")
        new[0], new[4] = both[:3], both[3:]
    else:
        packs = [(b[1], b[2]) for b in bwd] + [(keep_o, send_o), (keep_s, send_s)]
        owned = scatter_any(packs, jnp.concatenate([grads, jnp.concatenate(grad, 0)], 1))
        new = [adamw(states[n][0], owned[n], states[n][1], states[n][2], RATES[n]) for n in range(5)]
    return (
        result[None],
        grad_tokens[None],
        *[n[0] for n in new],
        *[n[1] for n in new],
        *[n[2] for n in new],
    )


def solution(mesh):
    rows = P("dp", None)
    small = P(None, "dp")
    state = (rows, rows, rows, rows, small)
    seqs = P(("dp", "rep"), None, None)
    return jax.shard_map(
        functools.partial(shards, wide=mesh.shape["dp"] == 16 and mesh.shape["rep"] == 2),
        mesh=mesh,
        in_specs=(seqs, P(("dp", "rep"), None), seqs) + state * 3,
        out_specs=(seqs, seqs) + state * 3,
        check_vma=False,
    )
```

```python
import functools
import math

import jax
import jax.numpy as jnp
from jax import lax
from jax.experimental import pallas as pl
from jax.experimental.pallas import tpu as pltpu
from jax.sharding import PartitionSpec as P

HEADS = 12
STEP = 10
BETA1 = 0.5
BETA2 = 0.5
ADAM_EPS = 1e-08
DECAY = 0.05
RATES = (0.04, 0.15, 0.04, 0.02, 0.3)

bf16 = jnp.bfloat16
f32 = jnp.float32

T = 1024
D = 768
FF = 3072
OWN = 16
RB = D // OWN
FB = FF // OWN // 3
FC = FF // 3
QR = 6 * RB
FR = 8 * RB + 6 * FB
SR = 16
B = 256
NB = T // B
LB = 256
LONGEST = 512
FBLK = 1024
FN = T // FBLK
FCOL = 256
MASK = 2.0**30
VMEM_LIMIT = 56 << 20

VM = pl.BlockSpec(memory_space=pltpu.VMEM)
SM = pl.BlockSpec(memory_space=pltpu.SMEM)


def params(**kw):
    return pltpu.CompilerParams(vmem_limit_bytes=VMEM_LIMIT, **kw)


ORDER = []
SIDE = []


def call(kernel, args, *, in_specs, out_specs, out_shape, main=False, token=None, **kw):
    side = list(SIDE) if main else []
    if main:
        SIDE.clear()
    extra = list(ORDER)
    single = not isinstance(out_shape, (list, tuple))
    shapes = [out_shape] if single else list(out_shape)
    specs = [out_specs] if single else list(out_specs)
    n, m = len(args), len(shapes)
    side_args = [a for _, more, _, _ in side for a in more]
    side_outs = [o for _, _, outs, _ in side for o in outs]
    grid = "grid" in kw
    whole = lambda a: pl.BlockSpec(a.shape, lambda r, k=len(a.shape): (0,) * k) if grid else VM

    def body(*refs):
        ins = refs[n : n + len(side_args)]
        rest = refs[n + len(side_args) + len(extra) :]
        outs = rest[m : m + len(side_outs)]

        def beside():
            i = o = 0
            for fn, more, results, _ in side:
                fn(*ins[i : i + len(more)], *outs[o : o + len(results)])
                i += len(more)
                o += len(results)

        if side:
            if grid:
                pl.when(pl.program_id(0) == 0)(beside)
            else:
                beside()
        return kernel(*refs[:n], *rest[:m], *rest[m + len(side_outs) :])

    out = pl.pallas_call(
        body,
        in_specs=list(in_specs)
        + [whole(a) for a in side_args]
        + [pl.BlockSpec(memory_space=pl.ANY)] * len(extra),
        out_specs=specs + [whole(a) for a in side_outs],
        out_shape=shapes + side_outs,
        **kw,
    )(*args, *side_args, *extra)
    out = list(out)
    ORDER[:] = [min(out[:m], key=lambda a: a.size) if token is None else out[token]]
    at = m
    for _, _, results, then in side:
        then(out[at : at + len(results)])
        at += len(results)
    return out[0] if single else out[:m]


def wait_here(*arrays):
    anywhere = pl.BlockSpec(memory_space=pl.ANY)
    order = list(ORDER)
    out = call(
        lambda *refs: None,
        arrays,
        out_shape=[sds(a.shape, a.dtype) for a in arrays],
        in_specs=[anywhere] * len(arrays),
        out_specs=[anywhere] * len(arrays),
        input_output_aliases={n: n for n in range(len(arrays))},
        name="wait_here",
    )
    ORDER[:] = order
    return out


def sds(shape, dtype):
    return jax.ShapeDtypeStruct(shape, dtype)


PACE = 0.7


def cost(us=3.0):
    return pl.CostEstimate(flops=int(us * PACE * 1e9), bytes_accessed=1, transcendentals=0)


def dot(a, b, ca, cb):
    return lax.dot_general(a, b, (((ca,), (cb,)), ((), ())), preferred_element_type=f32)


def fold(v):
    return jnp.sum(v.reshape(v.shape[0] // 8, 8, v.shape[1]), axis=0)


def rowsum(v):
    return jnp.sum(fold(v), axis=0, keepdims=True)


def gathered_rows(dst, refs, offs, base, tiles, rows, col):
    per = OWN // len(refs)
    for s in range(OWN):
        ref, at = refs[s // per], s % per
        off = s * rows if offs is None else pl.multiple_of(offs[s] * rows, 16)
        for t in range(tiles):
            dst[pl.ds(off, rows), col + 128 * t : col + 128 * t + 128] = ref[
                at, base + t * rows : base + (t + 1) * rows, :
            ]


def scattered_rows(src, outs, offs, base, tiles, rows, col):
    per = OWN // len(outs)
    for s in range(OWN):
        ref, at = outs[s // per], s % per
        off = s * rows if offs is None else pl.multiple_of(offs[s] * rows, 16)
        for t in range(tiles):
            ref[at, base + t * rows : base + (t + 1) * rows, :] = src[
                pl.ds(off, rows), col + 128 * t : col + 128 * t + 128
            ]


def pack_heads(dst, at, wq, g):
    for part in range(3):
        for t in range(2):
            c = D * part + 256 * g + 128 * t
            r = at + (2 * part + t) * RB
            dst[r : r + RB, :] = wq[:, c : c + 128].astype(bf16)


def pack_rest_kernel(wo, wu, wd, rest):
    for j in range(3):
        for t in range(8):
            r = FR * j + t * RB
            a = wu[:, 384 * t + 64 * j : 384 * t + 64 * j + 64]
            b = wu[:, 384 * t + 192 + 64 * j : 384 * t + 192 + 64 * j + 64]
            rest[r : r + RB, :] = jnp.concatenate([a, b], axis=1).astype(bf16)
        for t in range(6):
            r = FR * j + 8 * RB + t * FB
            rest[r : r + FB, :] = wd[FB * j : FB * j + FB, 128 * t : 128 * t + 128].astype(bf16)
    for t in range(6):
        r = 3 * FR + t * RB
        rest[r : r + RB, :] = wo[:, 128 * t : 128 * t + 128].astype(bf16)


def pack_heads_kernel(small, wq, q0, q12, token):
    token[...] = jnp.zeros_like(token)
    pack_heads(q0, 0, wq, 0)
    q0[QR : QR + SR, :] = jnp.zeros((SR, 128), bf16)
    q0[QR : QR + 12, :RB] = small[...].astype(bf16)
    pack_heads(q12, 0, wq, 1)
    pack_heads(q12, QR, wq, 2)


def pack(kernel, args, rows, name):
    return call(
        kernel,
        args,
        out_shape=[sds((r, 128), bf16) for r in rows],
        in_specs=[VM] * len(args),
        out_specs=[VM] * len(rows),
        compiler_params=params(),
        cost_estimate=cost(1.5),
        name=name,
    )


def norm_kernel(offs, x, p0, p1, p2, p3, n1, n1t, small, *, base):
    @pl.when(pl.program_id(0) == 0)
    def _():
        acc = jnp.zeros((SR, D), f32)
        row = lax.broadcasted_iota(jnp.int32, (128, D), 0)
        col = lax.broadcasted_iota(jnp.int32, (128, D), 1)
        for s in range(OWN):
            ref = (p0, p1, p2, p3)[s // 4]
            hot = jnp.where((col == row + offs[s] * RB) & (row < RB), 1.0, 0.0).astype(bf16)
            acc += dot(ref[s % 4, base : base + SR, :], hot, 1, 0)
        small[...] = acc

    v = x[...].astype(f32)
    c = v - jnp.mean(v, -1, keepdims=True)
    r = lax.rsqrt(jnp.mean(c * c, -1, keepdims=True) + 1e-06)
    n = (c * r * small[0:1, :] + small[1:2, :]).astype(bf16)
    n1[...] = n
    n1t[...] = n.T


def norm_first(offs, x, pieces, base):
    whole = [pl.BlockSpec(p.shape, lambda r: (0, 0, 0)) for p in pieces]
    return call(
        functools.partial(norm_kernel, base=base),
        [offs, x, *pieces],
        grid=(NB,),
        out_shape=[sds((T, D), bf16), sds((D, T), bf16), sds((SR, D), f32)],
        in_specs=[SM, pl.BlockSpec((B, D), lambda r: (r, 0))] + whole,
        out_specs=[
            pl.BlockSpec((B, D), lambda r: (r, 0)),
            pl.BlockSpec((D, B), lambda r: (0, r)),
            pl.BlockSpec((SR, D), lambda r: (0, 0)),
        ],
        compiler_params=params(),
        cost_estimate=cost(5),
        name="norm_first",
    )


def segment_tail(segc, segr, minus):
    lane = lax.broadcasted_iota(jnp.int32, (T, 128), 1)
    left = jnp.where((segc[...] == lane) | ((lane >= 4) & (lane < 7)), 1.0, 0.0).astype(bf16)
    sub = lax.broadcasted_iota(jnp.int32, (16, T), 0)
    right = jnp.where((segr[...] != sub) & (sub < 4), -MASK, 0.0)
    return left, right


def near(i):
    return [j for j in range(NB) if (abs(i - j) - 1) * B + 1 < LONGEST]


def three(v):
    hi = v.astype(bf16).astype(f32)
    rest = v - hi
    mid = rest.astype(bf16).astype(f32)
    return hi, mid, rest - mid


def attn_fwd_kernel(
    offs, n1, p0, p1, p2, p3, small, segc, segr,
    q_o, k_o, v_o, mix_o, mixt_o, lse_o, w_o, kn, qt, vt, s_s, *, g,
):
    gathered_rows(w_o, (p0, p1, p2, p3), offs, QR if g == 2 else 0, 6, RB, 0)
    qb = small[2:3, 256 * g : 256 * g + 256]
    vb = small[3:4, 256 * g : 256 * g + 256]
    q = (dot(n1[...], w_o[:, :256], 1, 0) + qb).astype(bf16)
    k = dot(n1[...], w_o[:, 256:512], 1, 0).astype(bf16)
    v = (dot(n1[...], w_o[:, 512:], 1, 0) + vb).astype(bf16)
    q_o[...] = q
    k_o[...] = k
    v_o[...] = v
    left, right = segment_tail(segc, segr, None)
    right = right.astype(bf16)
    qtt = (q * jnp.asarray(0.125, bf16)).T
    zero = jnp.zeros((64, T), bf16)
    pad = jnp.zeros((112, T), bf16)
    for p in range(2):
        kn[p, :, :128] = k[:, 128 * p : 128 * p + 128]
        kn[p, :, 128:] = left
        for e in range(2):
            h = 2 * p + e
            qt[h, 64 * e : 64 * e + 64, :] = qtt[64 * h : 64 * h + 64]
            qt[h, 64 - 64 * e : 128 - 64 * e, :] = zero
            qt[h, 128:144, :] = right
            qt[h, 144:, :] = pad
    vt[...] = v.T
    for i in range(NB):
        cols = slice(i * B, (i + 1) * B)
        tops, sums, accs = [], [], []
        for h in range(4):
            top = None
            for j in near(i):
                r = slice(j * B, (j + 1) * B)
                s = dot(kn[h // 2, r, :], qt[h, :, cols], 1, 0)
                s_s[h, r, :] = s
                most = jnp.max(s.reshape(B // 8, 8, B), axis=0)
                top = most if top is None else jnp.maximum(top, most)
            tops.append(jnp.max(top, axis=0, keepdims=True))
            part, acc = jnp.zeros((8, B), f32), jnp.zeros((64, B), f32)
            for j in near(i):
                r = slice(j * B, (j + 1) * B)
                e = jnp.exp(s_s[h, r, :] - tops[h])
                part += fold(e)
                acc += dot(vt[64 * h : 64 * h + 64, r], e.astype(bf16), 1, 0)
            sums.append(part)
            accs.append(acc)
        for h in range(4):
            total = jnp.sum(sums[h], axis=0, keepdims=True)
            mixt_o[64 * h : 64 * h + 64, cols] = (accs[h] / total).astype(bf16)
            lse_o[h : h + 1, cols] = tops[h] + jnp.log(total)
    mix_o[...] = mixt_o[...].T


def attn_fwd(g, offs, n1, pieces, small, segc, segr):
    return call(
        functools.partial(attn_fwd_kernel, g=g),
        [offs, n1, *pieces, small, segc, segr],
        out_shape=[sds((T, 256), bf16)] * 4
        + [sds((256, T), bf16), sds((4, T), f32), sds((D, D), bf16)],
        in_specs=[SM] + [VM] * 8,
        out_specs=[VM] * 7,
        scratch_shapes=[
            pltpu.VMEM((2, T, 256), bf16),
            pltpu.VMEM((4, 256, T), bf16),
            pltpu.VMEM((256, T), bf16),
            pltpu.VMEM((4, T, B), f32),
        ],
        compiler_params=params(),
        cost_estimate=cost(13),
        name="attn_fwd",
        main=True,
    )


def post_kernel(x, m0, m1, m2, rest, small, x1_o, n2_o, n2t_o, w):
    @pl.when(pl.program_id(0) == 0)
    def _():
        gathered_rows(w, (rest,), None, 0, 6, RB, 0)

    a = x[...].astype(f32) + small[4:5, :]
    for g, m in enumerate((m0, m1, m2)):
        a += dot(m[...], w[256 * g : 256 * g + 256, :], 1, 0)
    x1_o[...] = a
    c = a - jnp.mean(a, -1, keepdims=True)
    r = lax.rsqrt(jnp.mean(c * c, -1, keepdims=True) + 1e-06)
    n = (c * r * small[5:6, :] + small[6:7, :]).astype(bf16)
    n2_o[...] = n
    n2t_o[...] = n.T


def post_attn(x, mixes, rest, small):
    rows = pl.BlockSpec((B, D), lambda r: (r, 0))
    part = pl.BlockSpec((B, 256), lambda r: (r, 0))
    return call(
        post_kernel,
        [x, *mixes, rest, small],
        grid=(NB,),
        out_shape=[sds((T, D), f32), sds((T, D), bf16), sds((D, T), bf16)],
        in_specs=[rows, part, part, part, pl.BlockSpec((OWN, QR, 128), lambda r: (0, 3 * FR // QR, 0))]
        + [pl.BlockSpec((SR, D), lambda r: (0, 0))],
        out_specs=[rows, rows, pl.BlockSpec((D, B), lambda r: (0, r))],
        scratch_shapes=[pltpu.VMEM((D, D), bf16)],
        compiler_params=params(),
        cost_estimate=cost(6.5),
        name="post_attn",
        main=True,
    )


C0 = math.sqrt(2.0 / math.pi)
C1 = 0.044715


def ff_chunk(row, n2, dy, wu, wd, ub, dub, hid_o, ht, dp):
    size = n2.shape[0]
    rows = pl.ds(pl.multiple_of(row * size, size), size)
    for c in range(FC // FCOL):
        cols = slice(FCOL * c, FCOL * c + FCOL)
        pre = dot(n2, wu[:, cols], 1, 0) + ub[0:1, cols]
        dh = dot(dy, wd[cols, :], 1, 1)
        sq = pre * pre
        t = jnp.tanh(C0 * pre * (1.0 + C1 * sq))
        half = 0.5 + 0.5 * t
        hid = (pre * half).astype(bf16)
        slope = half + (0.5 * C0) * pre * (1.0 - t * t) * (1.0 + (3.0 * C1) * sq)
        dpre = dh * slope
        dub[0:8, cols] += fold(dpre)
        hid_o[:, cols] = hid
        ht[cols, rows] = hid.T
        dp[rows, cols] = dpre.astype(bf16)
    return dot(dp[rows, :], wu[...], 1, 1)


def ff_weights(rest, wu, wd):
    gathered_rows(wu, (rest,), None, 0, 8, RB, 0)
    gathered_rows(wd, (rest,), None, 8 * RB, 6, FB, 0)


def ff_bias(j, small, ub):
    for t in range(8):
        halves = []
        for d in (2 * t, 2 * t + 1):
            c = 192 * (d % 4) + FB * j
            halves.append(small[8 + d // 4 : 9 + d // 4, c : c + FB])
        ub[0:1, 128 * t : 128 * t + 128] = jnp.concatenate(halves, axis=1)


def ff_grads(grads, order, n2ts, dp, ht, dys, gu, gd):
    gu[...] = dot(n2ts[...], dp[...], 1, 0).astype(bf16)
    gd[...] = dot(ht[...], dys[...], 1, 0).astype(bf16)
    scattered_rows(gu, grads, order, 0, 8, RB, 0)
    scattered_rows(gd, grads, order, 8 * RB, 6, FB, 0)


FF_SCRATCH = [
    pltpu.VMEM((D, FC), bf16),
    pltpu.VMEM((FC, D), bf16),
    pltpu.VMEM((8, FC), f32),
    pltpu.VMEM((D, T), bf16),
    pltpu.VMEM((T, D), bf16),
    pltpu.VMEM((FC, T), bf16),
    pltpu.VMEM((T, FC), bf16),
    pltpu.VMEM((D, FC), bf16),
    pltpu.VMEM((FC, D), bf16),
]


def ff_two_kernel(n2, n2t, dy, rest, small, hid_o, acc_o, grads, dub,
                  wu, wd, ub, n2ts, dys, ht, dp, gu, gd, n2s, acc):
    j, row = pl.program_id(0), pl.program_id(1)
    rows = pl.ds(pl.multiple_of(row * FBLK, FBLK), FBLK)

    @pl.when(row == 0)
    def _():
        ff_weights(rest, wu, wd)
        dub[...] = jnp.zeros_like(dub)
        for n in range(2):
            pl.when(j == n)(functools.partial(ff_bias, n, small, ub))

    @pl.when(j == 0)
    def _():
        n2ts[:, rows] = n2t[...]
        dys[rows, :] = dy[...]
        n2s[rows, :] = n2[...]
        acc[rows, :] = jnp.zeros((FBLK, D), f32)

    dn = acc[rows, :] + ff_chunk(row, n2s[rows, :], dys[rows, :], wu, wd, ub, dub, hid_o, ht, dp)
    acc[rows, :] = dn
    acc_o[...] = dn

    @pl.when(row == FN - 1)
    def _():
        ff_grads((grads,), None, n2ts, dp, ht, dys, gu, gd)


def feed_forward_two(n2, n2t, dy, rest, small):
    first = lambda j, r: r + (FN - 1 - r) * j
    rows = pl.BlockSpec((FBLK, D), lambda j, r: (first(j, r), 0))
    return call(
        ff_two_kernel,
        [n2, n2t, dy, rest, small],
        grid=(2, FN),
        out_shape=[
            sds((T, 2 * FC), bf16),
            sds((T, D), f32),
            sds((OWN, 2 * FR, 128), bf16),
            sds((8, 2 * FC), f32),
        ],
        in_specs=[
            rows,
            pl.BlockSpec((D, FBLK), lambda j, r: (0, first(j, r))),
            rows,
            pl.BlockSpec((OWN, FR, 128), lambda j, r: (0, j, 0)),
            pl.BlockSpec((SR, D), lambda j, r: (0, 0)),
        ],
        out_specs=[
            pl.BlockSpec((FBLK, FC), lambda j, r: (r, j)),
            pl.BlockSpec((FBLK, D), lambda j, r: (r * j, 0)),
            pl.BlockSpec((OWN, FR, 128), lambda j, r: (0, j, 0)),
            pl.BlockSpec((8, FC), lambda j, r: (0, j)),
        ],
        scratch_shapes=FF_SCRATCH + [pltpu.VMEM((T, D), bf16), pltpu.VMEM((T, D), f32)],
        compiler_params=params(),
        cost_estimate=cost(28),
        name="feed_forward_two",
        main=True,
    )


def norm_back(v, up, gain):
    c = v - jnp.mean(v, -1, keepdims=True)
    r = lax.rsqrt(jnp.mean(c * c, -1, keepdims=True) + 1e-06)
    hat = c * r
    g = up * gain
    back = r * (g - jnp.mean(g, -1, keepdims=True) - hat * jnp.mean(g * hat, -1, keepdims=True))
    return back, up * hat


def ff_last_kernel(offs, n2, n2t, dy, rest, small, acc, x1, t0, t1, t2, rest_o,
                   hid_o, dub, dx1_o, dmix_o, keep, send, keep_o, send_o, sums,
                   wu, wd, ub, n2ts, dys, ht, dp, gu, gd, w, low, go):
    row = pl.program_id(0)
    rows = pl.ds(pl.multiple_of(row * B, B), B)

    @pl.when(row == 0)
    def _():
        ff_weights(rest, wu, wd)
        ff_bias(2, small, ub)
        gathered_rows(w, (rest_o,), None, 0, 6, RB, 0)
        dub[...] = jnp.zeros_like(dub)
        sums[...] = jnp.zeros_like(sums)

    n2ts[:, rows] = n2t[...]
    dys[rows, :] = dy[...]
    up = acc[...] + ff_chunk(row, n2[...], dy[...], wu, wd, ub, dub, hid_o, ht, dp)
    d = dy[...].astype(f32)
    back, hats = norm_back(x1[...], up, small[5:6, :])
    dx1 = d + back
    dx1_o[...] = dx1
    lowered = dx1.astype(bf16)
    low[rows, :] = lowered
    sums[0:8, :] += fold(dx1)
    sums[8:16, :] += fold(hats)
    sums[16:24, :] += fold(up)
    sums[24:32, :] += fold(d)
    dmix_o[...] = dot(lowered, w[...], 1, 1).astype(bf16)

    @pl.when(row == NB - 1)
    def _():
        ff_grads((keep, send), offs, n2ts, dp, ht, dys, gu, gd)
        for g, t in enumerate((t0, t1, t2)):
            go[256 * g : 256 * g + 256, :] = dot(t[...], low[...], 1, 0).astype(bf16)
        scattered_rows(go, (keep_o, send_o), offs, 0, 6, RB, 0)


def feed_forward_last(offs, n2, n2t, dy, rest, small, acc, x1, mixts):
    rows = pl.BlockSpec((B, D), lambda r: (r, 0))
    packed = pl.BlockSpec((8, FR, 128), lambda r: (0, 0, 0))
    packed_o = pl.BlockSpec((8, QR, 128), lambda r: (0, 0, 0))
    once = dict(pipeline_mode=pl.Buffered(1))
    return call(
        ff_last_kernel,
        [offs, n2, n2t, dy, rest, small, acc, x1, *mixts, rest],
        grid=(NB,),
        out_shape=[
            sds((T, FC), bf16),
            sds((8, FC), f32),
            sds((T, D), f32),
            sds((T, D), bf16),
            sds((8, FR, 128), bf16),
            sds((8, FR, 128), bf16),
            sds((8, QR, 128), bf16),
            sds((8, QR, 128), bf16),
            sds((32, D), f32),
        ],
        in_specs=[
            SM,
            rows,
            pl.BlockSpec((D, B), lambda r: (0, r)),
            rows,
            pl.BlockSpec((OWN, FR, 128), lambda r: (0, 2, 0), **once),
            pl.BlockSpec((SR, D), lambda r: (0, 0)),
            rows,
            rows,
        ]
        + [pl.BlockSpec((256, T), lambda r: (0, 0), **once)] * 3
        + [pl.BlockSpec((OWN, QR, 128), lambda r: (0, 3 * FR // QR, 0), **once)],
        out_specs=[
            pl.BlockSpec((B, FC), lambda r: (r, 0)),
            pl.BlockSpec((8, FC), lambda r: (0, 0)),
            rows,
            rows,
            packed,
            packed,
            packed_o,
            packed_o,
            pl.BlockSpec((32, D), lambda r: (0, 0)),
        ],
        scratch_shapes=FF_SCRATCH
        + [pltpu.VMEM((D, D), bf16), pltpu.VMEM((T, D), bf16), pltpu.VMEM((D, D), bf16)],
        compiler_params=params(),
        cost_estimate=cost(22),
        name="feed_forward_last",
        main=True,
    )


def attn_bwd_kernel(
    offs, q, k, v, do, mix, lse, n1t, segc, segr,
    dqkv_o, keep, send, sums, kn, vn, qt, dt, kt, qm, dm, dqt, gw,
):
    left, right = segment_tail(segc, segr, None)
    sub = lax.broadcasted_iota(jnp.int32, (16, T), 0)
    qs = q[...] * jnp.asarray(0.125, bf16)
    qtt = qs.T
    dtt = do[...].T
    kt[...] = k[...].T
    prod = (do[...].astype(f32) * mix[...].astype(f32)).T
    zero = jnp.zeros((64, T), bf16)
    pad = jnp.zeros((112, T), bf16)
    lane = lax.broadcasted_iota(jnp.int32, (T, 128), 1)
    nothing = jnp.zeros((T, 128), bf16)
    for p in range(2):
        at = slice(128 * p, 128 * p + 128)
        kn[p, :, :128] = k[:, at]
        kn[p, :, 128:] = left
        vn[p, :, :128] = v[:, at]
        vn[p, :, 128:] = left
        for e in range(2):
            h = 2 * p + e
            mine = (lane >= 64 * e) & (lane < 64 * e + 64)
            qm[p, e] = jnp.where(mine, qs[:, at], nothing)
            dm[p, e] = jnp.where(mine, do[:, at], nothing)
            for dst, src in ((qt, qtt), (dt, dtt)):
                dst[h, 64 * e : 64 * e + 64, :] = src[64 * h : 64 * h + 64]
                dst[h, 64 - 64 * e : 128 - 64 * e, :] = zero
                dst[h, 144:, :] = pad
            a, b, c = three(-lse[h : h + 1, :])
            tail = jnp.where(sub == 4, a, jnp.where(sub == 5, b, jnp.where(sub == 6, c, right)))
            qt[h, 128:144, :] = tail.astype(bf16)
            a, b, c = three(-rowsum(prod[64 * h : 64 * h + 64, :]))
            tail = jnp.where(sub == 4, a, jnp.where(sub == 5, b, jnp.where(sub == 6, c, 0.0)))
            dt[h, 128:144, :] = tail.astype(bf16)
    dqt[...] = jnp.zeros_like(dqt)
    for j in range(NB):
        keys = slice(j * B, (j + 1) * B)

        def step(i, carry):
            dks, dvs = carry
            cols = slice(i * B, (i + 1) * B)
            new_dk, new_dv = [], []
            s4 = [dot(kn[h // 2, keys, :], qt[h, :, cols], 1, 0) for h in range(4)]
            d4 = [dot(vn[h // 2, keys, :], dt[h, :, cols], 1, 0) for h in range(4)]
            p4 = [jnp.exp(s) for s in s4]
            g4 = [(a * b).astype(bf16) for a, b in zip(p4, d4)]
            p4 = [a.astype(bf16) for a in p4]
            for p in range(2):
                pr = jnp.concatenate(p4[2 * p : 2 * p + 2], axis=1)
                gr = jnp.concatenate(g4[2 * p : 2 * p + 2], axis=1)
                new_dv.append(dvs[p] + dot(pr, jnp.concatenate([dm[p, 0, cols, :], dm[p, 1, cols, :]], axis=0), 1, 0))
                new_dk.append(dks[p] + dot(gr, jnp.concatenate([qm[p, 0, cols, :], qm[p, 1, cols, :]], axis=0), 1, 0))
            for h in range(4):
                dqt[64 * h : 64 * h + 64, cols] += dot(kt[64 * h : 64 * h + 64, keys], g4[h], 1, 0)
            return tuple(new_dk), tuple(new_dv)

        dks = dvs = tuple(jnp.zeros((B, 128), f32) for _ in range(2))
        for i in near(j):
            dks, dvs = step(i, (dks, dvs))
        for p in range(2):
            dqkv_o[keys, 256 + 128 * p : 384 + 128 * p] = dks[p].astype(bf16)
            dqkv_o[keys, 512 + 128 * p : 640 + 128 * p] = dvs[p].astype(bf16)
    dqkv_o[:, :256] = (dqt[...] * 0.125).astype(bf16).T
    sums[:, :256] = fold(dqkv_o[:, :256].astype(f32))
    sums[:, 256:] = fold(dqkv_o[:, 512:].astype(f32))
    gw[...] = dot(n1t[...], dqkv_o[...], 1, 0).astype(bf16)
    scattered_rows(gw, (keep, send), offs, 0, 6, RB, 0)


def attn_bwd(g, offs, q, k, v, dmix, mix, lse, n1t, segc, segr):
    whole = lambda a: pl.BlockSpec(a.shape, lambda r: (0,) * a.ndim)
    outs = [
        sds((T, D), bf16),
        sds((8, QR, 128), bf16),
        sds((8, QR, 128), bf16),
        sds((8, 512), f32),
    ]
    return call(
        attn_bwd_kernel,
        [offs, q, k, v, dmix, mix, lse, n1t, segc, segr],
        grid=(1,),
        out_shape=outs,
        in_specs=[SM, whole(q), whole(k), whole(v), pl.BlockSpec((T, 256), lambda r: (0, g))]
        + [whole(a) for a in (mix, lse, n1t, segc, segr)],
        out_specs=[whole(a) for a in outs],
        scratch_shapes=[
            pltpu.VMEM((2, T, 256), bf16),
            pltpu.VMEM((2, T, 256), bf16),
            pltpu.VMEM((4, 256, T), bf16),
            pltpu.VMEM((4, 256, T), bf16),
            pltpu.VMEM((256, T), bf16),
            pltpu.VMEM((2, 2, T, 128), bf16),
            pltpu.VMEM((2, 2, T, 128), bf16),
            pltpu.VMEM((256, T), f32),
            pltpu.VMEM((D, D), bf16),
        ],
        compiler_params=params(),
        cost_estimate=cost(21),
        name="attn_bwd",
        main=True,
    )


def last_kernel(offs, d0, d1, d2, w0, w1, w2, x, dx1, small, mids, s0, s1, s2, u0, u1,
                gt_o, keep, send, sums, sg):
    step = pl.program_id(0)

    @pl.when(step == 0)
    def _():
        sums[...] = jnp.zeros_like(sums)

    dn = dot(d0[...], w0[...], 1, 1) + dot(d1[...], w1[...], 1, 1) + dot(d2[...], w2[...], 1, 1)
    back, hats = norm_back(x[...].astype(f32), dn, small[0:1, :])
    gt_o[...] = (dx1[...] + back).astype(bf16)
    sums[0:8, :] += fold(hats)
    sums[8:16, :] += fold(dn)

    @pl.when(step == T // LB - 1)
    def _():
        total = lambda v: jnp.sum(v, axis=0, keepdims=True)
        sg[...] = jnp.zeros_like(sg)
        sg[0:1, :] = total(sums[0:8, :])
        sg[1:2, :] = total(sums[8:16, :])
        for g, s in enumerate((s0, s1, s2)):
            sg[2:3, 256 * g : 256 * g + 256] = total(s[:, :256])
            sg[3:4, 256 * g : 256 * g + 256] = total(s[:, 256:])
        for n in range(4):
            sg[4 + n : 5 + n, :] = total(mids[8 * n : 8 * n + 8, :])
        ups = [total(u0[:, :FC]), total(u0[:, FC:]), total(u1[...])]
        for n in range(4):
            parts = []
            for d in range(4 * n, 4 * n + 4):
                for j in range(3):
                    parts.append(ups[j][:, FB * d : FB * d + FB])
            sg[8 + n : 9 + n, :] = jnp.concatenate(parts, axis=1)
        low = sg[...].astype(bf16)
        row = lax.broadcasted_iota(jnp.int32, (D, 128), 0)
        col = lax.broadcasted_iota(jnp.int32, (D, 128), 1)
        for s in range(OWN):
            hot = jnp.where((row == col + offs[s] * RB) & (col < RB), 1.0, 0.0).astype(bf16)
            (keep, send)[s // 8][s % 8, :, :] = dot(low, hot, 1, 0).astype(bf16)


def last_norm(offs, dqkvs, ws, x, dx1, small, mids, ssums, usums):
    rows = pl.BlockSpec((LB, D), lambda r: (r, 0))
    whole = lambda a: pl.BlockSpec(a.shape, lambda r: (0,) * a.ndim)
    packed = pl.BlockSpec((8, SR, 128), lambda r: (0, 0, 0))
    return call(
        last_kernel,
        [offs, *dqkvs, *ws, x, dx1, small, mids, *ssums, *usums],
        grid=(T // LB,),
        out_shape=[sds((T, D), bf16), sds((8, SR, 128), bf16), sds((8, SR, 128), bf16)],
        in_specs=[SM] + [rows] * 3 + [whole(w) for w in ws] + [rows, rows]
        + [whole(a) for a in (small, mids, *ssums, *usums)],
        out_specs=[rows, packed, packed],
        scratch_shapes=[pltpu.VMEM((16, D), f32), pltpu.VMEM((SR, D), f32)],
        compiler_params=params(),
        cost_estimate=cost(10.5),
        name="last_norm",
        main=True,
    )


def out_kernel(h01, h2, r0, r1, r2, x1, small, o, wd):
    @pl.when(pl.program_id(0) == 0)
    def _():
        for j, ref in enumerate((r0, r1, r2)):
            gathered_rows(wd.at[FC * j : FC * j + FC], (ref,), None, 0, 6, FB, 0)

    a = x1[...] + small[7:8, :]
    a += dot(h01[...], wd[: 2 * FC, :], 1, 0) + dot(h2[...], wd[2 * FC :, :], 1, 0)
    o[...] = a.astype(bf16)


def layer_out(h01, h2, rest, x1, small):
    rows = pl.BlockSpec((B, D), lambda r: (r, 0))
    downs = [pl.BlockSpec((OWN, FR // 2, 128), lambda r, j=j: (0, 2 * j + 1, 0)) for j in range(3)]
    return call(
        out_kernel,
        [h01, h2, rest, rest, rest, x1, small],
        grid=(NB,),
        out_shape=sds((T, D), bf16),
        in_specs=[pl.BlockSpec((B, 2 * FC), lambda r: (r, 0)), pl.BlockSpec((B, FC), lambda r: (r, 0))]
        + downs
        + [rows, pl.BlockSpec((SR, D), lambda r: (0, 0))],
        out_specs=rows,
        scratch_shapes=[pltpu.VMEM((FF, D), bf16)],
        compiler_params=params(),
        cost_estimate=cost(10),
        name="layer_out",
        main=True,
    )


def adamw(weight, grad, mom_one, mom_two, rate):
    next_one = BETA1 * mom_one + (1.0 - BETA1) * grad
    next_two = BETA2 * mom_two + (1.0 - BETA2) * grad * grad
    fixed_one = next_one / (1.0 - BETA1**STEP)
    fixed_two = next_two / (1.0 - BETA2**STEP)
    updated = weight - rate * (fixed_one / (jnp.sqrt(fixed_two) + ADAM_EPS) + DECAY * weight)
    return (updated, next_one, next_two)


def whole_rows(offs, pair, at, dst):
    half = dst.shape[0] // 2
    for n, y in enumerate((offs[OWN], 1 - offs[OWN])):
        dst[pl.ds(pl.multiple_of(y * half, 16), half), :] = pair[n][at : at + half, :]


def update(outs, at, state, grad, rate):
    for o, val in zip(outs, adamw(state[0][at], grad, state[1][at], state[2][at], rate)):
        o[at] = val


def adam_out_kernel(offs, *refs):
    pair, out, out_o, pack = refs[:2], refs[2:5], refs[5:8], refs[8]
    whole_rows(offs, pair, FR // 2, pack)
    for t in range(6):
        grad = pack[t * RB : (t + 1) * RB, :].astype(f32)
        update(out_o, (slice(None), slice(128 * t, 128 * t + 128)), out, grad, RATES[1])


def adam_heads_kernel(offs, *refs):
    last, qkv, small = refs[:2], refs[2:5], refs[5:8]
    qkv_o, small_o, packs = refs[8:11], refs[11:14], refs[14:]
    for n in range(2):
        whole_rows(offs, last, n * QR // 2, packs[n])
    both = lambda r, n: last[0][QR + r : QR + r + n, :].astype(f32) + last[1][QR + r : QR + r + n, :].astype(f32)
    for g in range(3):
        for part in range(3):
            for t in range(2):
                c = D * part + 256 * g + 128 * t
                r = (2 * part + t) * RB
                grad = packs[g][r : r + RB, :].astype(f32) if g < 2 else both(r, RB)
                update(qkv_o, (slice(None), slice(c, c + 128)), qkv, grad, RATES[0])
    update(small_o, Ellipsis, small, both(QR, SR)[:12, :RB], RATES[4])


def adam_ff_kernel(offs, *refs):
    two, pair, up, down = refs[:2], refs[2:4], refs[4:7], refs[7:10]
    up_o, down_o = refs[10:13], refs[13:16]
    pack = refs[16]
    whole_rows(offs, pair, 0, pack)

    def total(j, r, n):
        if j == 2:
            return pack[r : r + n, :].astype(f32)
        rows = slice(FR * j + r, FR * j + r + n)
        return two[0][rows, :].astype(f32) + two[1][rows, :].astype(f32)

    for t in range(8):
        parts = [total(j, t * RB, RB) for j in range(3)]
        grad = jnp.concatenate([p[:, :64] for p in parts] + [p[:, 64:] for p in parts], axis=1)
        update(up_o, (slice(None), slice(384 * t, 384 * t + 384)), up, grad, RATES[2])
    for j in range(3):
        for t in range(6):
            at = (slice(FB * j, FB * j + FB), slice(128 * t, 128 * t + 128))
            update(down_o, at, down, total(j, 8 * RB + t * FB, FB), RATES[3])


def adam_call(kernel, offs, grads, states, scratch, name):
    shapes = [sds(s.shape, f32) for s in states]
    return call(
        kernel,
        [offs, *grads, *states],
        out_shape=shapes,
        in_specs=[SM] + [VM] * (len(grads) + len(states)),
        out_specs=[VM] * len(shapes),
        scratch_shapes=[pltpu.VMEM((r, 128), bf16) for r in scratch],
        compiler_params=params(),
        cost_estimate=cost(),
        name=name,
    )


def shifted(f):
    pairs = []
    for z in range(4):
        for x in range(2):
            for c in range(2):
                tz, tx, tc = f(z, x, c)
                pairs.append(((z * 2 + x) * 2 + c, (tz * 2 + tx) * 2 + tc))
    return pairs


TO_CORE = shifted(lambda z, x, c: (z, x, 1 - c))
TO_X = shifted(lambda z, x, c: (z, 1 - x, c))
TO_Z = [shifted(lambda z, x, c, s=s: ((z + s) % 4, x, c)) for s in range(4)]
FROM_Z = [shifted(lambda z, x, c, s=s: ((z - s) % 4, x, c)) for s in range(4)]
TO_Y = [(0, 1), (1, 0)]


def stack_kernel(a, b, c, d, *refs):
    out = refs[len(refs) // 2]
    for n, ref in enumerate((a, b, c, d)):
        out[n] = ref[...]


class Gather:
    def __init__(self, own):
        self.own = own

    def along_z(self):
        self.parts = [self.own] + [lax.ppermute(self.own, "dp", TO_Z[s]) for s in (1, 2, 3)]

    def along_x(self, *later):
        anywhere = pl.BlockSpec(memory_space=pl.ANY)
        outs = call(
            stack_kernel,
            [*self.parts, *[g.own for g in later]],
            out_shape=[sds((4,) + self.own.shape, bf16)] + [sds(g.own.shape, bf16) for g in later],
            in_specs=[VM] * 4 + [anywhere] * len(later),
            out_specs=[VM] + [anywhere] * len(later),
            input_output_aliases={4 + n: 1 + n for n in range(len(later))},
            compiler_params=params(),
            cost_estimate=cost(1.7),
            name="stack",
        )
        for g, own in zip(later, outs[1:]):
            g.own = own
        line = outs[0]
        self.pieces = [line, lax.ppermute(line, "dp", TO_X), lax.ppermute(line, "dp", TO_CORE)]

    def to_core(self, hold=False):
        if hold:
            self.pieces[1] = wait_here(self.pieces[1])[0]
        self.pieces.append(lax.ppermute(self.pieces[1], "dp", TO_CORE))


def add_core_kernel(*refs):
    half = len(refs) // 2 - 1
    a, b = refs[-2:]
    at = 0
    for keep, got in zip(refs[:half], refs[half : 2 * half]):
        rows = keep.shape[1]
        a[:, at : at + rows] = (keep[:4].astype(f32) + got[:4].astype(f32)).astype(bf16)
        b[:, at : at + rows] = (keep[4:].astype(f32) + got[4:].astype(f32)).astype(bf16)
        at += rows


def add_core_half_kernel(offs, *refs):
    n = len(refs) // 2 - 1
    outs = refs[-2:]
    at = 0
    for keep, got in zip(refs[:n], refs[n : 2 * n]):
        half = keep.shape[1] // 2
        for out, y in zip(outs, (offs[OWN], 1 - offs[OWN])):
            rows = pl.ds(pl.multiple_of(y * half, 16), half)
            out[:, at : at + half] = (keep[:, rows].astype(f32) + got[:, rows].astype(f32)).astype(bf16)
        at += half


def add_y_kernel(*refs):
    n = len(refs) // 2 - 1
    a, b = refs[-2:]
    at = 0
    for keep, got in zip(refs[:n], refs[n : 2 * n]):
        rows = keep.shape[2]
        total = (keep[...].astype(f32) + got[...].astype(f32)).astype(bf16)
        a[:, at : at + rows] = total[0]
        b[:, at : at + rows] = total[1]
        at += rows


def add_x_kernel(*refs):
    pairs, outs = refs[:-4], refs[-4:]
    at = 0
    for keep, got in zip(pairs[::2], pairs[1::2]):
        rows = keep.shape[1]
        for s in range(4):
            outs[s][at : at + rows, :] = (keep[s].astype(f32) + got[s].astype(f32)).astype(bf16)
        at += rows


def add_z_kernel(a, b, c, d, o):
    o[...] = (a[...].astype(f32) + b[...].astype(f32) + c[...].astype(f32) + d[...].astype(f32)).astype(bf16)


def add_call(kernel, args, outs, name, then, beside):
    if beside:
        SIDE.append((kernel, args, outs, then))
        return
    then(add_alone(kernel, args, outs, name))


def add_alone(kernel, args, outs, name):
    return call(
        kernel,
        args,
        out_shape=outs,
        in_specs=[VM] * len(args),
        out_specs=[VM] * len(outs),
        compiler_params=params(),
        cost_estimate=cost(),
        name=name,
    )


class Scatter:
    def __init__(self, *packs):
        self.keeps = [p[0] for p in packs]
        self.rows = sum(k.shape[1] for k in self.keeps)
        self.gots = [lax.ppermute(p[1], "dp", TO_CORE) for p in packs]

    def half_along_y(self, offs):
        self.rows //= 2
        args = (*self.keeps, *self.gots)
        block = lambda r: pl.BlockSpec((4, r, 128), lambda i: (i, 0, 0))
        mine, other = call(
            add_core_half_kernel,
            [offs, *args],
            grid=(2,),
            out_shape=[sds((8, self.rows, 128), bf16)] * 2,
            in_specs=[SM] + [block(a.shape[1]) for a in args],
            out_specs=[block(self.rows)] * 2,
            compiler_params=params(),
            cost_estimate=cost(),
            name="add_core_half",
        )
        self.halves = (mine, lax.ppermute(other, "rep", TO_Y))

    def sums_along_x(self):
        cut = lambda a: a.reshape(2, 4, a.shape[1], 128)
        args = [cut(half) for half in self.halves]
        self.mine, send = call(
            add_y_kernel,
            args,
            grid=(2,),
            out_shape=[sds((4, self.rows, 128), bf16)] * 2,
            in_specs=[pl.BlockSpec((2, 2, a.shape[2], 128), lambda i: (0, i, 0, 0)) for a in args],
            out_specs=[pl.BlockSpec((2, self.rows, 128), lambda i: (i, 0, 0))] * 2,
            compiler_params=params(),
            cost_estimate=cost(),
            name="add_y",
        )
        self.got = lax.ppermute(send, "dp", TO_X)

    def along_x(self, beside=False):
        outs = [sds((4, self.rows, 128), bf16)] * 2

        def then(out):
            self.mine = out[0]
            self.got = lax.ppermute(out[1], "dp", TO_X)

        add_call(add_core_kernel, (*self.keeps, *self.gots), outs, "add_core", then, beside)

    def along_z(self, *others):
        pairs = [a for s in (self, *others) for a in (s.mine, s.got)]
        self.rows += sum(s.rows for s in others)
        outs = [sds((self.rows, 128), bf16)] * 4

        def then(parts):
            self.parts = [parts[0]] + [lax.ppermute(parts[s], "dp", FROM_Z[s]) for s in (1, 2, 3)]

        add_call(add_x_kernel, pairs, outs, "add_x", then, False)

    def along_y(self, beside=False):
        def then(out):
            self.done = (out[0], lax.ppermute(out[0], "rep", TO_Y))

        add_call(add_z_kernel, self.parts, [sds((self.rows, 128), bf16)], "add_z", then, beside)


def gather_any(small, wq, wo, wu, wd):
    full = lambda w, axis: lax.all_gather(w.astype(bf16), "dp", axis=axis, tiled=True)
    small = full(small, 1)
    blocks = small.reshape(small.shape[0], OWN, RB).transpose(1, 0, 2)
    blocks = jnp.pad(blocks, ((0, 0), (0, SR - small.shape[0]), (0, 128 - RB)))
    q = full(wq, 0).reshape(OWN, RB, 3, 3, 2, 128).transpose(3, 0, 2, 4, 1, 5).reshape(3, OWN, QR, 128)
    o = full(wo, 0).reshape(OWN, RB, 6, 128).transpose(0, 2, 1, 3).reshape(OWN, QR, 128)
    u = full(wu, 0).reshape(OWN, RB, 8, 2, 3, FB).transpose(4, 0, 2, 1, 3, 5).reshape(3, OWN, 8 * RB, 128)
    d = full(wd, 0).reshape(OWN, 3, FB, 6, 128).transpose(1, 0, 3, 2, 4).reshape(3, OWN, 6 * FB, 128)
    f = jnp.concatenate([u, d], 2)
    cut = lambda a: tuple(a[4 * n : 4 * n + 4] for n in range(4))
    heads = [cut(jnp.concatenate(p, 1)) for p in ((q[0], blocks), (q[1], q[2]))]
    return heads, jnp.concatenate([f[0], f[1], f[2], o], 1)


def scatter_any(packs, grads):
    q0, q1, q2, o, s = [jnp.concatenate(p, 0) for p in packs]
    q = jnp.stack([q0, q1, q2]).reshape(3, OWN, 3, 2, RB, 128).transpose(1, 4, 2, 0, 3, 5)
    f = grads.reshape(OWN, 3, FR, 128)
    u = f[:, :, : 8 * RB].reshape(OWN, 3, 8, RB, 2, FB).transpose(0, 3, 2, 4, 1, 5)
    d = f[:, :, 8 * RB :].reshape(OWN, 3, 6, FB, 128).transpose(0, 1, 3, 2, 4)
    o = o.reshape(OWN, 6, RB, 128).transpose(0, 2, 1, 3)
    s = s[:, :12, :RB].transpose(1, 0, 2).reshape(12, D)
    flat = ((q.reshape(D, 3 * D), 0), (o.reshape(D, D), 0), (u.reshape(D, FF), 0), (d.reshape(FF, D), 0), (s, 1))
    out = []
    for g, axis in flat:
        g = lax.psum_scatter(g, "dp", scatter_dimension=axis, tiled=True)
        out.append(lax.psum(g, "rep").astype(f32))
    return out


def shards(tokens, segment_ids, cotangent, *state, wide):
    masters, firsts, seconds = state[:5], state[5:10], state[10:15]
    w_qkv, w_out, w_up, w_down, small_params = masters
    x = tokens[0]
    dy = cotangent[0]
    seg = segment_ids[0]
    segc = seg.reshape(T, 1)
    segr = seg.reshape(1, T)
    ORDER.clear()
    if wide:
        me = lax.axis_index("dp")
        s = jnp.arange(OWN, dtype=jnp.int32)
        z = (me // 4 - s % 4) % 4
        xx = (me // 2 % 2) ^ (s // 4 % 2)
        cc = (me % 2) ^ (s // 8)
        offs = jnp.append((z * 2 + xx) * 2 + cc, lax.axis_index("rep")).astype(jnp.int32)
        (own_rest,) = pack(pack_rest_kernel, (w_out, w_up, w_down), (3 * FR + QR,), "pack_rest")
        rest = lax.all_gather(own_rest, "dp", axis=0, tiled=True).reshape(OWN, 3 * FR + QR, 128)
        owns = pack(pack_heads_kernel, (small_params, w_qkv), (QR + SR, 2 * QR, 16), "pack_heads")
        lines = [Gather(own) for own in owns[:2]]
        lines[0].along_z()
        lines[0].along_x(lines[1])
        lines[0].to_core()
        lines[1].along_z()
        heads = [lines[0].pieces, None]
    else:
        offs = jnp.arange(OWN, dtype=jnp.int32)
        heads, rest = gather_any(small_params, w_qkv, w_out, w_up, w_down)

    n1, n1t, small = norm_first(offs, x, heads[0], QR)
    fwd = []
    if wide:
        lines[1].along_x()
        heads[1] = lines[1].pieces
    for g in range(3):
        fwd.append(attn_fwd(g, offs, n1, heads[min(g, 1)], small, segc, segr))
        if wide and g == 0:
            lines[1].to_core(hold=True)
    x1, n2, n2t = post_attn(x, [f[3] for f in fwd], rest, small)
    sent = []

    def send(*packs):
        if wide:
            sent.append(Scatter(*packs))

    h01, acc, grads, u01 = feed_forward_two(n2, n2t, dy, rest, small)
    if wide:
        own_ff = lax.psum_scatter(grads.reshape(-1, 128), "dp", scatter_dimension=0, tiled=True)
    h2, u2, dx1, dmix, *grad, keep_o, send_o, mids = feed_forward_last(
        offs, n2, n2t, dy, rest, small, acc, x1, [f[4] for f in fwd]
    )
    send(grad, (keep_o, send_o))
    states = [(masters[n], firsts[n], seconds[n]) for n in range(5)]
    new = [None] * 5
    bwd = []
    for g in range(3):
        q, k, v, mix, _, lse, _ = fwd[g]
        bwd.append(attn_bwd(g, offs, q, k, v, dmix, mix, lse, n1t, segc, segr))
        if g == 0 and wide:
            sent[0].half_along_y(offs)
        if g == 1 and wide:
            send(bwd[0][1:3], bwd[1][1:3])
            sent[1].half_along_y(offs)
            sent[0].sums_along_x()
    if wide:
        sent[0].along_z()
        sent[1].sums_along_x()
        (own_ff,) = wait_here(own_ff)
        pair = (own_ff, lax.ppermute(own_ff, "rep", TO_Y))
    grad_tokens, keep_s, send_s = last_norm(
        offs, [b[0] for b in bwd], [f[6] for f in fwd], x, dx1, small, mids,
        [b[3] for b in bwd], [u01, u2],
    )
    if wide:
        send(bwd[2][1:3], (keep_s, send_s))
        ORDER.append(pair[1])
        sent[0].along_y()
        ORDER.append(sent[1].got)
        sent[2].along_x()
        both = adam_call(adam_ff_kernel, offs, (*pair, *sent[0].done), states[2] + states[3], (FR,), "adam_ff")
        new[2], new[3] = both[:3], both[3:]
        sent[1].along_z(sent[2])
    result = layer_out(h01, h2, rest, x1, small)
    if wide:
        sent[1].along_y()
        new[1] = adam_call(adam_out_kernel, offs, sent[0].done, states[1], (QR,), "adam_out")
        both = adam_call(adam_heads_kernel, offs, sent[1].done, states[0] + states[4], (QR, QR), "adam_heads")
        new[0], new[4] = both[:3], both[3:]
    else:
        packs = [(b[1], b[2]) for b in bwd] + [(keep_o, send_o), (keep_s, send_s)]
        owned = scatter_any(packs, jnp.concatenate([grads, jnp.concatenate(grad, 0)], 1))
        new = [adamw(states[n][0], owned[n], states[n][1], states[n][2], RATES[n]) for n in range(5)]
    return (
        result[None],
        grad_tokens[None],
        *[n[0] for n in new],
        *[n[1] for n in new],
        *[n[2] for n in new],
    )


def solution(mesh):
    rows = P("dp", None)
    small = P(None, "dp")
    state = (rows, rows, rows, rows, small)
    seqs = P(("dp", "rep"), None, None)
    return jax.shard_map(
        functools.partial(shards, wide=mesh.shape["dp"] == 16 and mesh.shape["rep"] == 2),
        mesh=mesh,
        in_specs=(seqs, P(("dp", "rep"), None), seqs) + state * 3,
        out_specs=(seqs, seqs) + state * 3,
        check_vma=False,
    )
```
